128 devices in a mesh: ctx: 16 (over z, y), smp: 8 (over x, core).
Axes of the slice: x: 4, y: 4, z: 4, core: 2. Of those that a mesh axis runs over, the one named last changes fastest.
Arguments:
- layer_input: bfloat16 [8192, 4096], P('ctx'), may hold values from -6 to 6
- proj_weight: bfloat16 [4096, 8192], P(None, 'smp'), may hold values from -0.09375 to 0.09375
- step_size: float32 [8192, 128], P('ctx', 'smp'), may hold values from 0.01 to 0.16
- decay_log: float32 [128], P('smp'), as said below
- skip_gain: float32 [128], P('smp'), may hold values from 0.5 to 1.5
- write_vec: bfloat16 [8192, 8, 128], P('ctx', 'smp'), may hold values from -0.52734375 to 0.52734375
- read_vec: bfloat16 [8192, 8, 128], P('ctx', 'smp'), may hold values from -0.52734375 to 0.52734375
- out_grad: bfloat16 [8192, 8192], P('ctx', 'smp'), may hold values from -6 to 6
- start_state: float32 [16, 128, 64, 128], P('ctx', 'smp'), may hold values from -1 to 1
- fork_grad: float32 [32, 128, 64, 128], P('ctx', 'smp'), may hold values from -4.2426405 to 4.2426405
Outputs:
- input_grad: bfloat16 [8192, 4096], P(('ctx', 'smp'))
- weight_grad: bfloat16 [4096, 8192], P('ctx', 'smp')
- write_grad: float32 [8192, 8, 128], P('ctx', 'smp')
- read_grad: float32 [8192, 8, 128], P('ctx', 'smp')
The draws below stay inside these ranges and needn't reach their ends.
Inputs may be any that keep to these rules, and one draw needn't show every extreme that they name: Minus exp(decay_log) is each head's decay coefficient.
All inputs are finite; a program needn't handle non-finite values.
Results may differ from the reference program's by a relative error of at most 0.022.
Values may be sent and summed in bfloat16 or wider, within the bound.
No kernel may reach another device: no remote copies, remote signals or barrier semaphores. Data moves between devices by JAX's collectives and lax.ppermute only.
A program may use at most 128 MiB of HBM per device.

```python
import math
import jax
import jax.numpy as jnp
from jax import lax

D = 4096
H = 128
P_SIZE = 64
N = 128
G = 8
TOK_DEV = 512
SHARDS = 16
TOKENS = 8192
SAMPLES = 32


def draw_step_size(key, part):
    key = jax.random.fold_in(key, 11)
    first, second = jax.random.split(key)
    blocks = TOKENS // TOK_DEV
    spread = math.log(2.0)
    block_factor = jnp.exp(jax.random.uniform(first, (blocks, 1, H), jnp.float32, -spread, spread))
    rough = jnp.exp(jax.random.uniform(second, (blocks, TOK_DEV, H), jnp.float32, -spread, spread))
    return (0.04 * block_factor * rough).reshape(TOKENS, H)


def draw_decay_log(key, part):
    key = jax.random.fold_in(key, 12)
    first, second = jax.random.split(key)
    share = 0.5
    slower = jax.random.uniform(first, (H,), jnp.float32) < share
    factor = jax.random.uniform(second, (H,), jnp.float32, 0.6, 1.4)
    coefficient = jnp.where(slower, 0.8 / (0.045 * TOKENS), 0.55) * factor
    return jnp.log(coefficient)


def level_of(stream_key, extent, shards, low, top_value):
    def one(axis_at, shards_of):
        draws = jax.random.uniform(jax.random.fold_in(jax.random.fold_in(stream_key, 6), axis_at), (shards_of,), jnp.float32, low / len(shards), top_value / len(shards))
        return jnp.repeat(jnp.exp(draws), extent[axis_at] // shards_of).reshape((-1,) + (1,) * (len(extent) - axis_at - 1))

    factor_of = one(*shards[0])
    for cut in shards[1:]:
        factor_of = factor_of * one(*cut)
    return factor_of


def noise(own_key, shape, scale, most, shards=(), dtype=jnp.bfloat16):
    drawn = scale * jax.random.normal(own_key, shape, jnp.float32)
    if shards:
        drawn = drawn * level_of(own_key, shape, shards, -0.22, 0.18)
    return jnp.clip(drawn, -most, most).astype(dtype)


def setup_inputs(seed: int = 0) -> dict:
    arg_keys = jax.random.split(jax.random.key(seed), 11)
    return {
        "layer_input": noise(arg_keys[0], (TOKENS, D), 1.0, 6.0, ((0, 16),)),
        "proj_weight": noise(arg_keys[1], (D, H * P_SIZE), D ** -0.5, 0.09375, ((1, 8),)),
        "step_size": draw_step_size(jax.random.fold_in(arg_keys[10], 71), 0),
        "decay_log": draw_decay_log(jax.random.fold_in(arg_keys[10], 71), 0),
        "skip_gain": jnp.clip(0.5 + 1.0 * jax.random.uniform(arg_keys[4], (H,), jnp.float32) ** level_of(arg_keys[4], (H,), ((0, 8),), -0.2, 0.2), 0.5, 1.5),
        "write_vec": noise(arg_keys[5], (TOKENS, G, N), (N ** -0.5), 0.52734375, ((0, 16), (1, 8))),
        "read_vec": noise(arg_keys[6], (TOKENS, G, N), (N ** -0.5), 0.52734375, ((0, 16), (1, 8))),
        "out_grad": noise(arg_keys[7], (TOKENS, H * P_SIZE), 1.0, 6.0, ((0, 16), (1, 8))),
        "start_state": noise(arg_keys[8], (SHARDS, H, P_SIZE, N), 0.125, 1.0, ((0, 16), (1, 8)), jnp.float32),
        "fork_grad": noise(arg_keys[9], (SAMPLES, H, P_SIZE, N), (4.0 * SAMPLES ** -0.5), 4.2426405, ((0, 16), (1, 8)), jnp.float32),
    }


highest = lax.Precision.HIGHEST


def block_grads(inputs, grad_heads, step_block, cumulative, write_block, read_block, carried, start_block, skip_vals):
    length, groups, per_group, head_width = grad_heads.shape
    head_count = groups * per_group
    inputs_wide = inputs.astype(jnp.float32)
    grads_wide = grad_heads.astype(jnp.float32)
    writes_wide = write_block.astype(jnp.float32)
    reads_wide = read_block.astype(jnp.float32)
    scores = jnp.einsum('jgn,tgn->gjt', reads_wide, writes_wide, precision=highest)
    cum_heads = cumulative.T.reshape(groups, per_group, length)
    offsets = cum_heads[:, :, :, None] - cum_heads[:, :, None, :]
    causal = jnp.arange(length)[:, None] >= jnp.arange(length)[None, :]
    kernel = jnp.where(causal, jnp.exp(jnp.minimum(offsets, 0.0)), 0.0)
    step_cols = step_block.T.reshape(groups, per_group, length)[:, :, None, :]
    mixing = (scores[:, None] * kernel * step_cols).astype(jnp.bfloat16)
    within = jnp.einsum('ghjt,jghp->tghp', mixing.astype(jnp.float32), grads_wide, precision=highest)
    intersections = jnp.einsum('jghp,tghp->ghjt', grads_wide, inputs_wide, precision=highest)
    coupling = jnp.sum(step_cols * kernel * intersections, axis=1).astype(jnp.bfloat16).astype(jnp.float32)
    end_weights = (step_block * jnp.exp(cumulative[length - 1][None, :] - cumulative)).reshape(length, groups, per_group)
    starts = jnp.exp(cumulative).reshape(length, groups, per_group)
    to_inputs = jnp.einsum('tgn,ghpn->tghp', writes_wide, carried, precision=highest)
    input_state = jnp.einsum('tghp,ghpn->tghn', inputs_wide, carried, precision=highest)
    from_start = jnp.einsum('tghp,ghpn->tghn', grads_wide, start_block, precision=highest)
    x_grad = within + end_weights[..., None] * to_inputs + skip_vals.reshape(groups, per_group)[None, :, :, None] * grads_wide
    write_grad = jnp.einsum('gjt,jgn->tgn', coupling, reads_wide, precision=highest) + jnp.sum(end_weights[..., None] * input_state, axis=2)
    read_grad = jnp.einsum('gjt,tgn->jgn', coupling, writes_wide, precision=highest) + jnp.sum(starts[..., None] * from_start, axis=2)
    return x_grad.reshape(length, head_count * head_width).astype(jnp.bfloat16), write_grad, read_grad


def reference(layer_input, proj_weight, step_size, decay_log, skip_gain, write_vec, read_vec, out_grad, start_state, fork_grad):
    per_group = H // G
    projected = jnp.dot(layer_input, proj_weight, preferred_element_type=jnp.float32).astype(jnp.bfloat16)
    inputs = projected.reshape(SHARDS, TOK_DEV, G, per_group, P_SIZE)
    grad_heads = out_grad.reshape(SHARDS, TOK_DEV, G, per_group, P_SIZE)
    step_block = step_size.reshape(SHARDS, TOK_DEV, H)
    cumulative = jnp.cumsum(step_block * (-jnp.exp(decay_log)), axis=1)
    write_block = write_vec.reshape(SHARDS, TOK_DEV, G, N)
    read_block = read_vec.reshape(SHARDS, TOK_DEV, G, N)

    def block_local(element):
        grad_part, cum_part, read_part = element
        weighted = jnp.exp(cum_part).reshape(TOK_DEV, G, per_group)[..., None] * read_part.astype(jnp.float32)[:, :, None, :]
        return jnp.einsum('tghp,tghn->ghpn', grad_part.astype(jnp.float32), weighted, precision=highest)

    local_sum = lax.map(block_local, (grad_heads, cumulative, read_block))
    decays = jnp.exp(cumulative[:, TOK_DEV - 1]).reshape(SHARDS, G, per_group)
    fork_sum = jnp.sum(fork_grad, axis=0).reshape(G, per_group, P_SIZE, N)

    def backward(carried_in, element):
        return element[0] + element[1][:, :, None, None] * carried_in, carried_in

    unused, carried = lax.scan(backward, fork_sum, (local_sum, decays), reverse=True)
    start_blocks = start_state.reshape(SHARDS, G, per_group, P_SIZE, N)

    def block_item(element):
        return block_grads(element[0], element[1], element[2], element[3], element[4], element[5], element[6], element[7], skip_gain)

    x_grad, write_grad, read_grad = lax.map(block_item, (inputs, grad_heads, step_block, cumulative, write_block, read_block, carried, start_blocks))
    x_grad = x_grad.reshape(TOKENS, H * P_SIZE)
    input_grad = jnp.dot(x_grad, proj_weight.T, preferred_element_type=jnp.float32).astype(jnp.bfloat16)
    weight_grad = (jnp.dot(layer_input.T, x_grad, preferred_element_type=jnp.float32) * (TOKENS ** -0.5)).astype(jnp.bfloat16)
    return (input_grad, weight_grad, write_grad.reshape(TOKENS, G, N), read_grad.reshape(TOKENS, G, N))
```

```python
import jax
import jax.numpy as jnp
from jax import lax
from jax.sharding import PartitionSpec as P

SIDE = 4


def hop(block, dz, dy):
    route = []
    for i in range(SIDE * SIDE):
        z, y = divmod(i, SIDE)
        route.append((i, ((z + dz) % SIDE) * SIDE + (y + dy) % SIDE))
    return lax.ppermute(block, "ctx", route)


def pick(stacked, index):
    return lax.dynamic_index_in_dim(stacked, index % stacked.shape[0], 0, keepdims=False)


def split_product(form, narrow, wide):
    high_part = wide.astype(jnp.bfloat16)
    low_part = (wide - high_part.astype(jnp.float32)).astype(jnp.bfloat16)
    first_term = jnp.einsum(form, narrow, high_part, preferred_element_type=jnp.float32)
    return first_term + jnp.einsum(form, narrow, low_part, preferred_element_type=jnp.float32)


def packed(state, extra, decay):
    high = decay.astype(jnp.bfloat16)
    low = (decay - high.astype(jnp.float32)).astype(jnp.bfloat16)
    tail = jnp.concatenate([high, low, jnp.zeros((8,), jnp.bfloat16)])
    tail = jnp.broadcast_to(tail[:, None], (16, 128))
    return jnp.concatenate(
        [
            state.reshape(-1, 128).astype(jnp.bfloat16),
            extra.reshape(-1, 128).astype(jnp.bfloat16),
            tail,
        ]
    )


def unpacked(message):
    message = message.astype(jnp.float32)
    state = message[:256].reshape(4, 64, 128)
    extra = message[256:512].reshape(4, 64, 128)
    decay = message[512:516, 0] + message[516:520, 0]
    return state, extra, decay[:, None, None]


def relay(local_sum, fork_part, decays, z, y):
    local_q = local_sum.reshape(SIDE, 4, 64, 128)
    fork_q = fork_part.reshape(SIDE, 4, 64, 128)
    decay_q = decays.reshape(SIDE, 4)
    messages = [
        packed(pick(local_q, y + d), pick(fork_q, y + d), pick(decay_q, y + d)) for d in range(SIDE)
    ]
    arrived = [messages[0]] + [hop(messages[d], 0, d) for d in range(1, SIDE)]
    stacked = jnp.stack(arrived)
    by_y = [unpacked(pick(stacked, y - b)) for b in range(SIDE)]
    fork_y = by_y[0][1] + by_y[1][1] + by_y[2][1] + by_y[3][1]
    total, rate = by_y[3][0], by_y[3][2]
    for b in (2, 1, 0):
        total = by_y[b][0] + by_y[b][2] * total
        rate = by_y[b][2] * rate
    message = packed(total, fork_y, rate[:, 0, 0])
    arrived = [message] + [hop(message, d, 0) for d in range(1, SIDE)]
    stacked = jnp.stack(arrived)
    by_z = [unpacked(pick(stacked, z - b)) for b in range(SIDE)]
    carry = by_z[0][1] + by_z[1][1] + by_z[2][1] + by_z[3][1]
    mine = carry
    for b in (3, 2, 1):
        carry = by_z[b][0] + by_z[b][2] * carry
        mine = jnp.where(z == b - 1, carry, mine)
    carried = [None] * SIDE
    carried[3] = mine
    for b in (2, 1, 0):
        carried[b] = by_y[b + 1][0] + by_y[b + 1][2] * carried[b + 1]
    stacked = jnp.stack(carried).astype(jnp.bfloat16).reshape(SIDE, 256, 128)
    arrived = [pick(stacked, y)] + [hop(pick(stacked, y + d), 0, d) for d in range(1, SIDE)]
    stacked = jnp.stack(arrived)
    return jnp.stack([pick(stacked, y - q) for q in range(SIDE)]).reshape(16, 64, 128).astype(
        jnp.float32
    )


def body(
    layer_input,
    proj_weight,
    step_size,
    decay_log,
    skip_gain,
    write_vec,
    read_vec,
    out_grad,
    start_state,
    fork_grad,
):
    length = layer_input.shape[0]
    head_count = step_size.shape[1]
    head_width = out_grad.shape[1] // head_count
    state_size = write_vec.shape[2]
    position = lax.axis_index("ctx")
    z, y = position // SIDE, position % SIDE
    writes = write_vec[:, 0]
    reads = read_vec[:, 0]
    grad_heads = out_grad.reshape(length, head_count, head_width)
    cumulative = jnp.cumsum(step_size * -jnp.exp(decay_log), axis=0)
    decays = jnp.exp(cumulative[length - 1])
    starts = jnp.exp(cumulative)
    weighted = starts[..., None] * reads.astype(jnp.float32)[:, None, :]
    local_sum = split_product("thp,thn->hpn", grad_heads, weighted)
    carried = relay(local_sum, jnp.sum(fork_grad, axis=0), decays, z, y)
    scores = jnp.einsum("jn,tn->jt", reads, writes, preferred_element_type=jnp.float32)
    cum_heads = cumulative.T
    offsets = cum_heads[:, :, None] - cum_heads[:, None, :]
    causal = jnp.arange(length)[:, None] >= jnp.arange(length)[None, :]
    kernel = jnp.where(causal, jnp.exp(jnp.minimum(offsets, 0.0)), 0.0)
    step_cols = step_size.T[:, None, :]
    mixing = (scores[None] * kernel * step_cols).astype(jnp.bfloat16)
    within = jnp.einsum("hjt,jhp->thp", mixing, grad_heads, preferred_element_type=jnp.float32)
    end_weights = step_size * jnp.exp(cumulative[length - 1][None, :] - cumulative)
    to_inputs = split_product("tn,hpn->thp", writes, carried)
    skip_term = skip_gain[None, :, None] * grad_heads.astype(jnp.float32)
    x_wide = within + end_weights[..., None] * to_inputs + skip_term
    x_grad = x_wide.reshape(length, head_count * head_width).astype(jnp.bfloat16)

    columns = layer_input.reshape(length, SIDE, SIDE, 256)
    x_first, x_second = x_grad[:, :512], x_grad[:, 512:]

    def part_a(y_to):
        rows = lax.dynamic_index_in_dim(columns, y_to % SIDE, 2, keepdims=False).reshape(length, 1024)
        return lax.dot_general(
            rows, x_first, (((0,), (0,)), ((), ())), preferred_element_type=jnp.float32
        ).reshape(SIDE, 256, 512)

    def part_b(z_to):
        rows = lax.dynamic_index_in_dim(columns, z_to % SIDE, 1, keepdims=False).reshape(length, 1024)
        return lax.dot_general(
            rows, x_second, (((0,), (0,)), ((), ())), preferred_element_type=jnp.float32
        ).reshape(SIDE, 256, 512)

    def ring(part, here, move):
        half = jnp.bfloat16
        far = part(here + 2).astype(half)
        n = far.shape[0] // 2
        up = move(far[:n], 1)
        down = move(far[n:], -1)
        upper = part(here + 1)
        lower = part(here - 1)
        upper = jnp.concatenate([upper[:n] + up.astype(jnp.float32), upper[n:]]).astype(half)
        lower = jnp.concatenate([lower[:n], lower[n:] + down.astype(jnp.float32)]).astype(half)
        from_below = move(upper, 1)
        from_above = move(lower, -1)
        own = part(here)
        return own + from_below.astype(jnp.float32) + from_above.astype(jnp.float32)

    by_y = lambda b, s: hop(b, 0, s)
    by_z = lambda b, s: hop(b, s, 0)
    sum_a = ring(part_a, y, by_y)
    sum_b = ring(part_b, z, by_z)
    sum_a = ring(lambda i: pick(sum_a, i), z, by_z)
    sum_b = ring(lambda i: pick(sum_b, i), y, by_y)
    scale_factor = (length * lax.axis_size("ctx")) ** (-0.5)
    weight_grad = (jnp.concatenate([sum_a, sum_b], axis=1) * scale_factor).astype(jnp.bfloat16)

    input_grad = lax.psum_scatter(
        lax.dot_general(
            x_grad, proj_weight, (((1,), (1,)), ((), ())), preferred_element_type=jnp.float32
        ).astype(jnp.bfloat16),
        "smp",
        scatter_dimension=0,
        tiled=True,
    )

    projected = jnp.dot(layer_input, proj_weight, preferred_element_type=jnp.float32).astype(
        jnp.bfloat16
    )
    inputs = projected.reshape(length, head_count, head_width)
    intersections = jnp.einsum(
        "jhp,thp->hjt", grad_heads, inputs, preferred_element_type=jnp.float32
    )
    coupling = jnp.sum(step_cols * kernel * intersections, axis=0).astype(jnp.bfloat16)
    input_state = split_product("thp,hpn->thn", inputs, carried)
    from_start = split_product("thp,hpn->thn", grad_heads, start_state[0])
    write_grad = jnp.einsum("jt,jn->tn", coupling, reads, preferred_element_type=jnp.float32) + jnp.sum(
        end_weights[..., None] * input_state, axis=1
    )
    read_grad = jnp.einsum("jt,tn->jn", coupling, writes, preferred_element_type=jnp.float32) + jnp.sum(
        starts[..., None] * from_start, axis=1
    )
    return (input_grad, weight_grad, write_grad[:, None], read_grad[:, None])


def solution(mesh):
    placed = (
        P("ctx", None),
        P(None, "smp"),
        P("ctx", "smp"),
        P("smp"),
        P("smp"),
        P("ctx", "smp", None),
        P("ctx", "smp", None),
        P("ctx", "smp"),
        P("ctx", "smp", None, None),
        P("ctx", "smp", None, None),
    )
    return jax.shard_map(
        body,
        mesh=mesh,
        in_specs=placed,
        out_specs=(
            P(("ctx", "smp"), None),
            P("ctx", "smp"),
            P("ctx", "smp", None),
            P("ctx", "smp", None),
        ),
        check_vma=False,
    )
```

```python
import functools

import jax
import jax.numpy as jnp
from jax import lax
from jax.experimental import pallas as pl
from jax.experimental.pallas import tpu as pltpu
from jax.sharding import PartitionSpec as P

SIDE = 4
CHUNK = 128
CHUNKS = 4
HEADS = 16
WIDE = 1024
QUARTER = WIDE // SIDE
TAIL = 16
F32 = jnp.float32
BF16 = jnp.bfloat16
ORDER = (2, 1, 3, 0)
VMEM_LIMIT = 48 * 1024 * 1024


def params(**kw):
    return pltpu.CompilerParams(vmem_limit_bytes=VMEM_LIMIT, **kw)


def cost(flops, moved, exps=0):
    return pl.CostEstimate(flops=flops, bytes_accessed=moved, transcendentals=exps)


def whole(space=pltpu.VMEM):
    return pl.BlockSpec(memory_space=space)


def hop(block, dz, dy):
    route = []
    for i in range(SIDE * SIDE):
        z, y = divmod(i, SIDE)
        route.append((i, ((z + dz) % SIDE) * SIDE + (y + dy) % SIDE))
    return lax.ppermute(block, "ctx", route)


def hop_smp(block, dx, dc):
    route = []
    for i in range(SIDE * 2):
        x, c = divmod(i, 2)
        route.append((i, ((x + dx) % SIDE) * 2 + (c + dc) % 2))
    return lax.ppermute(block, "smp", route)


def dot(a, b):
    return lax.dot_general(a, b, (((1,), (0,)), ((), ())), preferred_element_type=F32)


def dot_nt(a, b):
    return lax.dot_general(a, b, (((1,), (1,)), ((), ())), preferred_element_type=F32)


def dot_tn(a, b):
    return lax.dot_general(a, b, (((0,), (0,)), ((), ())), preferred_element_type=F32)


def halves(v):
    high = v.astype(BF16)
    return high, (v - high.astype(F32)).astype(BF16)


def spread_matrix():
    lane = lax.broadcasted_iota(jnp.int32, (HEADS, WIDE), 1)
    head = lax.broadcasted_iota(jnp.int32, (HEADS, WIDE), 0)
    return ((lane >= head * 64) & (lane < head * 64 + 64)).astype(F32).astype(BF16)


def spread(v, matrix):
    high, low = halves(v)
    return dot(high, matrix) + dot(low, matrix)


def spread_row(v, matrix):
    return spread(jnp.broadcast_to(v, (8, HEADS)), matrix)[0:1]


def tail_rows(row):
    high, low = halves(row)
    at = lax.broadcasted_iota(jnp.int32, (TAIL, row.shape[1]), 0)
    wide = jnp.where(at == 0, high.astype(F32), jnp.where(at == 1, low.astype(F32), 0.0))
    return wide.astype(BF16)


def tail_value(rows):
    rows = rows.astype(F32)
    return rows[0:1] + rows[1:2]


def turn(a, b):
    return lax.rem(a + b + 2 * SIDE, SIDE)


def pre_kernel(
    y_ref, step_ref, dlog_ref, grad_ref, read_ref, fork_ref,
    rel_ref, scaled_ref, state_ref, m0, m1, m2, m3, message,
):
    y = y_ref[0]
    row = lax.broadcasted_iota(jnp.int32, (CHUNK, CHUNK), 0)
    col = lax.broadcasted_iota(jnp.int32, (CHUNK, CHUNK), 1)
    lower = jnp.where(row >= col, 1.0, 0.0).astype(BF16)
    matrix = spread_matrix()
    rates = step_ref[...] * -jnp.exp(dlog_ref[...])
    totals = []
    for c in range(CHUNKS):
        here = slice(c * CHUNK, (c + 1) * CHUNK)
        part = rates[here]
        high, rest = part.astype(BF16), None
        rest = part - high.astype(F32)
        middle, low = halves(rest)
        rel = dot(lower, high) + dot(lower, middle) + dot(lower, low)
        rel_ref[c] = rel
        totals.append(rel[CHUNK - 1 : CHUNK])
        scaled_ref[here] = (spread(jnp.exp(rel), matrix) * grad_ref[here].astype(F32)).astype(BF16)
    state = None
    for c in reversed(range(CHUNKS)):
        here = slice(c * CHUNK, (c + 1) * CHUNK)
        local = dot_tn(read_ref[here], scaled_ref[here])
        if state is None:
            state = local
        else:
            state = local + spread_row(jnp.exp(totals[c]), matrix) * state
        if c > 0:
            state_ref[c - 1] = state.astype(BF16)
    message[0:128] = state.astype(BF16)
    message[128:256] = (fork_ref[0] + fork_ref[1]).T.astype(BF16)
    decay = spread_row(jnp.exp(totals[0] + totals[1] + totals[2] + totals[3]), matrix)
    message[256 : 256 + TAIL] = tail_rows(decay)
    for d, out in enumerate((m0, m1, m2, m3)):
        start = pl.multiple_of(turn(y, d) * QUARTER, QUARTER)
        out[...] = message[:, pl.ds(start, QUARTER)]


def pre(y, step_size, decay_log, out_grad, reads, fork_grad):
    sent = jax.ShapeDtypeStruct((256 + TAIL, QUARTER), BF16)
    return pl.pallas_call(
        pre_kernel,
        out_shape=[
            jax.ShapeDtypeStruct((CHUNKS, CHUNK, HEADS), F32),
            jax.ShapeDtypeStruct((CHUNKS * CHUNK, WIDE), BF16),
            jax.ShapeDtypeStruct((CHUNKS - 1, 128, WIDE), BF16),
        ]
        + [sent] * 4,
        in_specs=[whole(pltpu.SMEM)] + [whole()] * 5,
        out_specs=[whole()] * 7,
        scratch_shapes=[pltpu.VMEM((256 + TAIL, WIDE), BF16)],
        compiler_params=params(),
        cost_estimate=cost(400_000_000, 5_000_000),
    )(y, step_size, decay_log, out_grad, reads, fork_grad)


def group_kernel(y_ref, a0, a1, a2, a3, out_ref, stack):
    y = y_ref[0]
    for d, ref in enumerate((a0, a1, a2, a3)):
        stack[d] = ref[...]
    total = rate = fork = None
    for b in reversed(range(SIDE)):
        at = turn(y, -b)
        local = stack[at, 0:128].astype(F32)
        decay = tail_value(stack[at, 256 : 256 + TAIL])
        share = stack[at, 128:256].astype(F32)
        if total is None:
            total, rate, fork = local, decay, share
        else:
            total, rate, fork = local + decay * total, rate * decay, fork + share
    out_ref[0:128] = total.astype(BF16)
    out_ref[128:256] = fork.astype(BF16)
    out_ref[256 : 256 + TAIL] = tail_rows(rate)


def group(y, arrived):
    return pl.pallas_call(
        group_kernel,
        out_shape=jax.ShapeDtypeStruct((256 + TAIL, QUARTER), BF16),
        in_specs=[whole(pltpu.SMEM)] + [whole()] * 4,
        out_specs=whole(),
        scratch_shapes=[pltpu.VMEM((SIDE, 256 + TAIL, QUARTER), BF16)],
        compiler_params=params(),
        cost_estimate=cost(1_000_000, 600_000),
    )(y, *arrived)


def carry_kernel(y_ref, z_ref, a0, a1, a2, a3, b0, b1, b2, b3, c0, c1, c2, c3, first, second, out):
    y, z = y_ref[0], z_ref[0]
    for d, ref in enumerate((a0, a1, a2, a3)):
        first[d] = ref[...]
    for d, ref in enumerate((b0, b1, b2, b3)):
        second[d] = ref[...]
    carry = jnp.zeros((128, QUARTER), F32)
    for d in range(SIDE):
        carry = carry + second[d, 128:256].astype(F32)
    mine = carry
    for b in (3, 2, 1):
        at = turn(z, -b)
        decay = tail_value(second[at, 256 : 256 + TAIL])
        carry = second[at, 0:128].astype(F32) + decay * carry
        mine = jnp.where(z == b - 1, carry, mine)
    out[SIDE - 1] = mine.astype(BF16)
    for b in (3, 2, 1):
        at = turn(y, -b)
        decay = tail_value(first[at, 256 : 256 + TAIL])
        mine = first[at, 0:128].astype(F32) + decay * mine
        out[b - 1] = mine.astype(BF16)
    for d, ref in enumerate((c0, c1, c2, c3)):
        ref[...] = out[turn(y, d)]


def carry_over(y, z, first, second):
    return pl.pallas_call(
        carry_kernel,
        out_shape=[jax.ShapeDtypeStruct((128, QUARTER), BF16)] * 4,
        in_specs=[whole(pltpu.SMEM)] * 2 + [whole()] * 8,
        out_specs=[whole()] * 4,
        scratch_shapes=[
            pltpu.VMEM((SIDE, 256 + TAIL, QUARTER), BF16),
            pltpu.VMEM((SIDE, 256 + TAIL, QUARTER), BF16),
            pltpu.VMEM((SIDE, 128, QUARTER), BF16),
        ],
        compiler_params=params(),
        cost_estimate=cost(1_000_000, 1_400_000),
    )(y, z, *first, *second)


def diag_kernel(rel_ref, relt_ref, step_ref, skip_ref, read_ref, write_ref, grad_ref, out_ref):
    matrix = spread_matrix()
    row = lax.broadcasted_iota(jnp.int32, (CHUNK, CHUNK), 0)
    col = lax.broadcasted_iota(jnp.int32, (CHUNK, CHUNK), 1)
    scores = jnp.where(col >= row, dot_nt(write_ref[...], read_ref[...]), 0.0)
    rel, relt = rel_ref[0], relt_ref[0]
    parts = []
    for pair in range(HEADS // 2):
        grads = grad_ref[:, pair * 128 : pair * 128 + 128]
        both = []
        for h in (2 * pair, 2 * pair + 1):
            kernel = jnp.exp(jnp.minimum(relt[h : h + 1] - rel[:, h : h + 1], 0.0))
            both.append(dot((scores * kernel).astype(BF16), grads))
        parts.append(jnp.where(col < 64, both[0], both[1]))
    steps = spread(step_ref[...], matrix)
    for pair in range(HEADS // 2):
        at = slice(pair * 128, pair * 128 + 128)
        out_ref[:, at] = steps[:, at] * parts[pair] + skip_ref[:, at] * grad_ref[:, at].astype(F32)


def diag(rel, relt, step_size, skip_row, reads, writes, out_grad):
    by_chunk = lambda c: (c, 0)
    return pl.pallas_call(
        diag_kernel,
        grid=(CHUNKS,),
        out_shape=jax.ShapeDtypeStruct((CHUNKS * CHUNK, WIDE), F32),
        in_specs=[
            pl.BlockSpec((1, CHUNK, HEADS), lambda c: (c, 0, 0)),
            pl.BlockSpec((1, HEADS, CHUNK), lambda c: (c, 0, 0)),
            pl.BlockSpec((CHUNK, HEADS), by_chunk),
            pl.BlockSpec((1, WIDE), lambda c: (0, 0)),
            pl.BlockSpec((CHUNK, 128), by_chunk),
            pl.BlockSpec((CHUNK, 128), by_chunk),
            pl.BlockSpec((CHUNK, WIDE), by_chunk),
        ],
        out_specs=pl.BlockSpec((CHUNK, WIDE), by_chunk),
        compiler_params=params(),
        cost_estimate=cost(1_500_000_000, 3_500_000, 1_000_000),
    )(rel, relt, step_size, skip_row, reads, writes, out_grad)


def x_kernel(
    y_ref, q0, q1, q2, q3, state_ref, rel_ref, step_ref, write_ref, base_ref,
    x_ref, full_ref, carried,
):
    y, c = y_ref[0], pl.program_id(0)
    matrix = spread_matrix()

    @pl.when(c == 0)
    def _():
        for d, ref in enumerate((q0, q1, q2, q3)):
            start = pl.multiple_of(turn(y, -d) * QUARTER, QUARTER)
            carried[:, pl.ds(start, QUARTER)] = ref[...]

    later = jnp.zeros((1, HEADS), F32)
    for k in range(CHUNKS):
        later = later + jnp.where(k > c, rel_ref[k, CHUNK - 1 : CHUNK], 0.0)
    share = spread_row(jnp.exp(later), matrix) * carried[...].astype(F32)
    full = jnp.where(c < CHUNKS - 1, state_ref[0].astype(F32) + share, share).astype(BF16)
    full_ref[0] = full
    rel = rel_ref[c]
    weights = spread(step_ref[...] * jnp.exp(rel[CHUNK - 1 : CHUNK] - rel), matrix)
    x_ref[...] = (base_ref[...] + weights * dot(write_ref[...], full)).astype(BF16)


def x_final(y, quarters, states, rel, step_size, writes, base):
    by_chunk = lambda c: (c, 0)
    return pl.pallas_call(
        x_kernel,
        grid=(CHUNKS,),
        out_shape=[
            jax.ShapeDtypeStruct((CHUNKS * CHUNK, WIDE), BF16),
            jax.ShapeDtypeStruct((CHUNKS, 128, WIDE), BF16),
        ],
        in_specs=[whole(pltpu.SMEM)]
        + [pl.BlockSpec((128, QUARTER), lambda c: (0, 0))] * 4
        + [
            pl.BlockSpec((1, 128, WIDE), lambda c: (jnp.minimum(c, CHUNKS - 2), 0, 0)),
            pl.BlockSpec((CHUNKS, CHUNK, HEADS), lambda c: (0, 0, 0)),
            pl.BlockSpec((CHUNK, HEADS), by_chunk),
            pl.BlockSpec((CHUNK, 128), by_chunk),
            pl.BlockSpec((CHUNK, WIDE), by_chunk),
        ],
        out_specs=[
            pl.BlockSpec((CHUNK, WIDE), by_chunk),
            pl.BlockSpec((1, 128, WIDE), lambda c: (c, 0, 0)),
        ],
        scratch_shapes=[pltpu.VMEM((128, WIDE), BF16)],
        compiler_params=params(),
        cost_estimate=cost(300_000_000, 5_500_000),
    )(y, *quarters, states, rel, step_size, writes, base)


def vector_kernel(
    rel_ref, relt_ref, step_ref, read_ref, write_ref, grad_ref, scaled_ref, inputs_ref, full_ref,
    start_ref, wgrad_ref, rgrad_ref, state,
):
    matrix = spread_matrix()

    @pl.when(pl.program_id(0) == 0)
    def _():
        state[...] = start_ref[...].T

    row = lax.broadcasted_iota(jnp.int32, (CHUNK, CHUNK), 0)
    col = lax.broadcasted_iota(jnp.int32, (CHUNK, CHUNK), 1)
    rel, relt, step = rel_ref[0], relt_ref[0], step_ref[...]
    coupling = jnp.zeros((CHUNK, CHUNK), F32)
    for pair in range(HEADS // 2):
        at = slice(pair * 128, pair * 128 + 128)
        grads = grad_ref[:, at]
        inputs = inputs_ref[:, at]
        for k in range(2):
            h = 2 * pair + k
            own = jnp.where((col >= 64) == (k == 1), inputs.astype(F32), 0.0).astype(BF16)
            kernel = jnp.exp(jnp.minimum(relt[h : h + 1] - rel[:, h : h + 1], 0.0))
            coupling = coupling + step[:, h : h + 1] * kernel * dot_nt(own, grads)
    coupling = jnp.where(col >= row, coupling, 0.0).astype(BF16)
    last = rel[CHUNK - 1 : CHUNK]
    weights = spread(step * jnp.exp(last - rel), matrix)
    weighted = (weights * inputs_ref[...].astype(F32)).astype(BF16)
    wgrad_ref[...] = dot_nt(weighted, full_ref[0]) + dot(coupling, read_ref[...])
    rgrad_ref[...] = dot_nt(scaled_ref[...], state[...].astype(BF16)) + dot_tn(
        coupling, write_ref[...]
    )
    state[...] = spread_row(jnp.exp(last), matrix) * state[...] + dot_tn(write_ref[...], weighted)


def vectors(rel, relt, step_size, reads, writes, out_grad, scaled, inputs, full, start_state):
    by_chunk = lambda c: (c, 0)
    return pl.pallas_call(
        vector_kernel,
        grid=(CHUNKS,),
        out_shape=[jax.ShapeDtypeStruct((CHUNKS * CHUNK, 128), F32)] * 2,
        in_specs=[
            pl.BlockSpec((1, CHUNK, HEADS), lambda c: (c, 0, 0)),
            pl.BlockSpec((1, HEADS, CHUNK), lambda c: (c, 0, 0)),
            pl.BlockSpec((CHUNK, HEADS), by_chunk),
            pl.BlockSpec((CHUNK, 128), by_chunk),
            pl.BlockSpec((CHUNK, 128), by_chunk),
            pl.BlockSpec((CHUNK, WIDE), by_chunk),
            pl.BlockSpec((CHUNK, WIDE), by_chunk),
            pl.BlockSpec((CHUNK, WIDE), by_chunk),
            pl.BlockSpec((1, 128, WIDE), lambda c: (c, 0, 0)),
            pl.BlockSpec((WIDE, 128), lambda c: (0, 0)),
        ],
        out_specs=[pl.BlockSpec((CHUNK, 128), by_chunk)] * 2,
        scratch_shapes=[pltpu.VMEM((128, WIDE), F32)],
        compiler_params=params(),
        cost_estimate=cost(3_000_000_000, 5_000_000, 1_000_000),
    )(rel, relt, step_size, reads, writes, out_grad, scaled, inputs, full, start_state)


def project_kernel(x_ref, w_ref, out_ref):
    out_ref[...] = dot(x_ref[...], w_ref[...]).astype(BF16)


def project(layer_input, proj_weight):
    rows, depth = layer_input.shape
    wide = proj_weight.shape[1]
    tile = 256
    return pl.pallas_call(
        project_kernel,
        grid=(wide // tile,),
        out_shape=jax.ShapeDtypeStruct((rows, wide), BF16),
        in_specs=[
            pl.BlockSpec((rows, depth), lambda i: (0, 0)),
            pl.BlockSpec((depth, tile), lambda i: (0, i)),
        ],
        out_specs=pl.BlockSpec((rows, tile), lambda i: (0, i)),
        compiler_params=params(),
        cost_estimate=cost(2 * rows * depth * wide, 2 * (rows * depth + depth * wide + rows * wide)),
    )(layer_input, proj_weight)


def pair_kernel(idx_ref, up_ref, down_ref, x_ref, *refs):
    more, (up_out, down_out) = refs[:-2], refs[-2:]
    up = dot_tn(up_ref[...], x_ref[...])
    down = dot_tn(down_ref[...], x_ref[...])
    if more:
        up = up + more[0][0].astype(F32)
        down = down + more[1][0].astype(F32)
    up_out[0] = up.astype(BF16)
    down_out[0] = down.astype(BF16)


def pair_product(idx, layer_input, x_grad, side, more=()):
    rows = layer_input.shape[0]
    block = pl.BlockSpec((1, 256, 512), lambda g, s: (g, 0, 0))
    return pl.pallas_call(
        pair_kernel,
        grid_spec=pltpu.PrefetchScalarGridSpec(
            num_scalar_prefetch=1,
            grid=(2,),
            in_specs=[
                pl.BlockSpec((rows, 256), lambda g, s: (0, s[g])),
                pl.BlockSpec((rows, 256), lambda g, s: (0, s[g + 2])),
                pl.BlockSpec((rows, 512), lambda g, s: (0, side)),
            ]
            + [block] * len(more),
            out_specs=[block] * 2,
        ),
        out_shape=[jax.ShapeDtypeStruct((2, 256, 512), BF16)] * 2,
        compiler_params=params(),
        cost_estimate=cost(2 * 1024 * 512 * rows, 2 * (1024 * rows + 512 * rows + 1024 * 512)),
    )(idx, layer_input, layer_input, x_grad, *more)


def own_kernel(
    idx_ref, cols_ref, x_ref, below_add, below_plain, above_plain, above_add,
    up_out, down_out, up_keep, down_keep, own_out,
):
    g = pl.program_id(0)
    product = dot_tn(cols_ref[...], x_ref[...])
    below = jnp.where(g < 2, below_add[0].astype(F32), below_plain[0].astype(F32))
    above = jnp.where(g < 2, above_plain[0].astype(F32), above_add[0].astype(F32))
    total = product + below + above

    @pl.when(g == 0)
    def _():
        up_out[0:128] = total[0:128].astype(BF16)
        down_out[0:128] = total[128:256].astype(BF16)

    @pl.when(g == 1)
    def _():
        up_keep[...] = total[0:128].astype(BF16)
        up_out[128:256] = total[128:256].astype(BF16)

    @pl.when(g == 2)
    def _():
        down_out[128:256] = total[0:128].astype(BF16)
        down_keep[...] = total[128:256].astype(BF16)

    @pl.when(g == 3)
    def _():
        own_out[...] = total


def own_product(idx, layer_input, x_grad, side, below_add, below_plain, above_plain, above_add):
    rows = layer_input.shape[0]
    first = pl.BlockSpec((1, 256, 512), lambda g, s: (jnp.minimum(g, 1), 0, 0))
    second = pl.BlockSpec((1, 256, 512), lambda g, s: (jnp.maximum(g - 2, 0), 0, 0))
    kept = lambda n: pl.BlockSpec((n, 512), lambda g, s: (0, 0))
    return pl.pallas_call(
        own_kernel,
        grid_spec=pltpu.PrefetchScalarGridSpec(
            num_scalar_prefetch=1,
            grid=(4,),
            in_specs=[
                pl.BlockSpec((rows, 256), lambda g, s: (0, s[g])),
                pl.BlockSpec((rows, 512), lambda g, s: (0, side)),
                first,
                second,
                first,
                second,
            ],
            out_specs=[kept(256), kept(256), kept(128), kept(128), kept(256)],
        ),
        out_shape=[
            jax.ShapeDtypeStruct((256, 512), BF16),
            jax.ShapeDtypeStruct((256, 512), BF16),
            jax.ShapeDtypeStruct((128, 512), BF16),
            jax.ShapeDtypeStruct((128, 512), BF16),
            jax.ShapeDtypeStruct((256, 512), F32),
        ],
        compiler_params=params(),
        cost_estimate=cost(2 * 1024 * 512 * rows, 2 * (1024 * rows + 512 * rows + 3 * 1024 * 512)),
    )(idx, layer_input, x_grad, below_add, below_plain, above_plain, above_add)


def add_kernel(up_keep, down_keep, from_below, from_above, up_out, down_out):
    n = up_keep.shape[0]
    up_out[...] = (up_keep[...].astype(F32) + from_below[0:n].astype(F32)).astype(BF16)
    down_out[...] = (down_keep[...].astype(F32) + from_above[0:n].astype(F32)).astype(BF16)


def add_two(up_keep, down_keep, from_below, from_above):
    size = up_keep.shape
    return pl.pallas_call(
        add_kernel,
        out_shape=[jax.ShapeDtypeStruct(size, BF16)] * 2,
        in_specs=[whole()] * 4,
        out_specs=[whole()] * 2,
        compiler_params=params(),
        cost_estimate=cost(2 * size[0] * size[1], 12 * size[0] * size[1]),
    )(up_keep, down_keep, from_below, from_above)


def weight_kernel(scale, *refs):
    out = refs[-1]
    for side in range(2):
        own, below, above, below_add, above_add = refs[5 * side : 5 * side + 5]
        at = slice(512 * side, 512 * side + 512)
        top = own[0:128] + below_add[...].astype(F32) + above[128:256].astype(F32)
        bottom = own[128:256] + below[128:256].astype(F32) + above_add[...].astype(F32)
        out[0:128, at] = (top * scale).astype(BF16)
        out[128:256, at] = (bottom * scale).astype(BF16)


def weight_final(scale, first, second):
    return pl.pallas_call(
        functools.partial(weight_kernel, scale),
        out_shape=jax.ShapeDtypeStruct((256, WIDE), BF16),
        in_specs=[whole()] * 10,
        out_specs=whole(),
        compiler_params=params(),
        cost_estimate=cost(1_000_000, 3_000_000),
    )(*first, *second)


def weight_grad_of(layer_input, x_grad, z, y, scale):
    def blocks(side, to, groups):
        out = []
        for g in groups:
            if side == 0:
                out.append(turn(z, ORDER[g]) * SIDE + turn(y, to))
            else:
                out.append(turn(z, to) * SIDE + turn(y, ORDER[g]))
        return out

    moves = (lambda b, s: hop(b, 0, s), lambda b, s: hop(b, s, 0))
    arrived = []
    for side in range(2):
        idx = jnp.stack(blocks(side, 2, (0, 1)) + blocks(side, 2, (2, 3)))
        up, down = pair_product(idx, layer_input, x_grad, side)
        arrived.append((moves[side](up, 1), moves[side](down, -1)))
    plain = []
    for side in range(2):
        idx = jnp.stack(blocks(side, 1, (2, 3)) + blocks(side, -1, (0, 1)))
        up, down = pair_product(idx, layer_input, x_grad, side)
        plain.append((moves[side](up, 1), moves[side](down, -1)))
    added = []
    for side in range(2):
        idx = jnp.stack(blocks(side, 1, (0, 1)) + blocks(side, -1, (2, 3)))
        up, down = pair_product(idx, layer_input, x_grad, side, arrived[side])
        added.append((moves[side](up, 1), moves[side](down, -1)))
    results = []
    for side in range(2):
        idx = jnp.stack(blocks(side, 0, (0, 1, 2, 3)))
        move = moves[1 - side]
        up, down, up_keep, down_keep, own = own_product(
            idx, layer_input, x_grad, side,
            added[side][0], plain[side][0], plain[side][1], added[side][1],
        )
        below, above = move(up, 1), move(down, -1)
        up, down = add_two(up_keep, down_keep, below, above)
        results.append((own, below, above, move(up, 1), move(down, -1)))
    return weight_final(scale, *results)


def theirs_kernel(c_ref, x_ref, w_ref, out_ref):
    rows = x_ref[...].reshape(256, WIDE)
    out_ref[...] = dot_nt(rows, w_ref[...]).astype(BF16)


def theirs(other, x_rows, proj_weight):
    depth, tile = proj_weight.shape[0], 512
    return pl.pallas_call(
        theirs_kernel,
        grid_spec=pltpu.PrefetchScalarGridSpec(
            num_scalar_prefetch=1,
            grid=(depth // tile,),
            in_specs=[
                pl.BlockSpec((SIDE, 1, 64, WIDE), lambda i, s: (0, s[0], 0, 0)),
                pl.BlockSpec((tile, WIDE), lambda i, s: (i, 0)),
            ],
            out_specs=pl.BlockSpec((256, tile), lambda i, s: (0, i)),
        ),
        out_shape=jax.ShapeDtypeStruct((256, depth), BF16),
        compiler_params=params(),
        cost_estimate=cost(2 * 256 * depth * WIDE, 2 * depth * WIDE + 512 * depth),
    )(other, x_rows, proj_weight)


def mine_kernel(at_ref, x_ref, w_ref, add_ref, up_out, down_out, up_keep, down_keep, own_out, total):
    x = at_ref[1]
    rows = x_ref[...].reshape(256, WIDE)
    total[...] = (dot_nt(rows, w_ref[...]) + add_ref[...].astype(F32)).reshape(SIDE, 64, -1)
    far, after, before = turn(x, 2), turn(x, 1), turn(x, -1)
    up_out[0:32] = total[far, 0:32].astype(BF16)
    up_out[32:64] = total[after, 32:64].astype(BF16)
    up_keep[...] = total[after, 0:32].astype(BF16)
    down_out[0:32] = total[far, 32:64].astype(BF16)
    down_out[32:64] = total[before, 0:32].astype(BF16)
    down_keep[...] = total[before, 32:64].astype(BF16)
    own_out[...] = total[x]


def mine(at, x_rows, proj_weight, add):
    depth, tile = proj_weight.shape[0], 512
    out = lambda n: pl.BlockSpec((n, tile), lambda i, s: (0, i))
    return pl.pallas_call(
        mine_kernel,
        grid_spec=pltpu.PrefetchScalarGridSpec(
            num_scalar_prefetch=1,
            grid=(depth // tile,),
            in_specs=[
                pl.BlockSpec((SIDE, 1, 64, WIDE), lambda i, s: (0, s[0], 0, 0)),
                pl.BlockSpec((tile, WIDE), lambda i, s: (i, 0)),
                pl.BlockSpec((256, tile), lambda i, s: (0, i)),
            ],
            out_specs=[out(64), out(64), out(32), out(32), out(64)],
            scratch_shapes=[pltpu.VMEM((SIDE, 64, tile), F32)],
        ),
        out_shape=[
            jax.ShapeDtypeStruct((64, depth), BF16),
            jax.ShapeDtypeStruct((64, depth), BF16),
            jax.ShapeDtypeStruct((32, depth), BF16),
            jax.ShapeDtypeStruct((32, depth), BF16),
            jax.ShapeDtypeStruct((64, depth), F32),
        ],
        compiler_params=params(),
        cost_estimate=cost(2 * 256 * depth * WIDE, 2 * depth * WIDE + 1536 * depth),
    )(at, x_rows, proj_weight, add)


def input_kernel(own, below, above, below_add, above_add, out):
    top = own[0:32] + below_add[...].astype(F32) + above[32:64].astype(F32)
    bottom = own[32:64] + below[32:64].astype(F32) + above_add[...].astype(F32)
    out[0:32] = top.astype(BF16)
    out[32:64] = bottom.astype(BF16)


def input_grad_of(x_grad, proj_weight, x, core):
    x_rows = x_grad.reshape(SIDE, 2, 64, WIDE)
    sent = theirs((1 - core).reshape(1), x_rows, proj_weight)
    at = jnp.stack([core, x])
    up, down, up_keep, down_keep, own = mine(at, x_rows, proj_weight, hop_smp(sent, 0, 1))
    below, above = hop_smp(up, 1, 0), hop_smp(down, -1, 0)
    up, down = add_two(up_keep, down_keep, below, above)
    below_add, above_add = hop_smp(up, 1, 0), hop_smp(down, -1, 0)
    return pl.pallas_call(
        input_kernel,
        out_shape=jax.ShapeDtypeStruct((64, proj_weight.shape[0]), BF16),
        in_specs=[whole()] * 5,
        out_specs=whole(),
        compiler_params=params(),
        cost_estimate=cost(1_000_000, 3_000_000),
    )(own, below, above, below_add, above_add)


def body(
    layer_input,
    proj_weight,
    step_size,
    decay_log,
    skip_gain,
    write_vec,
    read_vec,
    out_grad,
    start_state,
    fork_grad,
):
    length = layer_input.shape[0]
    position = lax.axis_index("ctx")
    z, y = position // SIDE, position % SIDE
    column = lax.axis_index("smp")
    x, core = column // 2, column % 2
    y_at, z_at = y.reshape(1), z.reshape(1)
    writes = write_vec[:, 0]
    reads = read_vec[:, 0]
    rel, scaled, states, *messages = pre(
        y_at, step_size, decay_log[None], out_grad, reads, fork_grad.reshape(2, WIDE, 128)
    )
    first = [messages[0]] + [hop(messages[d], 0, d) for d in range(1, SIDE)]
    message = group(y_at, first)
    second = [message] + [hop(message, d, 0) for d in range(1, SIDE)]
    sent = carry_over(y_at, z_at, first, second)
    quarters = [sent[0]] + [hop(sent[d], 0, d) for d in range(1, SIDE)]
    relt = rel.transpose(0, 2, 1)
    skip_row = jnp.repeat(skip_gain, 64)[None]
    base = diag(rel, relt, step_size, skip_row, reads, writes, out_grad)
    inputs = project(layer_input, proj_weight)
    x_grad, full = x_final(y_at, quarters, states, rel, step_size, writes, base)
    scale = (length * lax.axis_size("ctx")) ** (-0.5)
    weight_grad = weight_grad_of(layer_input, x_grad, z, y, scale)
    input_grad = input_grad_of(x_grad, proj_weight, x, core)
    write_grad, read_grad = vectors(
        rel, relt, step_size, reads, writes, out_grad, scaled, inputs, full,
        start_state.reshape(WIDE, 128),
    )
    return (input_grad, weight_grad, write_grad[:, None], read_grad[:, None])


def solution(mesh):
    placed = (
        P("ctx", None),
        P(None, "smp"),
        P("ctx", "smp"),
        P("smp"),
        P("smp"),
        P("ctx", "smp", None),
        P("ctx", "smp", None),
        P("ctx", "smp"),
        P("ctx", "smp", None, None),
        P("ctx", "smp", None, None),
    )
    return jax.shard_map(
        body,
        mesh=mesh,
        in_specs=placed,
        out_specs=(
            P(("ctx", "smp"), None),
            P("ctx", "smp"),
            P("ctx", "smp", None),
            P("ctx", "smp", None),
        ),
        check_vma=False,
    )
```

```python
import functools

import jax
import jax.numpy as jnp
from jax import lax
from jax.experimental import pallas as pl
from jax.experimental.pallas import tpu as pltpu
from jax.sharding import PartitionSpec as P

SIDE = 4
CHUNK = 128
CHUNKS = 4
HEADS = 16
WIDE = 1024
QUARTER = WIDE // SIDE
TAIL = 16
F32 = jnp.float32
BF16 = jnp.bfloat16
ORDER = (2, 1, 3, 0)
VMEM_LIMIT = 64 * 1024 * 1024


def params(limit=VMEM_LIMIT):
    return pltpu.CompilerParams(vmem_limit_bytes=limit)


COST = pl.CostEstimate(flops=1, bytes_accessed=1, transcendentals=0)


def whole(space=pltpu.VMEM):
    return pl.BlockSpec(memory_space=space)


def full_block(*shape):
    return pl.BlockSpec(shape, lambda *_: (0,) * len(shape))


def routed(block, move):
    route = []
    for i in range(SIDE**3 * 2):
        z, y, x, core = i // 32, i // 8 % 4, i // 2 % 4, i % 2
        z, y, x, core = move(z, y, x, core)
        route.append((i, ((z % SIDE * SIDE + y % SIDE) * SIDE + x % SIDE) * 2 + core % 2))
    return lax.ppermute(block, ("ctx", "smp"), route)


def hop(block, dz, dy):
    return routed(block, lambda z, y, x, core: (z + dz, y + dy, x, core))


def hop_smp(block, dx, dc):
    return routed(block, lambda z, y, x, core: (z, y, x + dx, core + dc))


def first_hop(block, d, to_other):
    def move(z, y, x, core):
        core = core ^ to_other
        return (z, y + d, x, core) if core == 0 else (z + d, y, x, core)

    return routed(block, move)


def second_hop(block, d, to_other):
    def move(z, y, x, core):
        return (z + d, y, x, core ^ to_other) if core == 0 else (z, y + d, x, core ^ to_other)

    return routed(block, move)


def dot(a, b):
    return lax.dot_general(a, b, (((1,), (0,)), ((), ())), preferred_element_type=F32)


def dot_nt(a, b):
    return lax.dot_general(a, b, (((1,), (1,)), ((), ())), preferred_element_type=F32)


def dot_tn(a, b):
    return lax.dot_general(a, b, (((0,), (0,)), ((), ())), preferred_element_type=F32)


def halves(v):
    high = v.astype(BF16)
    return high, (v - high.astype(F32)).astype(BF16)


def spread_matrix():
    lane = lax.broadcasted_iota(jnp.int32, (HEADS, WIDE), 1)
    head = lax.broadcasted_iota(jnp.int32, (HEADS, WIDE), 0)
    return ((lane >= head * 64) & (lane < head * 64 + 64)).astype(F32).astype(BF16)


def spread(v, matrix):
    high, low = halves(v)
    return dot(high, matrix) + dot(low, matrix)


def spread_row(v, matrix):
    return spread(jnp.broadcast_to(v, (8, HEADS)), matrix)[0:1]


def tail_rows(row):
    high, low = halves(row)
    at = lax.broadcasted_iota(jnp.int32, (TAIL, row.shape[1]), 0)
    wide = jnp.where(at == 0, high.astype(F32), jnp.where(at == 1, low.astype(F32), 0.0))
    return wide.astype(BF16)


def tail_value(rows):
    rows = rows.astype(F32)
    return rows[0:1] + rows[1:2]


def turn(a, b):
    return lax.rem(a + b + 2 * SIDE, SIDE)


def pieces(v):
    high = v.astype(BF16)
    middle, low = halves(v - high.astype(F32))
    return high, middle, low


def pre_kernel(
    at_ref, dlog_ref, stept_ref, grad_ref, read_ref, fork_ref,
    rel_ref, relt_ref, step_ref, scaled_ref, state_ref, m0, m1, m2, m3, message,
):
    y = at_ref[1]
    row = lax.broadcasted_iota(jnp.int32, (CHUNK, CHUNK), 0)
    col = lax.broadcasted_iota(jnp.int32, (CHUNK, CHUNK), 1)
    lower = jnp.where(row >= col, 1.0, 0.0).astype(BF16)
    upper = jnp.where(row <= col, 1.0, 0.0).astype(BF16)
    same = jnp.where(row == col, 1.0, 0.0).astype(BF16)
    matrix = spread_matrix()
    head = lax.broadcasted_iota(jnp.int32, (HEADS, CHUNK), 0)
    decay_log = jnp.zeros((HEADS, CHUNK), F32)
    for h in range(HEADS):
        decay_log = jnp.where(head == h, dlog_ref[h], decay_log)
    decay_rate = -jnp.exp(decay_log)
    totals = []
    for c in range(CHUNKS):
        here = slice(c * CHUNK, (c + 1) * CHUNK)
        steps = stept_ref[:, here]
        rates = pieces(steps * decay_rate)
        rel = dot_nt(lower, rates[0]) + dot_nt(lower, rates[1]) + dot_nt(lower, rates[2])
        rel_ref[c] = rel
        relt_ref[c] = dot(rates[0], upper) + dot(rates[1], upper) + dot(rates[2], upper)
        cut = pieces(steps)
        step_ref[here] = dot_nt(same, cut[0]) + dot_nt(same, cut[1]) + dot_nt(same, cut[2])
        totals.append(rel[CHUNK - 1 : CHUNK])
        scaled_ref[here] = (spread(jnp.exp(rel), matrix) * grad_ref[here].astype(F32)).astype(BF16)
    state = None
    for c in reversed(range(CHUNKS)):
        here = slice(c * CHUNK, (c + 1) * CHUNK)
        local = dot_tn(read_ref[here], scaled_ref[here])
        if state is None:
            state = local
        else:
            state = local + spread_row(jnp.exp(totals[c]), matrix) * state
        if c > 0:
            state_ref[c - 1] = state.astype(BF16)
    message[0:128] = state.astype(BF16)
    message[128:256] = (fork_ref[0] + fork_ref[1]).T.astype(BF16)
    decay = spread_row(jnp.exp(totals[0] + totals[1] + totals[2] + totals[3]), matrix)
    message[256 : 256 + TAIL] = tail_rows(decay)
    for d, out in enumerate((m0, m1, m2, m3)):
        start = pl.multiple_of(turn(y, d) * QUARTER, QUARTER)
        out[...] = message[:, pl.ds(start, QUARTER)]


def pre(at, decay_log, stept, out_grad, reads, fork_grad):
    length = CHUNKS * CHUNK
    sent = jax.ShapeDtypeStruct((256 + TAIL, QUARTER), BF16)
    return pl.pallas_call(
        pre_kernel,
        grid=(1,),
        out_shape=[
            jax.ShapeDtypeStruct((CHUNKS, CHUNK, HEADS), F32),
            jax.ShapeDtypeStruct((CHUNKS, HEADS, CHUNK), F32),
            jax.ShapeDtypeStruct((length, HEADS), F32),
            jax.ShapeDtypeStruct((length, WIDE), BF16),
            jax.ShapeDtypeStruct((CHUNKS - 1, 128, WIDE), BF16),
        ]
        + [sent] * 4,
        in_specs=[
            whole(pltpu.SMEM),
            whole(pltpu.SMEM),
            full_block(HEADS, length),
            full_block(length, WIDE),
            full_block(length, 128),
            full_block(2, WIDE, 128),
        ],
        out_specs=[
            full_block(CHUNKS, CHUNK, HEADS),
            full_block(CHUNKS, HEADS, CHUNK),
            full_block(length, HEADS),
            full_block(length, WIDE),
            full_block(CHUNKS - 1, 128, WIDE),
        ]
        + [full_block(256 + TAIL, QUARTER)] * 4,
        scratch_shapes=[pltpu.VMEM((256 + TAIL, WIDE), BF16)],
        compiler_params=params(),
        cost_estimate=COST,
    )(at, decay_log, stept, out_grad, reads, fork_grad)


def group_kernel(at_ref, a0, a1, a2, a3, out_ref, stack):
    y = at_ref[1]
    for d, ref in enumerate((a0, a1, a2, a3)):
        stack[d] = ref[...]
    total = rate = fork = None
    for b in reversed(range(SIDE)):
        at = turn(y, -b)
        local = stack[at, 0:128].astype(F32)
        decay = tail_value(stack[at, 256 : 256 + TAIL])
        share = stack[at, 128:256].astype(F32)
        if total is None:
            total, rate, fork = local, decay, share
        else:
            total, rate, fork = local + decay * total, rate * decay, fork + share
    out_ref[0:128] = total.astype(BF16)
    out_ref[128:256] = fork.astype(BF16)
    out_ref[256 : 256 + TAIL] = tail_rows(rate)


def group(at, arrived):
    return pl.pallas_call(
        group_kernel,
        grid=(1,),
        out_shape=jax.ShapeDtypeStruct((256 + TAIL, QUARTER), BF16),
        in_specs=[whole(pltpu.SMEM)] + [full_block(256 + TAIL, QUARTER)] * 4,
        out_specs=full_block(256 + TAIL, QUARTER),
        scratch_shapes=[pltpu.VMEM((SIDE, 256 + TAIL, QUARTER), BF16)],
        compiler_params=params(),
        cost_estimate=COST,
    )(at, *arrived)


def carry_kernel(at_ref, a0, a1, a2, a3, b0, b1, b2, b3, c0, c1, c2, c3, first, second, out):
    z, y = at_ref[0], at_ref[1]
    for d, ref in enumerate((a0, a1, a2, a3)):
        first[d] = ref[...]
    for d, ref in enumerate((b0, b1, b2, b3)):
        second[d] = ref[...]
    carry = jnp.zeros((128, QUARTER), F32)
    for d in range(SIDE):
        carry = carry + second[d, 128:256].astype(F32)
    mine = carry
    for b in (3, 2, 1):
        at = turn(z, -b)
        decay = tail_value(second[at, 256 : 256 + TAIL])
        carry = second[at, 0:128].astype(F32) + decay * carry
        mine = jnp.where(z == b - 1, carry, mine)
    out[SIDE - 1] = mine.astype(BF16)
    for b in (3, 2, 1):
        at = turn(y, -b)
        decay = tail_value(first[at, 256 : 256 + TAIL])
        mine = first[at, 0:128].astype(F32) + decay * mine
        out[b - 1] = mine.astype(BF16)
    for d, ref in enumerate((c0, c1, c2, c3)):
        ref[...] = out[turn(y, d)]


def carry_over(at, first, second):
    return pl.pallas_call(
        carry_kernel,
        grid=(1,),
        out_shape=[jax.ShapeDtypeStruct((128, QUARTER), BF16)] * 4,
        in_specs=[whole(pltpu.SMEM)] + [full_block(256 + TAIL, QUARTER)] * 8,
        out_specs=[full_block(128, QUARTER)] * 4,
        scratch_shapes=[
            pltpu.VMEM((SIDE, 256 + TAIL, QUARTER), BF16),
            pltpu.VMEM((SIDE, 256 + TAIL, QUARTER), BF16),
            pltpu.VMEM((SIDE, 128, QUARTER), BF16),
        ],
        compiler_params=params(),
        cost_estimate=COST,
    )(at, *first, *second)


def diag_kernel(skip_ref, rel_ref, relt_ref, step_ref, read_ref, write_ref, grad_ref, out_ref):
    matrix = spread_matrix()
    row = lax.broadcasted_iota(jnp.int32, (CHUNK, CHUNK), 0)
    col = lax.broadcasted_iota(jnp.int32, (CHUNK, CHUNK), 1)
    for c in range(2):
        here = slice(c * CHUNK, (c + 1) * CHUNK)
        scores = jnp.where(col >= row, dot_nt(write_ref[here], read_ref[here]), 0.0)
        rel, relt = rel_ref[c], relt_ref[c]
        steps = spread(step_ref[here], matrix)
        for pair in range(HEADS // 2):
            at = slice(pair * 128, pair * 128 + 128)
            grads = grad_ref[here, at]
            both = []
            for h in (2 * pair, 2 * pair + 1):
                kernel = jnp.exp(jnp.minimum(relt[h : h + 1] - rel[:, h : h + 1], 0.0))
                both.append(dot((scores * kernel).astype(BF16), grads))
            part = steps[:, at] * jnp.where(col < 64, both[0], both[1])
            skip = jnp.where(col < 64, skip_ref[2 * pair], skip_ref[2 * pair + 1])
            out_ref[here, at] = (part + skip * grads.astype(F32)).astype(BF16)


def diag(skip_gain, rel, relt, step_size, reads, writes, out_grad):
    by_two = lambda c: (c, 0)
    rows = 2 * CHUNK
    return pl.pallas_call(
        diag_kernel,
        grid=(CHUNKS // 2,),
        out_shape=jax.ShapeDtypeStruct((CHUNKS * CHUNK, WIDE), BF16),
        in_specs=[
            whole(pltpu.SMEM),
            pl.BlockSpec((2, CHUNK, HEADS), lambda c: (c, 0, 0)),
            pl.BlockSpec((2, HEADS, CHUNK), lambda c: (c, 0, 0)),
            pl.BlockSpec((rows, HEADS), by_two),
            pl.BlockSpec((rows, 128), by_two),
            pl.BlockSpec((rows, 128), by_two),
            pl.BlockSpec((rows, WIDE), by_two),
        ],
        out_specs=pl.BlockSpec((rows, WIDE), by_two),
        compiler_params=params(),
        cost_estimate=COST,
    )(skip_gain, rel, relt, step_size, reads, writes, out_grad)


def x_kernel(
    at_ref, q0, q1, q2, q3, state_ref, rel_ref, step_ref, write_ref, base_ref,
    keep_ref, give_ref, mine_ref, theirs_ref, full_ref, carried, x_ref,
):
    y, core = at_ref[1], at_ref[3]
    matrix = spread_matrix()
    for d, ref in enumerate((q0, q1, q2, q3)):
        start = pl.multiple_of(turn(y, -d) * QUARTER, QUARTER)
        carried[:, pl.ds(start, QUARTER)] = ref[...]
    later = jnp.zeros((1, HEADS), F32)
    for c in reversed(range(CHUNKS)):
        here = slice(c * CHUNK, (c + 1) * CHUNK)
        rel = rel_ref[c]
        last = rel[CHUNK - 1 : CHUNK]
        if c == CHUNKS - 1:
            full = carried[...]
        else:
            share = spread_row(jnp.exp(later), matrix) * carried[...].astype(F32)
            full = (state_ref[c].astype(F32) + share).astype(BF16)
        full_ref[c] = full
        weights = spread(step_ref[here] * jnp.exp(last - rel), matrix)
        x = (base_ref[here].astype(F32) + weights * dot(write_ref[here], full)).astype(BF16)
        for k in range(2):
            x_ref[c, k] = x[k * 64 : k * 64 + 64]
        later = later + last
    start = pl.multiple_of(core * 512, 512)
    other = pl.multiple_of((1 - core) * 512, 512)
    for c in range(CHUNKS):
        for k in range(2):
            here = slice(c * CHUNK + k * 64, c * CHUNK + k * 64 + 64)
            keep_ref[here] = x_ref[c, k, :, pl.ds(start, 512)]
            give_ref[here] = x_ref[c, k, :, pl.ds(other, 512)]
        there = slice(c * 64, c * 64 + 64)
        mine_ref[there] = x_ref[c, core]
        theirs_ref[there] = x_ref[c, 1 - core]


def x_final(at, quarters, states, rel, step_size, writes, base):
    rows = CHUNKS * CHUNK
    half, rest = (rows, 512), (rows // 2, WIDE)
    return pl.pallas_call(
        x_kernel,
        grid=(1,),
        in_specs=[whole(pltpu.SMEM)]
        + [full_block(128, QUARTER)] * 4
        + [
            full_block(CHUNKS - 1, 128, WIDE),
            full_block(CHUNKS, CHUNK, HEADS),
            full_block(rows, HEADS),
            full_block(rows, 128),
            full_block(rows, WIDE),
        ],
        out_specs=[full_block(*half)] * 2 + [full_block(*rest)] * 2 + [full_block(CHUNKS, 128, WIDE)],
        scratch_shapes=[pltpu.VMEM((128, WIDE), BF16), pltpu.VMEM((CHUNKS, 2, 64, WIDE), BF16)],
        out_shape=[jax.ShapeDtypeStruct(half, BF16)] * 2
        + [jax.ShapeDtypeStruct(rest, BF16)] * 2
        + [jax.ShapeDtypeStruct((CHUNKS, 128, WIDE), BF16)],
        compiler_params=params(),
        cost_estimate=COST,
    )(at, *quarters, states, rel, step_size, writes, base)


def vector_kernel(
    rel_ref, relt_ref, step_ref, read_ref, write_ref, grad_ref, scaled_ref, first_ref, second_ref,
    full_ref, start_ref, wgrad_ref, rgrad_ref, state, inputs_ref,
):
    matrix = spread_matrix()
    inputs_ref[:, : WIDE // 2] = first_ref[...]
    inputs_ref[:, WIDE // 2 :] = second_ref[...]

    @pl.when(pl.program_id(0) == 0)
    def _():
        state[...] = start_ref[...].T

    row = lax.broadcasted_iota(jnp.int32, (CHUNK, CHUNK), 0)
    col = lax.broadcasted_iota(jnp.int32, (CHUNK, CHUNK), 1)
    rel, relt, step = rel_ref[0], relt_ref[0], step_ref[...]
    coupling = jnp.zeros((CHUNK, CHUNK), F32)
    for pair in range(HEADS // 2):
        at = slice(pair * 128, pair * 128 + 128)
        grads = grad_ref[:, at]
        inputs = inputs_ref[:, at]
        for k in range(2):
            h = 2 * pair + k
            own = jnp.where((col >= 64) == (k == 1), inputs.astype(F32), 0.0).astype(BF16)
            kernel = jnp.exp(jnp.minimum(relt[h : h + 1] - rel[:, h : h + 1], 0.0))
            coupling = coupling + step[:, h : h + 1] * kernel * dot_nt(own, grads)
    coupling = jnp.where(col >= row, coupling, 0.0).astype(BF16)
    last = rel[CHUNK - 1 : CHUNK]
    weights = spread(step * jnp.exp(last - rel), matrix)
    weighted = (weights * inputs_ref[...].astype(F32)).astype(BF16)
    wgrad_ref[...] = dot_nt(weighted, full_ref[0]) + dot(coupling, read_ref[...])
    rgrad_ref[...] = dot_nt(scaled_ref[...], state[...].astype(BF16)) + dot_tn(
        coupling, write_ref[...]
    )
    state[...] = spread_row(jnp.exp(last), matrix) * state[...] + dot_tn(write_ref[...], weighted)


def vectors(rel, relt, step_size, reads, writes, out_grad, scaled, first, second, full, start_state):
    by_chunk = lambda c: (c, 0)
    return pl.pallas_call(
        vector_kernel,
        grid=(CHUNKS,),
        out_shape=[jax.ShapeDtypeStruct((CHUNKS * CHUNK, 128), F32)] * 2,
        in_specs=[
            pl.BlockSpec((1, CHUNK, HEADS), lambda c: (c, 0, 0)),
            pl.BlockSpec((1, HEADS, CHUNK), lambda c: (c, 0, 0)),
            pl.BlockSpec((CHUNK, HEADS), by_chunk),
            pl.BlockSpec((CHUNK, 128), by_chunk),
            pl.BlockSpec((CHUNK, 128), by_chunk),
            pl.BlockSpec((CHUNK, WIDE), by_chunk),
            pl.BlockSpec((CHUNK, WIDE), by_chunk),
            pl.BlockSpec((CHUNK, WIDE // 2), by_chunk),
            pl.BlockSpec((CHUNK, WIDE // 2), by_chunk),
            pl.BlockSpec((1, 128, WIDE), lambda c: (c, 0, 0)),
            pl.BlockSpec((WIDE, 128), lambda c: (0, 0)),
        ],
        out_specs=[pl.BlockSpec((CHUNK, 128), by_chunk)] * 2,
        scratch_shapes=[pltpu.VMEM((128, WIDE), F32), pltpu.VMEM((CHUNK, WIDE), BF16)],
        compiler_params=params(),
        cost_estimate=COST,
    )(rel, relt, step_size, reads, writes, out_grad, scaled, first, second, full, start_state)


def project_kernel(x_ref, w_ref, out_ref, total):
    step = pl.program_id(0)
    product = dot(x_ref[...], w_ref[...])

    @pl.when(step == 0)
    def _():
        total[...] = product

    @pl.when(step == 1)
    def _():
        out_ref[...] = (total[...] + product).astype(BF16)


def project(layer_input, proj_weight, part):
    rows, depth = layer_input.shape
    wide = WIDE // 2
    return pl.pallas_call(
        project_kernel,
        grid=(2,),
        out_shape=jax.ShapeDtypeStruct((rows, wide), BF16),
        in_specs=[
            pl.BlockSpec((rows, depth // 2), lambda i: (0, i)),
            pl.BlockSpec((depth // 2, wide), lambda i: (i, part)),
        ],
        out_specs=pl.BlockSpec((rows, wide), lambda i: (0, 0)),
        scratch_shapes=[pltpu.VMEM((rows, wide), F32)],
        compiler_params=params(),
        cost_estimate=COST,
    )(layer_input, proj_weight)


FAR = ((2, (0, 1)), (2, (2, 3)))
PLAIN = ((1, (2, 3)), (-1, (0, 1)))
ADDED = ((1, (0, 1)), (-1, (2, 3)))


def column_block(s, d, part):
    for_y = turn(s[0], part) * SIDE + turn(s[1], d)
    for_z = turn(s[0], d) * SIDE + turn(s[1], part)
    return jnp.where(s[3] == 0, for_y, for_z)


def columns_spec(d, parts):
    def index(g, s):
        return 0, column_block(s, d, jnp.where(g == 0, ORDER[parts[0]], ORDER[parts[1]]))

    return pl.BlockSpec((CHUNKS * CHUNK, 256), index)


def ring_kernel(at_ref, up_ref, down_ref, keep_ref, got_ref, *refs):
    more, outs = refs[:-2], refs[-2:]
    for k, cols in enumerate((up_ref, down_ref)):
        turned = cols[...].T
        for half, x_ref in enumerate((keep_ref, got_ref)):
            at = slice(512 * half, 512 * half + 512)
            product = dot(turned, x_ref[...])
            if more:
                product = product + more[k][0, :, at].astype(F32)
            outs[k][0, :, at] = product.astype(BF16)


def ring_product(at, way, layer_input, keep, got, more=()):
    rows = layer_input.shape[0]
    (up_to, up_parts), (down_to, down_parts) = way
    block = pl.BlockSpec((1, 256, WIDE), lambda g, s: (g, 0, 0))
    return pl.pallas_call(
        ring_kernel,
        grid_spec=pltpu.PrefetchScalarGridSpec(
            num_scalar_prefetch=1,
            grid=(2,),
            in_specs=[columns_spec(up_to, up_parts), columns_spec(down_to, down_parts)]
            + [full_block(rows, 512)] * 2
            + [block] * len(more),
            out_specs=[block] * 2,
        ),
        out_shape=[jax.ShapeDtypeStruct((2, 256, WIDE), BF16)] * 2,
        compiler_params=params(),
        cost_estimate=COST,
    )(at, layer_input, layer_input, keep, got, *more)


def own_kernel(
    at_ref, first_ref, second_ref, keep_ref, got_ref,
    below_add, below_plain, above_plain, above_add, *outs,
):
    g = pl.program_id(0)
    for k, cols in enumerate((first_ref, second_ref)):
        turned = cols[...].T
        for half, x_ref in enumerate((keep_ref, got_ref)):
            at = slice(512 * half, 512 * half + 512)
            product = dot(turned, x_ref[...])
            early, late = outs[SIDE * half + k], outs[SIDE * half + 2 + k]

            @pl.when(g == 0)
            def _():
                total = product + below_add[k, :, at].astype(F32) + above_plain[k, :, at].astype(F32)
                early[...] = total.astype(early.dtype)

            @pl.when(g == 1)
            def _():
                total = product + below_plain[k, :, at].astype(F32) + above_add[k, :, at].astype(F32)
                late[...] = total.astype(late.dtype)


def own_product(at, layer_input, keep, got, arrived):
    rows = layer_input.shape[0]
    shape = lambda dtype: jax.ShapeDtypeStruct((256, 512), dtype)
    return pl.pallas_call(
        own_kernel,
        grid_spec=pltpu.PrefetchScalarGridSpec(
            num_scalar_prefetch=1,
            grid=(2,),
            in_specs=[columns_spec(0, (0, 2)), columns_spec(0, (1, 3))]
            + [full_block(rows, 512)] * 2
            + [full_block(2, 256, WIDE)] * 4,
            out_specs=[full_block(256, 512)] * 8,
        ),
        out_shape=[shape(BF16)] * 3 + [shape(F32)] + [shape(BF16)] * 4,
        compiler_params=params(),
        cost_estimate=COST,
    )(at, layer_input, layer_input, keep, got, *arrived)


def weight_kernel(scale, at_ref, *refs):
    same, cross, out = refs[:4], refs[4:8], refs[8]
    for terms, place in ((same, at_ref[3]), (cross, 1 - at_ref[3])):
        total = terms[0][...].astype(F32)
        for term in terms[1:]:
            total = total + term[...].astype(F32)
        out[:, pl.ds(pl.multiple_of(place * 512, 512), 512)] = (total * scale).astype(BF16)


def weight_final(at, scale, terms):
    return pl.pallas_call(
        functools.partial(weight_kernel, scale),
        grid=(1,),
        out_shape=jax.ShapeDtypeStruct((256, WIDE), BF16),
        in_specs=[whole(pltpu.SMEM)] + [full_block(256, 512)] * 8,
        out_specs=full_block(256, WIDE),
        compiler_params=params(),
        cost_estimate=COST,
    )(at, *terms)


def theirs_kernel(at_ref, x_ref, w_ref, out_ref):
    out_ref[...] = dot_nt(x_ref[...], w_ref[...]).astype(BF16)


def theirs(at, x_rows, proj_weight):
    depth, tile = proj_weight.shape[0], 2048
    return pl.pallas_call(
        theirs_kernel,
        grid_spec=pltpu.PrefetchScalarGridSpec(
            num_scalar_prefetch=1,
            grid=(depth // tile,),
            in_specs=[
                full_block(256, WIDE),
                pl.BlockSpec((tile, WIDE), lambda i, s: (i, 0)),
            ],
            out_specs=pl.BlockSpec((256, tile), lambda i, s: (0, i)),
        ),
        out_shape=jax.ShapeDtypeStruct((256, depth), BF16),
        compiler_params=params(),
        cost_estimate=COST,
    )(at, x_rows, proj_weight)


def mine_kernel(at_ref, x_ref, w_ref, add_ref, up_out, down_out, up_keep, down_keep, own_out, total):
    x = at_ref[2]
    total[...] = (dot_nt(x_ref[...], w_ref[...]) + add_ref[...].astype(F32)).reshape(SIDE, 64, -1)
    far, above, below = turn(x, 2), turn(x, 1), turn(x, -1)
    up_out[0:32] = total[far, 0:32].astype(BF16)
    up_out[32:64] = total[above, 32:64].astype(BF16)
    up_keep[...] = total[above, 0:32].astype(BF16)
    down_out[0:32] = total[far, 32:64].astype(BF16)
    down_out[32:64] = total[below, 0:32].astype(BF16)
    down_keep[...] = total[below, 32:64].astype(BF16)
    own_out[...] = total[x]


def mine(at, x_rows, proj_weight, add):
    depth, tile = proj_weight.shape[0], 2048
    out = lambda n: pl.BlockSpec((n, tile), lambda i, s: (0, i))
    shape = lambda n, dtype: jax.ShapeDtypeStruct((n, depth), dtype)
    return pl.pallas_call(
        mine_kernel,
        grid_spec=pltpu.PrefetchScalarGridSpec(
            num_scalar_prefetch=1,
            grid=(depth // tile,),
            in_specs=[
                full_block(256, WIDE),
                pl.BlockSpec((tile, WIDE), lambda i, s: (i, 0)),
                pl.BlockSpec((256, tile), lambda i, s: (0, i)),
            ],
            out_specs=[out(64), out(64), out(32), out(32), out(64)],
            scratch_shapes=[pltpu.VMEM((SIDE, 64, tile), F32)],
        ),
        out_shape=[shape(64, BF16), shape(64, BF16), shape(32, BF16), shape(32, BF16), shape(64, F32)],
        compiler_params=params(),
        cost_estimate=COST,
    )(at, x_rows, proj_weight, add)


def add_kernel(up_keep, down_keep, from_below, from_above, up_out, down_out):
    n = up_keep.shape[0]
    up_out[...] = (up_keep[...].astype(F32) + from_below[0:n].astype(F32)).astype(BF16)
    down_out[...] = (down_keep[...].astype(F32) + from_above[0:n].astype(F32)).astype(BF16)


def add_two(up_keep, down_keep, from_below, from_above):
    n, depth = up_keep.shape
    return pl.pallas_call(
        add_kernel,
        grid=(1,),
        out_shape=[jax.ShapeDtypeStruct((n, depth), BF16)] * 2,
        in_specs=[full_block(n, depth)] * 4,
        out_specs=[full_block(n, depth)] * 2,
        compiler_params=params(),
        cost_estimate=COST,
    )(up_keep, down_keep, from_below, from_above)


def input_kernel(own, below, above, below_add, above_add, out):
    top = own[0:32] + below_add[...].astype(F32) + above[32:64].astype(F32)
    bottom = own[32:64] + below[32:64].astype(F32) + above_add[...].astype(F32)
    out[0:32] = top.astype(BF16)
    out[32:64] = bottom.astype(BF16)


def input_final(own, below, above, below_add, above_add):
    rows, depth = own.shape
    full, part = full_block(rows, depth), full_block(rows // 2, depth)
    return pl.pallas_call(
        input_kernel,
        grid=(1,),
        out_shape=jax.ShapeDtypeStruct((rows, depth), BF16),
        in_specs=[full, full, full, part, part],
        out_specs=full,
        compiler_params=params(),
        cost_estimate=COST,
    )(own, below, above, below_add, above_add)


def after(value, *earlier):
    return lax.optimization_barrier((value, earlier))[0]


def body(
    layer_input,
    proj_weight,
    step_size,
    decay_log,
    skip_gain,
    write_vec,
    read_vec,
    out_grad,
    start_state,
    fork_grad,
):
    length = layer_input.shape[0]
    position = lax.axis_index("ctx")
    z, y = position // SIDE, position % SIDE
    column = lax.axis_index("smp")
    x, core = column // 2, column % 2
    at = jnp.stack([z, y, x, core])
    writes = write_vec[:, 0]
    reads = read_vec[:, 0]
    rel, relt, steps, scaled, states, *messages = pre(
        at, decay_log, step_size.T, out_grad, reads, fork_grad.reshape(2, WIDE, 128)
    )
    far, above, below = (hop(messages[d], 0, d) for d in (2, 1, 3))
    inputs_a = project(after(layer_input, *messages), proj_weight, 0)
    first = after([messages[0], above, far, below], inputs_a)
    message = group(at, first)
    far, above, below = (hop(message, d, 0) for d in (2, 1, 3))
    base = diag(skip_gain, rel, relt, steps, reads, writes, after(out_grad, message))
    second = after([message, above, far, below], base)
    sent = carry_over(at, first, second)
    far, above, below = (hop(sent[d], 0, d) for d in (2, 1, 3))
    inputs_b = project(after(layer_input, sent[0]), proj_weight, 1)
    quarters = after([sent[0], above, far, below], inputs_b)
    keep, give, x_mine, x_theirs, full = x_final(at, quarters, states, rel, steps, writes, base)
    got = first_hop(give, 0, 1)
    other = theirs(at, x_theirs, proj_weight)
    far = ring_product(at, FAR, layer_input, keep, after(got, other))
    far_in = first_hop(far[0], 1, 0), first_hop(far[1], -1, 0)
    other_in = hop_smp(other, 0, 1)
    plain = ring_product(at, PLAIN, layer_input, after(keep, *far), got)
    plain_in = first_hop(plain[0], 1, 0), first_hop(plain[1], -1, 0)
    up, down, up_keep, down_keep, own = mine(at, after(x_mine, *plain), proj_weight, other_in)
    added = ring_product(at, ADDED, layer_input, keep, got, after(far_in, own))
    added_in = first_hop(added[0], 1, 0), first_hop(added[1], -1, 0)
    below_x, above_x = hop_smp(up, 1, 0), hop_smp(down, -1, 0)
    write_grad, read_grad = vectors(
        rel, relt, steps, reads, writes, out_grad, scaled, inputs_a, inputs_b, after(full, *added),
        start_state.reshape(WIDE, 128),
    )
    up, down = add_two(up_keep, down_keep, below_x, after(above_x, write_grad))
    below_add, above_add = hop_smp(up, 1, 0), hop_smp(down, -1, 0)
    arrived = after((added_in[0], plain_in[0], plain_in[1], added_in[1]), up)
    sums = own_product(at, layer_input, keep, got, arrived)
    same, cross = list(sums[:4]), list(sums[4:])
    for g in range(3):
        same[g] = second_hop(same[g], ORDER[g], 0)
        cross[g] = second_hop(cross[g], ORDER[g], 1)
    cross[3] = second_hop(cross[3], 0, 1)
    input_grad = input_final(after(own, *sums), below_x, above_x, below_add, above_add)
    scale = (length * lax.axis_size("ctx")) ** (-0.5)
    weight_grad = weight_final(at, scale, same + cross)
    return (input_grad, weight_grad, write_grad[:, None], read_grad[:, None])


def solution(mesh):
    placed = (
        P("ctx", None),
        P(None, "smp"),
        P("ctx", "smp"),
        P("smp"),
        P("smp"),
        P("ctx", "smp", None),
        P("ctx", "smp", None),
        P("ctx", "smp"),
        P("ctx", "smp", None, None),
        P("ctx", "smp", None, None),
    )
    return jax.shard_map(
        body,
        mesh=mesh,
        in_specs=placed,
        out_specs=(
            P(("ctx", "smp"), None),
            P("ctx", "smp"),
            P("ctx", "smp", None),
            P("ctx", "smp", None),
        ),
        check_vma=False,
    )
```

```python
import functools

import jax
import jax.numpy as jnp
from jax import lax
from jax.experimental import pallas as pl
from jax.experimental.pallas import tpu as pltpu
from jax.sharding import PartitionSpec as P

SIDE = 4
CHUNK = 128
CHUNKS = 4
HEADS = 16
WIDE = 1024
QUARTER = WIDE // SIDE
TAIL = 16
F32 = jnp.float32
BF16 = jnp.bfloat16
ORDER = (2, 1, 3, 0)
VMEM_LIMIT = 64 * 1024 * 1024
ROOMY_LIMIT = 61 * 1024 * 1024
SMALL_LIMIT = 8 * 1024 * 1024


def params(limit=VMEM_LIMIT):
    return pltpu.CompilerParams(vmem_limit_bytes=limit)


COST = pl.CostEstimate(flops=1, bytes_accessed=1, transcendentals=0)


def whole(space=pltpu.VMEM):
    return pl.BlockSpec(memory_space=space)


def full_block(*shape):
    return pl.BlockSpec(shape, lambda *_: (0,) * len(shape))


def routed(block, move):
    route = []
    for i in range(SIDE**3 * 2):
        z, y, x, core = i // 32, i // 8 % 4, i // 2 % 4, i % 2
        z, y, x, core = move(z, y, x, core)
        route.append((i, ((z % SIDE * SIDE + y % SIDE) * SIDE + x % SIDE) * 2 + core % 2))
    return lax.ppermute(block, ("ctx", "smp"), route)


def hop(block, dz, dy):
    return routed(block, lambda z, y, x, core: (z + dz, y + dy, x, core))


def hop_smp(block, dx, dc):
    return routed(block, lambda z, y, x, core: (z, y, x + dx, core + dc))


def x_hop(block, d):
    return routed(block, lambda z, y, x, core: (z, y, x + (d if core == 0 else -d), core))


def first_hop(block, d, to_other):
    def move(z, y, x, core):
        core = core ^ to_other
        return (z, y + d, x, core) if core == 0 else (z + d, y, x, core)

    return routed(block, move)


def second_hop(block, d, to_other):
    def move(z, y, x, core):
        return (z + d, y, x, core ^ to_other) if core == 0 else (z, y + d, x, core ^ to_other)

    return routed(block, move)


def dot(a, b):
    return lax.dot_general(a, b, (((1,), (0,)), ((), ())), preferred_element_type=F32)


def dot_nt(a, b):
    return lax.dot_general(a, b, (((1,), (1,)), ((), ())), preferred_element_type=F32)


def dot_tn(a, b):
    return lax.dot_general(a, b, (((0,), (0,)), ((), ())), preferred_element_type=F32)


def halves(v):
    high = v.astype(BF16)
    return high, (v - high.astype(F32)).astype(BF16)


def spread_matrix():
    lane = lax.broadcasted_iota(jnp.int32, (HEADS, WIDE), 1)
    head = lax.broadcasted_iota(jnp.int32, (HEADS, WIDE), 0)
    return ((lane >= head * 64) & (lane < head * 64 + 64)).astype(F32).astype(BF16)


def spread(v, matrix):
    high, low = halves(v)
    return dot(high, matrix) + dot(low, matrix)


def spread_row(v, matrix):
    return spread(jnp.broadcast_to(v, (8, HEADS)), matrix)[0:1]


def tail_rows(row):
    high, low = halves(row)
    at = lax.broadcasted_iota(jnp.int32, (TAIL, row.shape[1]), 0)
    wide = jnp.where(at == 0, high.astype(F32), jnp.where(at == 1, low.astype(F32), 0.0))
    return wide.astype(BF16)


def tail_value(rows):
    rows = rows.astype(F32)
    return rows[0:1] + rows[1:2]


def turn(a, b):
    return lax.rem(a + b + 2 * SIDE, SIDE)


def pieces(v):
    high = v.astype(BF16)
    middle, low = halves(v - high.astype(F32))
    return high, middle, low


def pre_kernel(
    dlog_ref, stept_ref, grad_ref, read_ref, fork_ref,
    rel_ref, relt_ref, step_ref, scaled_ref, state_ref, m0, m1, m2, m3, message,
):
    y = lax.rem(lax.axis_index("ctx"), SIDE)
    row = lax.broadcasted_iota(jnp.int32, (CHUNK, CHUNK), 0)
    col = lax.broadcasted_iota(jnp.int32, (CHUNK, CHUNK), 1)
    lower = jnp.where(row >= col, 1.0, 0.0).astype(BF16)
    upper = jnp.where(row <= col, 1.0, 0.0).astype(BF16)
    same = jnp.where(row == col, 1.0, 0.0).astype(BF16)
    matrix = spread_matrix()
    head = lax.broadcasted_iota(jnp.int32, (HEADS, CHUNK), 0)
    decay_log = jnp.zeros((HEADS, CHUNK), F32)
    for h in range(HEADS):
        decay_log = jnp.where(head == h, dlog_ref[h], decay_log)
    decay_rate = -jnp.exp(decay_log)
    totals = []
    for c in range(CHUNKS):
        here = slice(c * CHUNK, (c + 1) * CHUNK)
        steps = stept_ref[:, here]
        rates = pieces(steps * decay_rate)
        rel = dot_nt(lower, rates[0]) + dot_nt(lower, rates[1]) + dot_nt(lower, rates[2])
        rel_ref[c] = rel
        relt_ref[c] = dot(rates[0], upper) + dot(rates[1], upper) + dot(rates[2], upper)
        cut = pieces(steps)
        step_ref[here] = dot_nt(same, cut[0]) + dot_nt(same, cut[1]) + dot_nt(same, cut[2])
        totals.append(rel[CHUNK - 1 : CHUNK])
        scaled_ref[here] = (spread(jnp.exp(rel), matrix) * grad_ref[here].astype(F32)).astype(BF16)
    state = None
    for c in reversed(range(CHUNKS)):
        here = slice(c * CHUNK, (c + 1) * CHUNK)
        local = dot_tn(read_ref[here], scaled_ref[here])
        if state is None:
            state = local
        else:
            state = local + spread_row(jnp.exp(totals[c]), matrix) * state
        if c > 0:
            state_ref[c - 1] = state.astype(BF16)
    message[0:128] = state.astype(BF16)
    message[128:256] = (fork_ref[0] + fork_ref[1]).T.astype(BF16)
    decay = spread_row(jnp.exp(totals[0] + totals[1] + totals[2] + totals[3]), matrix)
    message[256 : 256 + TAIL] = tail_rows(decay)
    for d, out in enumerate((m0, m1, m2, m3)):
        start = pl.multiple_of(turn(y, d) * QUARTER, QUARTER)
        out[...] = message[:, pl.ds(start, QUARTER)]


def pre(decay_log, stept, out_grad, reads, fork_grad):
    length = CHUNKS * CHUNK
    sent = jax.ShapeDtypeStruct((256 + TAIL, QUARTER), BF16)
    return pl.pallas_call(
        pre_kernel,
        grid=(1,),
        out_shape=[
            jax.ShapeDtypeStruct((CHUNKS, CHUNK, HEADS), F32),
            jax.ShapeDtypeStruct((CHUNKS, HEADS, CHUNK), F32),
            jax.ShapeDtypeStruct((length, HEADS), F32),
            jax.ShapeDtypeStruct((length, WIDE), BF16),
            jax.ShapeDtypeStruct((CHUNKS - 1, 128, WIDE), BF16),
        ]
        + [sent] * 4,
        in_specs=[
            whole(pltpu.SMEM),
            full_block(HEADS, length),
            full_block(length, WIDE),
            full_block(length, 128),
            full_block(2, WIDE, 128),
        ],
        out_specs=[
            full_block(CHUNKS, CHUNK, HEADS),
            full_block(CHUNKS, HEADS, CHUNK),
            full_block(length, HEADS),
            full_block(length, WIDE),
            full_block(CHUNKS - 1, 128, WIDE),
        ]
        + [full_block(256 + TAIL, QUARTER)] * 4,
        scratch_shapes=[pltpu.VMEM((256 + TAIL, WIDE), BF16)],
        compiler_params=params(),
        cost_estimate=COST,
    )(decay_log, stept, out_grad, reads, fork_grad)


def group_kernel(at_ref, a0, a1, a2, a3, out_ref, stack):
    y = at_ref[1]
    for d, ref in enumerate((a0, a1, a2, a3)):
        stack[d] = ref[...]
    total = rate = fork = None
    for b in reversed(range(SIDE)):
        at = turn(y, -b)
        local = stack[at, 0:128].astype(F32)
        decay = tail_value(stack[at, 256 : 256 + TAIL])
        share = stack[at, 128:256].astype(F32)
        if total is None:
            total, rate, fork = local, decay, share
        else:
            total, rate, fork = local + decay * total, rate * decay, fork + share
    out_ref[0:128] = total.astype(BF16)
    out_ref[128:256] = fork.astype(BF16)
    out_ref[256 : 256 + TAIL] = tail_rows(rate)


def group(at, arrived):
    return pl.pallas_call(
        group_kernel,
        out_shape=jax.ShapeDtypeStruct((256 + TAIL, QUARTER), BF16),
        in_specs=[whole(pltpu.SMEM)] + [whole()] * 4,
        out_specs=whole(),
        scratch_shapes=[pltpu.VMEM((SIDE, 256 + TAIL, QUARTER), BF16)],
        compiler_params=params(SMALL_LIMIT),
        cost_estimate=COST,
    )(at, *arrived)


def carry_kernel(at_ref, a0, a1, a2, a3, b0, b1, b2, b3, c0, c1, c2, c3, first, second, out):
    z, y = at_ref[0], at_ref[1]
    for d, ref in enumerate((a0, a1, a2, a3)):
        first[d] = ref[...]
    for d, ref in enumerate((b0, b1, b2, b3)):
        second[d] = ref[...]
    carry = jnp.zeros((128, QUARTER), F32)
    for d in range(SIDE):
        carry = carry + second[d, 128:256].astype(F32)
    mine = carry
    for b in (3, 2, 1):
        at = turn(z, -b)
        decay = tail_value(second[at, 256 : 256 + TAIL])
        carry = second[at, 0:128].astype(F32) + decay * carry
        mine = jnp.where(z == b - 1, carry, mine)
    out[SIDE - 1] = mine.astype(BF16)
    for b in (3, 2, 1):
        at = turn(y, -b)
        decay = tail_value(first[at, 256 : 256 + TAIL])
        mine = first[at, 0:128].astype(F32) + decay * mine
        out[b - 1] = mine.astype(BF16)
    for d, ref in enumerate((c0, c1, c2, c3)):
        ref[...] = out[turn(y, d)]


def carry_over(at, first, second):
    return pl.pallas_call(
        carry_kernel,
        out_shape=[jax.ShapeDtypeStruct((128, QUARTER), BF16)] * 4,
        in_specs=[whole(pltpu.SMEM)] + [whole()] * 8,
        out_specs=[whole()] * 4,
        scratch_shapes=[
            pltpu.VMEM((SIDE, 256 + TAIL, QUARTER), BF16),
            pltpu.VMEM((SIDE, 256 + TAIL, QUARTER), BF16),
            pltpu.VMEM((SIDE, 128, QUARTER), BF16),
        ],
        compiler_params=params(SMALL_LIMIT),
        cost_estimate=COST,
    )(at, *first, *second)


def diag_kernel(skip_ref, rel_ref, relt_ref, step_ref, read_ref, write_ref, grad_ref, out_ref):
    matrix = spread_matrix()
    row = lax.broadcasted_iota(jnp.int32, (CHUNK, CHUNK), 0)
    col = lax.broadcasted_iota(jnp.int32, (CHUNK, CHUNK), 1)
    for c in range(2):
        here = slice(c * CHUNK, (c + 1) * CHUNK)
        scores = jnp.where(col >= row, dot_nt(write_ref[here], read_ref[here]), 0.0)
        rel, relt = rel_ref[c], relt_ref[c]
        steps = spread(step_ref[here], matrix)
        for pair in range(HEADS // 2):
            at = slice(pair * 128, pair * 128 + 128)
            grads = grad_ref[here, at]
            both = []
            for h in (2 * pair, 2 * pair + 1):
                kernel = jnp.exp(jnp.minimum(relt[h : h + 1] - rel[:, h : h + 1], 0.0))
                both.append(dot((scores * kernel).astype(BF16), grads))
            part = steps[:, at] * jnp.where(col < 64, both[0], both[1])
            skip = jnp.where(col < 64, skip_ref[2 * pair], skip_ref[2 * pair + 1])
            out_ref[here, at] = (part + skip * grads.astype(F32)).astype(BF16)


def diag(skip_gain, rel, relt, step_size, reads, writes, out_grad):
    by_two = lambda c: (c, 0)
    rows = 2 * CHUNK
    return pl.pallas_call(
        diag_kernel,
        grid=(CHUNKS // 2,),
        out_shape=jax.ShapeDtypeStruct((CHUNKS * CHUNK, WIDE), BF16),
        in_specs=[
            whole(pltpu.SMEM),
            pl.BlockSpec((2, CHUNK, HEADS), lambda c: (c, 0, 0)),
            pl.BlockSpec((2, HEADS, CHUNK), lambda c: (c, 0, 0)),
            pl.BlockSpec((rows, HEADS), by_two),
            pl.BlockSpec((rows, 128), by_two),
            pl.BlockSpec((rows, 128), by_two),
            pl.BlockSpec((rows, WIDE), by_two),
        ],
        out_specs=pl.BlockSpec((rows, WIDE), by_two),
        compiler_params=params(ROOMY_LIMIT),
        cost_estimate=COST,
    )(skip_gain, rel, relt, step_size, reads, writes, out_grad)


def x_kernel(
    at_ref, q0, q1, q2, q3, state_ref, rel_ref, step_ref, write_ref, base_ref,
    keep_ref, give_ref, mine_ref, full_ref, carried, x_ref,
):
    y, core = at_ref[1], at_ref[3]
    matrix = spread_matrix()
    for d, ref in enumerate((q0, q1, q2, q3)):
        start = pl.multiple_of(turn(y, -d) * QUARTER, QUARTER)
        carried[:, pl.ds(start, QUARTER)] = ref[...]
    later = jnp.zeros((1, HEADS), F32)
    for c in reversed(range(CHUNKS)):
        here = slice(c * CHUNK, (c + 1) * CHUNK)
        rel = rel_ref[c]
        last = rel[CHUNK - 1 : CHUNK]
        if c == CHUNKS - 1:
            full = carried[...]
        else:
            share = spread_row(jnp.exp(later), matrix) * carried[...].astype(F32)
            full = (state_ref[c].astype(F32) + share).astype(BF16)
        full_ref[c] = full
        weights = spread(step_ref[here] * jnp.exp(last - rel), matrix)
        x = (base_ref[here].astype(F32) + weights * dot(write_ref[here], full)).astype(BF16)
        for k in range(2):
            x_ref[c, k] = x[k * 64 : k * 64 + 64]
        later = later + last
    start = pl.multiple_of(core * 512, 512)
    other = pl.multiple_of((1 - core) * 512, 512)
    for c in range(CHUNKS):
        for k in range(2):
            here = slice(c * CHUNK + k * 64, c * CHUNK + k * 64 + 64)
            keep_ref[here] = x_ref[c, k, :, pl.ds(start, 512)]
            give_ref[here] = x_ref[c, k, :, pl.ds(other, 512)]
        there = slice(c * 64, c * 64 + 64)
        mine_ref[there] = x_ref[c, core]
        for k in range(2):
            there = slice(512 + k * 256 + c * 64, 512 + k * 256 + c * 64 + 64)
            give_ref[there] = x_ref[c, 1 - core, :, k * 512 : k * 512 + 512]


def x_final(at, quarters, states, rel, step_size, writes, base):
    rows = CHUNKS * CHUNK
    shapes = (rows, 512), (2 * rows, 512), (rows // 2, WIDE)
    return pl.pallas_call(
        x_kernel,
        grid=(1,),
        in_specs=[whole(pltpu.SMEM)]
        + [full_block(128, QUARTER)] * 4
        + [
            full_block(CHUNKS - 1, 128, WIDE),
            full_block(CHUNKS, CHUNK, HEADS),
            full_block(rows, HEADS),
            full_block(rows, 128),
            full_block(rows, WIDE),
        ],
        out_specs=[full_block(*shape) for shape in shapes] + [full_block(CHUNKS, 128, WIDE)],
        scratch_shapes=[pltpu.VMEM((128, WIDE), BF16), pltpu.VMEM((CHUNKS, 2, 64, WIDE), BF16)],
        out_shape=[jax.ShapeDtypeStruct(shape, BF16) for shape in shapes]
        + [jax.ShapeDtypeStruct((CHUNKS, 128, WIDE), BF16)],
        compiler_params=params(ROOMY_LIMIT),
        cost_estimate=COST,
    )(at, *quarters, states, rel, step_size, writes, base)


def vector_kernel(
    rel_ref, relt_ref, step_ref, read_ref, write_ref, grad_ref, scaled_ref, first_ref, second_ref,
    full_ref, start_ref, wgrad_ref, rgrad_ref, state,
):
    matrix = spread_matrix()

    @pl.when(pl.program_id(0) == 0)
    def _():
        state[...] = start_ref[...].T

    row = lax.broadcasted_iota(jnp.int32, (CHUNK, CHUNK), 0)
    col = lax.broadcasted_iota(jnp.int32, (CHUNK, CHUNK), 1)
    later = jnp.where(col >= 64, 1.0, 0.0).astype(BF16)
    for c in range(2):
        here = slice(c * CHUNK, (c + 1) * CHUNK)
        rel, relt, step = rel_ref[c], relt_ref[c], step_ref[here]
        last = rel[CHUNK - 1 : CHUNK]
        steps = spread(step, matrix)
        weights = spread(step * jnp.exp(last - rel), matrix)
        weighted, coupling = [], None
        for half, inputs_ref in enumerate((first_ref, second_ref)):
            inputs = inputs_ref[here].astype(F32)
            wide = slice(half * 512, half * 512 + 512)
            weighted.append((weights[:, wide] * inputs).astype(BF16))
            stepped = (steps[:, wide] * inputs).astype(BF16)
            for pair in range(HEADS // 4):
                at = slice(pair * 128, pair * 128 + 128)
                grads = grad_ref[here, half * 512 + pair * 128 : half * 512 + pair * 128 + 128].T
                for k in range(2):
                    h = half * HEADS // 2 + 2 * pair + k
                    own = stepped[:, at] * (later if k == 1 else 1 - later)
                    kernel = jnp.exp(jnp.minimum(relt[h : h + 1] - rel[:, h : h + 1], 0.0))
                    term = kernel * dot(own, grads)
                    coupling = term if coupling is None else coupling + term
        coupling = jnp.where(col >= row, coupling, 0.0).astype(BF16)
        full, scaled = full_ref[c], scaled_ref[here]
        wgrad = dot(coupling, read_ref[here])
        new_state = []
        for half in range(2):
            wide = slice(half * 512, half * 512 + 512)
            wgrad = wgrad + dot_nt(weighted[half], full[:, wide])
            new_state.append(dot_tn(write_ref[here], weighted[half]))
        wgrad_ref[here] = wgrad
        rgrad_ref[here] = dot_nt(scaled, state[...].astype(BF16)) + dot_tn(coupling, write_ref[here])
        decay = spread_row(jnp.exp(last), matrix)
        for half in range(2):
            wide = slice(half * 512, half * 512 + 512)
            state[:, wide] = decay[:, wide] * state[:, wide] + new_state[half]


def vectors(rel, relt, step_size, reads, writes, out_grad, scaled, first, second, full, start_state):
    by_two = lambda c: (c, 0)
    by_first = lambda c: (c, 0, 0)
    rows = 2 * CHUNK
    return pl.pallas_call(
        vector_kernel,
        grid=(CHUNKS // 2,),
        out_shape=[jax.ShapeDtypeStruct((CHUNKS * CHUNK, 128), F32)] * 2,
        in_specs=[
            pl.BlockSpec((2, CHUNK, HEADS), by_first),
            pl.BlockSpec((2, HEADS, CHUNK), by_first),
            pl.BlockSpec((rows, HEADS), by_two),
            pl.BlockSpec((rows, 128), by_two),
            pl.BlockSpec((rows, 128), by_two),
            pl.BlockSpec((rows, WIDE), by_two),
            pl.BlockSpec((rows, WIDE), by_two),
            pl.BlockSpec((rows, WIDE // 2), by_two),
            pl.BlockSpec((rows, WIDE // 2), by_two),
            pl.BlockSpec((2, 128, WIDE), by_first),
            pl.BlockSpec((WIDE, 128), lambda c: (0, 0)),
        ],
        out_specs=[pl.BlockSpec((rows, 128), by_two)] * 2,
        scratch_shapes=[pltpu.VMEM((128, WIDE), F32)],
        compiler_params=params(),
        cost_estimate=pl.CostEstimate(flops=50000000000, bytes_accessed=1, transcendentals=0),
    )(rel, relt, step_size, reads, writes, out_grad, scaled, first, second, full, start_state)


def project_kernel(x_ref, w_ref, out_ref, total):
    step = pl.program_id(0)
    product = dot(x_ref[...], w_ref[...])

    @pl.when(step == 0)
    def _():
        total[...] = product

    @pl.when(step == 1)
    def _():
        out_ref[...] = (total[...] + product).astype(BF16)


def project(layer_input, proj_weight, part):
    rows, depth = layer_input.shape
    wide = WIDE // 2
    return pl.pallas_call(
        project_kernel,
        grid=(2,),
        out_shape=jax.ShapeDtypeStruct((rows, wide), BF16),
        in_specs=[
            pl.BlockSpec((rows, depth // 2), lambda i: (0, i)),
            pl.BlockSpec((depth // 2, wide), lambda i: (i, part)),
        ],
        out_specs=pl.BlockSpec((rows, wide), lambda i: (0, 0)),
        scratch_shapes=[pltpu.VMEM((rows, wide), F32)],
        compiler_params=params(ROOMY_LIMIT),
        cost_estimate=COST,
    )(layer_input, proj_weight)


FAR = ((2, (0, 1)), (2, (2, 3)))
PLAIN = ((1, (2, 3)), (-1, (0, 1)))
ADDED = ((1, (0, 1)), (-1, (2, 3)))


def column_block(s, d, part):
    for_y = turn(s[0], part) * SIDE + turn(s[1], d)
    for_z = turn(s[0], d) * SIDE + turn(s[1], part)
    return jnp.where(s[3] == 0, for_y, for_z)


def columns_spec(d, parts):
    def index(g, s):
        return 0, column_block(s, d, jnp.where(g == 0, ORDER[parts[0]], ORDER[parts[1]]))

    return pl.BlockSpec((CHUNKS * CHUNK, 256), index)


def ring_kernel(at_ref, up_ref, down_ref, keep_ref, got_ref, *refs):
    more, outs = refs[:-2], refs[-2:]
    for k, cols in enumerate((up_ref, down_ref)):
        turned = cols[...].T
        for half, x_ref in enumerate((keep_ref, got_ref)):
            at = slice(512 * half, 512 * half + 512)
            product = dot(turned, x_ref[...])
            if more:
                product = product + more[k][0, :, at].astype(F32)
            outs[k][0, :, at] = product.astype(BF16)


def ring_product(at, way, layer_input, keep, got, more=()):
    rows = layer_input.shape[0]
    (up_to, up_parts), (down_to, down_parts) = way
    block = pl.BlockSpec((1, 256, WIDE), lambda g, s: (g, 0, 0))
    return pl.pallas_call(
        ring_kernel,
        grid_spec=pltpu.PrefetchScalarGridSpec(
            num_scalar_prefetch=1,
            grid=(2,),
            in_specs=[columns_spec(up_to, up_parts), columns_spec(down_to, down_parts)]
            + [pl.BlockSpec((rows, 512), lambda g, s: (0, 0))] * 2
            + [block] * len(more),
            out_specs=[block] * 2,
        ),
        out_shape=[jax.ShapeDtypeStruct((2, 256, WIDE), BF16)] * 2,
        compiler_params=params(),
        cost_estimate=COST,
    )(at, layer_input, layer_input, keep, got, *more)


def own_kernel(at_ref, first_ref, second_ref, keep_ref, got_ref, below_plain, above_plain, out):
    g = pl.program_id(0)
    for k, cols in enumerate((first_ref, second_ref)):
        turned = cols[...].T
        for half, x_ref in enumerate((keep_ref, got_ref)):
            at = slice(512 * half, 512 * half + 512)
            plain = jnp.where(g == 0, above_plain[k, :, at], below_plain[k, :, at])
            out[k, :, at] = (dot(turned, x_ref[...]) + plain.astype(F32)).astype(BF16)


def own_product(at, layer_input, keep, got, below_plain, above_plain):
    rows = layer_input.shape[0]
    return pl.pallas_call(
        own_kernel,
        grid_spec=pltpu.PrefetchScalarGridSpec(
            num_scalar_prefetch=1,
            grid=(2,),
            in_specs=[columns_spec(0, (0, 2)), columns_spec(0, (1, 3))]
            + [pl.BlockSpec((rows, 512), lambda g, s: (0, 0))] * 2
            + [full_block(2, 256, WIDE)] * 2,
            out_specs=pl.BlockSpec((2, 256, WIDE), lambda g, s: (g, 0, 0)),
        ),
        out_shape=jax.ShapeDtypeStruct((4, 256, WIDE), BF16),
        compiler_params=params(),
        cost_estimate=COST,
    )(at, layer_input, layer_input, keep, got, below_plain, above_plain)


def total_kernel(own_ref, below_add, above_add, *outs):
    g = pl.program_id(0)
    for k in range(2):
        for half in range(2):
            at = slice(512 * half, 512 * half + 512)
            early, late = outs[SIDE * half + k], outs[SIDE * half + 2 + k]

            @pl.when(g == 0)
            def _():
                early[...] = (own_ref[k, :, at].astype(F32) + below_add[k, :, at].astype(F32)).astype(early.dtype)

            @pl.when(g == 1)
            def _():
                late[...] = (own_ref[k, :, at].astype(F32) + above_add[k, :, at].astype(F32)).astype(late.dtype)


def own_total(own, below_add, above_add):
    shape = lambda dtype: jax.ShapeDtypeStruct((256, 512), dtype)
    return pl.pallas_call(
        total_kernel,
        grid=(2,),
        in_specs=[pl.BlockSpec((2, 256, WIDE), lambda g: (g, 0, 0))] + [full_block(2, 256, WIDE)] * 2,
        out_specs=[full_block(256, 512)] * 8,
        out_shape=[shape(BF16)] * 3 + [shape(F32)] + [shape(BF16)] * 4,
        compiler_params=params(),
        cost_estimate=COST,
    )(own, below_add, above_add)


def weight_kernel(scale, at_ref, *refs):
    same, cross, out = refs[:4], refs[4:8], refs[8]
    for terms, place in ((same, at_ref[3]), (cross, 1 - at_ref[3])):
        total = terms[0][...].astype(F32)
        for term in terms[1:]:
            total = total + term[...].astype(F32)
        out[:, pl.ds(pl.multiple_of(place * 512, 512), 512)] = (total * scale).astype(BF16)


def weight_final(at, scale, terms):
    return pl.pallas_call(
        functools.partial(weight_kernel, scale),
        grid=(1,),
        out_shape=jax.ShapeDtypeStruct((256, WIDE), BF16),
        in_specs=[whole(pltpu.SMEM)] + [full_block(256, 512)] * 8,
        out_specs=full_block(256, WIDE),
        compiler_params=params(),
        cost_estimate=COST,
    )(at, *terms)


def input_kernel(x_ref, w_ref, out_ref):
    out_ref[...] = dot_nt(x_ref[...], w_ref[...]).astype(BF16)


def input_product(x_rows, proj_weight):
    depth, tile = proj_weight.shape[0], 2048
    return pl.pallas_call(
        input_kernel,
        grid=(depth // tile,),
        in_specs=[full_block(256, WIDE), pl.BlockSpec((tile, WIDE), lambda i: (i, 0))],
        out_specs=pl.BlockSpec((256, tile), lambda i: (0, i)),
        out_shape=jax.ShapeDtypeStruct((256, depth), BF16),
        compiler_params=params(),
        cost_estimate=COST,
    )(x_rows, proj_weight)


def rest_kernel(at_ref, left_ref, right_ref, w_ref, part_ref, far, next_out, last_out, own, total):
    x, core = at_ref[2], at_ref[3]
    product = dot_nt(left_ref[...], w_ref[:, :512]) + dot_nt(right_ref[...], w_ref[:, 512:])
    total[...] = (product + part_ref[...].astype(F32)).reshape(SIDE, 64, -1)
    step = 1 - 2 * core
    for d, out in ((2, far), (step, next_out), (-step, last_out), (0, own)):
        out[...] = total[turn(x, d)].astype(out.dtype)


def input_rest(at, got, other_weight, part):
    depth, tile = other_weight.shape[0], 2048
    out = pl.BlockSpec((64, tile), lambda i, s: (0, i))
    shape = lambda dtype: jax.ShapeDtypeStruct((64, depth), dtype)
    return pl.pallas_call(
        rest_kernel,
        grid_spec=pltpu.PrefetchScalarGridSpec(
            num_scalar_prefetch=1,
            grid=(depth // tile,),
            in_specs=[
                pl.BlockSpec((256, 512), lambda i, s: (2, 0)),
                pl.BlockSpec((256, 512), lambda i, s: (3, 0)),
                pl.BlockSpec((tile, WIDE), lambda i, s: (i, 0)),
                pl.BlockSpec((256, tile), lambda i, s: (0, i)),
            ],
            out_specs=[out] * 4,
            scratch_shapes=[pltpu.VMEM((SIDE, 64, tile), F32)],
        ),
        out_shape=[shape(BF16), shape(BF16), shape(BF16), shape(F32)],
        compiler_params=params(),
        cost_estimate=COST,
    )(at, got, got, other_weight, part)


def sum_kernel(own, first, second, third, out):
    total = own[...] + first[...].astype(F32) + second[...].astype(F32) + third[...].astype(F32)
    out[...] = total.astype(BF16)


def input_final(own, *arrived):
    rows, depth = own.shape
    return pl.pallas_call(
        sum_kernel,
        grid=(1,),
        out_shape=jax.ShapeDtypeStruct((rows, depth), BF16),
        in_specs=[full_block(rows, depth)] * 4,
        out_specs=full_block(rows, depth),
        compiler_params=params(),
        cost_estimate=COST,
    )(own, *arrived)


def after(value, *earlier):
    return lax.optimization_barrier((value, earlier))[0]


def body(
    layer_input,
    proj_weight,
    step_size,
    decay_log,
    skip_gain,
    write_vec,
    read_vec,
    out_grad,
    start_state,
    fork_grad,
):
    length = layer_input.shape[0]
    position = lax.axis_index("ctx")
    z, y = position // SIDE, position % SIDE
    column = lax.axis_index("smp")
    x, core = column // 2, column % 2
    writes = write_vec[:, 0]
    reads = read_vec[:, 0]
    rel, relt, steps, scaled, states, *messages = pre(
        decay_log, step_size.T, out_grad, reads, fork_grad.reshape(2, WIDE, 128)
    )
    at = jnp.stack(after([z, y, x, core], *messages))
    far, above, below = (hop(messages[d], 0, d) for d in (2, 1, 3))
    other_weight = hop_smp(proj_weight, 0, 1)
    inputs_a = project(after(layer_input, *messages), proj_weight, 0)
    first = after([messages[0], above, far, below], inputs_a)
    message = group(at, first)
    far, above, below = (hop(message, d, 0) for d in (2, 1, 3))
    inputs_b = project(after(layer_input, message), proj_weight, 1)
    second = after([message, above, far, below], inputs_b, other_weight)
    sent = carry_over(at, first, second)
    far, above, below = (hop(sent[d], 0, d) for d in (2, 1, 3))
    base = diag(skip_gain, rel, relt, steps, reads, writes, after(out_grad, sent[0]))
    quarters = [sent[0], above, far, below]
    keep, give, x_mine, full = x_final(at, quarters, states, rel, steps, writes, base)
    got = first_hop(give, 0, 1)
    part = input_product(x_mine, proj_weight)
    far = ring_product(at, FAR, layer_input, keep, after(got, part))
    far_in = first_hop(far[0], 1, 0), first_hop(far[1], -1, 0)
    plain = ring_product(at, PLAIN, layer_input, after(keep, *far), got)
    plain_in = first_hop(plain[0], 1, 0), first_hop(plain[1], -1, 0)
    sums = input_rest(at, after(got, *plain), other_weight, part)
    near_terms = x_hop(sums[1], 1), x_hop(after(sums[2], plain_in), -1)
    added = ring_product(at, ADDED, layer_input, keep, got, after(far_in, *sums))
    added_in = first_hop(added[0], 1, 0), first_hop(added[1], -1, 0)
    far_term = x_hop(after(sums[0], plain_in), 2)
    write_grad, read_grad = vectors(
        rel, relt, steps, reads, writes, out_grad, scaled, inputs_a, inputs_b, after(full, *added),
        start_state.reshape(WIDE, 128),
    )
    own = own_product(at, layer_input, keep, got, *after(plain_in, write_grad))
    totals = own_total(own, *after(added_in, own, near_terms[0]))
    same, cross = list(totals[:4]), list(totals[4:])
    for g in range(3):
        same[g] = second_hop(same[g], ORDER[g], 0)
        cross[g] = second_hop(cross[g], ORDER[g], 1)
    cross[3] = second_hop(cross[3], 0, 1)
    input_grad = input_final(after(sums[3], *totals), *near_terms, far_term)
    scale = (length * lax.axis_size("ctx")) ** (-0.5)
    weight_grad = weight_final(at, scale, same + cross)
    return (input_grad, weight_grad, write_grad[:, None], read_grad[:, None])


def solution(mesh):
    placed = (
        P("ctx", None),
        P(None, "smp"),
        P("ctx", "smp"),
        P("smp"),
        P("smp"),
        P("ctx", "smp", None),
        P("ctx", "smp", None),
        P("ctx", "smp"),
        P("ctx", "smp", None, None),
        P("ctx", "smp", None, None),
    )
    return jax.shard_map(
        body,
        mesh=mesh,
        in_specs=placed,
        out_specs=(
            P(("ctx", "smp"), None),
            P("ctx", "smp"),
            P("ctx", "smp", None),
            P("ctx", "smp", None),
        ),
        check_vma=False,
    )
```

```python
import functools

import jax
import jax.numpy as jnp
from jax import lax
from jax.experimental import pallas as pl
from jax.experimental.pallas import tpu as pltpu
from jax.sharding import PartitionSpec as P

SIDE = 4
CHUNK = 128
CHUNKS = 4
HEADS = 16
WIDE = 1024
QUARTER = WIDE // SIDE
TAIL = 16
F32 = jnp.float32
BF16 = jnp.bfloat16
ORDER = (2, 1, 3, 0)
MIB = 1024 * 1024
VMEM_LIMIT = 24 * MIB
ROOMY_LIMIT = 24 * MIB
SMALL_LIMIT = 8 * MIB


def params(limit=VMEM_LIMIT):
    return pltpu.CompilerParams(vmem_limit_bytes=limit)


COST = pl.CostEstimate(flops=1, bytes_accessed=1, transcendentals=0)


def whole(space=pltpu.VMEM):
    return pl.BlockSpec(memory_space=space)


def full_block(*shape):
    return pl.BlockSpec(shape, lambda *_: (0,) * len(shape))


def routed(block, move):
    route = []
    for i in range(SIDE**3 * 2):
        z, y, x, core = i // 32, i // 8 % 4, i // 2 % 4, i % 2
        z, y, x, core = move(z, y, x, core)
        route.append((i, ((z % SIDE * SIDE + y % SIDE) * SIDE + x % SIDE) * 2 + core % 2))
    return lax.ppermute(block, ("ctx", "smp"), route)


def hop(block, dz, dy):
    return routed(block, lambda z, y, x, core: (z + dz, y + dy, x, core))


def hop_smp(block, dx, dc):
    return routed(block, lambda z, y, x, core: (z, y, x + dx, core + dc))


def x_hop(block, d):
    return routed(block, lambda z, y, x, core: (z, y, x + (d if core == 0 else -d), core))


def first_hop(block, d, to_other):
    def move(z, y, x, core):
        core = core ^ to_other
        return (z, y + d, x, core) if core == 0 else (z + d, y, x, core)

    return routed(block, move)


def second_hop(block, d, to_other):
    def move(z, y, x, core):
        return (z + d, y, x, core ^ to_other) if core == 0 else (z, y + d, x, core ^ to_other)

    return routed(block, move)


def dot(a, b):
    return lax.dot_general(a, b, (((1,), (0,)), ((), ())), preferred_element_type=F32)


def dot_nt(a, b):
    return lax.dot_general(a, b, (((1,), (1,)), ((), ())), preferred_element_type=F32)


def dot_tn(a, b):
    return lax.dot_general(a, b, (((0,), (0,)), ((), ())), preferred_element_type=F32)


def halves(v):
    high = v.astype(BF16)
    return high, (v - high.astype(F32)).astype(BF16)


def spread_matrix():
    lane = lax.broadcasted_iota(jnp.int32, (HEADS, WIDE), 1)
    head = lax.broadcasted_iota(jnp.int32, (HEADS, WIDE), 0)
    return ((lane >= head * 64) & (lane < head * 64 + 64)).astype(F32).astype(BF16)


def spread(v, matrix):
    high, low = halves(v)
    return dot(high, matrix) + dot(low, matrix)


def spread_row(v, matrix):
    return spread(jnp.broadcast_to(v, (8, HEADS)), matrix)[0:1]


def tail_rows(row):
    high, low = halves(row)
    at = lax.broadcasted_iota(jnp.int32, (TAIL, row.shape[1]), 0)
    wide = jnp.where(at == 0, high.astype(F32), jnp.where(at == 1, low.astype(F32), 0.0))
    return wide.astype(BF16)


def tail_value(rows):
    rows = rows.astype(F32)
    return rows[0:1] + rows[1:2]


def turn(a, b):
    return lax.rem(a + b + 2 * SIDE, SIDE)


def pieces(v):
    high = v.astype(BF16)
    middle, low = halves(v - high.astype(F32))
    return high, middle, low


def pre_kernel(
    dlog_ref, stept_ref, grad_ref, read_ref, fork_ref,
    rel_ref, relt_ref, step_ref, scaled_ref, state_ref, m0, m1, m2, m3, message,
):
    y = lax.rem(lax.axis_index("ctx"), SIDE)
    row = lax.broadcasted_iota(jnp.int32, (CHUNK, CHUNK), 0)
    col = lax.broadcasted_iota(jnp.int32, (CHUNK, CHUNK), 1)
    lower = jnp.where(row >= col, 1.0, 0.0).astype(BF16)
    upper = jnp.where(row <= col, 1.0, 0.0).astype(BF16)
    same = jnp.where(row == col, 1.0, 0.0).astype(BF16)
    matrix = spread_matrix()
    head = lax.broadcasted_iota(jnp.int32, (HEADS, CHUNK), 0)
    decay_log = jnp.zeros((HEADS, CHUNK), F32)
    for h in range(HEADS):
        decay_log = jnp.where(head == h, dlog_ref[h], decay_log)
    decay_rate = -jnp.exp(decay_log)
    totals = []
    for c in range(CHUNKS):
        here = slice(c * CHUNK, (c + 1) * CHUNK)
        steps = stept_ref[:, here]
        rates = pieces(steps * decay_rate)
        rel = dot_nt(lower, rates[0]) + dot_nt(lower, rates[1]) + dot_nt(lower, rates[2])
        rel_ref[c] = rel
        relt_ref[c] = dot(rates[0], upper) + dot(rates[1], upper) + dot(rates[2], upper)
        cut = pieces(steps)
        step_ref[here] = dot_nt(same, cut[0]) + dot_nt(same, cut[1]) + dot_nt(same, cut[2])
        totals.append(rel[CHUNK - 1 : CHUNK])
        scaled_ref[here] = (spread(jnp.exp(rel), matrix) * grad_ref[here].astype(F32)).astype(BF16)
    state = None
    for c in reversed(range(CHUNKS)):
        here = slice(c * CHUNK, (c + 1) * CHUNK)
        local = dot_tn(read_ref[here], scaled_ref[here])
        if state is None:
            state = local
        else:
            state = local + spread_row(jnp.exp(totals[c]), matrix) * state
        if c > 0:
            state_ref[c - 1] = state.astype(BF16)
    message[0:128] = state.astype(BF16)
    message[128:256] = (fork_ref[0] + fork_ref[1]).T.astype(BF16)
    decay = spread_row(jnp.exp(totals[0] + totals[1] + totals[2] + totals[3]), matrix)
    message[256 : 256 + TAIL] = tail_rows(decay)
    for d, out in enumerate((m0, m1, m2, m3)):
        start = pl.multiple_of(turn(y, d) * QUARTER, QUARTER)
        out[...] = message[:, pl.ds(start, QUARTER)]


def pre(decay_log, stept, out_grad, reads, fork_grad):
    length = CHUNKS * CHUNK
    sent = jax.ShapeDtypeStruct((256 + TAIL, QUARTER), BF16)
    return pl.pallas_call(
        pre_kernel,
        grid=(1,),
        out_shape=[
            jax.ShapeDtypeStruct((CHUNKS, CHUNK, HEADS), F32),
            jax.ShapeDtypeStruct((CHUNKS, HEADS, CHUNK), F32),
            jax.ShapeDtypeStruct((length, HEADS), F32),
            jax.ShapeDtypeStruct((length, WIDE), BF16),
            jax.ShapeDtypeStruct((CHUNKS - 1, 128, WIDE), BF16),
        ]
        + [sent] * 4,
        in_specs=[
            whole(pltpu.SMEM),
            full_block(HEADS, length),
            full_block(length, WIDE),
            full_block(length, 128),
            full_block(2, WIDE, 128),
        ],
        out_specs=[
            full_block(CHUNKS, CHUNK, HEADS),
            full_block(CHUNKS, HEADS, CHUNK),
            full_block(length, HEADS),
            full_block(length, WIDE),
            full_block(CHUNKS - 1, 128, WIDE),
        ]
        + [full_block(256 + TAIL, QUARTER)] * 4,
        scratch_shapes=[pltpu.VMEM((256 + TAIL, WIDE), BF16)],
        compiler_params=params(64 * MIB),
        cost_estimate=COST,
    )(decay_log, stept, out_grad, reads, fork_grad)


def group_kernel(at_ref, a0, a1, a2, a3, out_ref, stack):
    y = at_ref[1]
    for d, ref in enumerate((a0, a1, a2, a3)):
        stack[d] = ref[...]
    total = rate = fork = None
    for b in reversed(range(SIDE)):
        at = turn(y, -b)
        local = stack[at, 0:128].astype(F32)
        decay = tail_value(stack[at, 256 : 256 + TAIL])
        share = stack[at, 128:256].astype(F32)
        if total is None:
            total, rate, fork = local, decay, share
        else:
            total, rate, fork = local + decay * total, rate * decay, fork + share
    out_ref[0:128] = total.astype(BF16)
    out_ref[128:256] = fork.astype(BF16)
    out_ref[256 : 256 + TAIL] = tail_rows(rate)


def group(at, arrived):
    return pl.pallas_call(
        group_kernel,
        out_shape=jax.ShapeDtypeStruct((256 + TAIL, QUARTER), BF16),
        in_specs=[whole(pltpu.SMEM)] + [whole()] * 4,
        out_specs=whole(),
        scratch_shapes=[pltpu.VMEM((SIDE, 256 + TAIL, QUARTER), BF16)],
        compiler_params=params(SMALL_LIMIT),
        cost_estimate=COST,
    )(at, *arrived)


def carry_kernel(at_ref, a0, a1, a2, a3, b0, b1, b2, b3, c0, c1, c2, c3, first, second, out):
    z, y = at_ref[0], at_ref[1]
    for d, ref in enumerate((a0, a1, a2, a3)):
        first[d] = ref[...]
    for d, ref in enumerate((b0, b1, b2, b3)):
        second[d] = ref[...]
    carry = jnp.zeros((128, QUARTER), F32)
    for d in range(SIDE):
        carry = carry + second[d, 128:256].astype(F32)
    mine = carry
    for b in (3, 2, 1):
        at = turn(z, -b)
        decay = tail_value(second[at, 256 : 256 + TAIL])
        carry = second[at, 0:128].astype(F32) + decay * carry
        mine = jnp.where(z == b - 1, carry, mine)
    out[SIDE - 1] = mine.astype(BF16)
    for b in (3, 2, 1):
        at = turn(y, -b)
        decay = tail_value(first[at, 256 : 256 + TAIL])
        mine = first[at, 0:128].astype(F32) + decay * mine
        out[b - 1] = mine.astype(BF16)
    for d, ref in enumerate((c0, c1, c2, c3)):
        ref[...] = out[turn(y, d)]


def carry_over(at, first, second):
    return pl.pallas_call(
        carry_kernel,
        out_shape=[jax.ShapeDtypeStruct((128, QUARTER), BF16)] * 4,
        in_specs=[whole(pltpu.SMEM)] + [whole()] * 8,
        out_specs=[whole()] * 4,
        scratch_shapes=[
            pltpu.VMEM((SIDE, 256 + TAIL, QUARTER), BF16),
            pltpu.VMEM((SIDE, 256 + TAIL, QUARTER), BF16),
            pltpu.VMEM((SIDE, 128, QUARTER), BF16),
        ],
        compiler_params=params(SMALL_LIMIT),
        cost_estimate=COST,
    )(at, *first, *second)


def diag_kernel(skip_ref, rel_ref, relt_ref, step_ref, read_ref, write_ref, grad_ref, out_ref):
    matrix = spread_matrix()
    row = lax.broadcasted_iota(jnp.int32, (CHUNK, CHUNK), 0)
    col = lax.broadcasted_iota(jnp.int32, (CHUNK, CHUNK), 1)
    for c in range(2):
        here = slice(c * CHUNK, (c + 1) * CHUNK)
        scores = jnp.where(col >= row, dot_nt(write_ref[here], read_ref[here]), 0.0)
        rel, relt = rel_ref[c], relt_ref[c]
        steps = spread(step_ref[here], matrix)
        for pair in range(HEADS // 2):
            at = slice(pair * 128, pair * 128 + 128)
            grads = grad_ref[here, at]
            both = []
            for h in (2 * pair, 2 * pair + 1):
                kernel = jnp.exp(jnp.minimum(relt[h : h + 1] - rel[:, h : h + 1], 0.0))
                both.append(dot((scores * kernel).astype(BF16), grads))
            part = steps[:, at] * jnp.where(col < 64, both[0], both[1])
            skip = jnp.where(col < 64, skip_ref[2 * pair], skip_ref[2 * pair + 1])
            out_ref[here, at] = (part + skip * grads.astype(F32)).astype(BF16)


def diag(skip_gain, rel, relt, step_size, reads, writes, out_grad):
    by_two = lambda c: (c, 0)
    rows = 2 * CHUNK
    return pl.pallas_call(
        diag_kernel,
        grid=(CHUNKS // 2,),
        out_shape=jax.ShapeDtypeStruct((CHUNKS * CHUNK, WIDE), BF16),
        in_specs=[
            whole(pltpu.SMEM),
            pl.BlockSpec((2, CHUNK, HEADS), lambda c: (c, 0, 0)),
            pl.BlockSpec((2, HEADS, CHUNK), lambda c: (c, 0, 0)),
            pl.BlockSpec((rows, HEADS), by_two),
            pl.BlockSpec((rows, 128), by_two),
            pl.BlockSpec((rows, 128), by_two),
            pl.BlockSpec((rows, WIDE), by_two),
        ],
        out_specs=pl.BlockSpec((rows, WIDE), by_two),
        compiler_params=params(ROOMY_LIMIT),
        cost_estimate=COST,
    )(skip_gain, rel, relt, step_size, reads, writes, out_grad)


def x_kernel(
    at_ref, q0, q1, q2, q3, state_ref, rel_ref, step_ref, write_ref, base_ref,
    keep_ref, give_ref, mine_ref, full_ref, carried, x_ref,
):
    y, core = at_ref[1], at_ref[3]
    matrix = spread_matrix()
    for d, ref in enumerate((q0, q1, q2, q3)):
        start = pl.multiple_of(turn(y, -d) * QUARTER, QUARTER)
        carried[:, pl.ds(start, QUARTER)] = ref[...]
    later = jnp.zeros((1, HEADS), F32)
    for c in reversed(range(CHUNKS)):
        here = slice(c * CHUNK, (c + 1) * CHUNK)
        rel = rel_ref[c]
        last = rel[CHUNK - 1 : CHUNK]
        if c == CHUNKS - 1:
            full = carried[...]
        else:
            share = spread_row(jnp.exp(later), matrix) * carried[...].astype(F32)
            full = (state_ref[c].astype(F32) + share).astype(BF16)
        full_ref[c] = full
        weights = spread(step_ref[here] * jnp.exp(last - rel), matrix)
        x = (base_ref[here].astype(F32) + weights * dot(write_ref[here], full)).astype(BF16)
        for k in range(2):
            x_ref[c, k] = x[k * 64 : k * 64 + 64]
        later = later + last
    start = pl.multiple_of(core * 512, 512)
    other = pl.multiple_of((1 - core) * 512, 512)
    for c in range(CHUNKS):
        for k in range(2):
            here = slice(c * CHUNK + k * 64, c * CHUNK + k * 64 + 64)
            keep_ref[here] = x_ref[c, k, :, pl.ds(start, 512)]
            give_ref[here] = x_ref[c, k, :, pl.ds(other, 512)]
        there = slice(c * 64, c * 64 + 64)
        mine_ref[there] = x_ref[c, core]
        for k in range(2):
            there = slice(512 + k * 256 + c * 64, 512 + k * 256 + c * 64 + 64)
            give_ref[there] = x_ref[c, 1 - core, :, k * 512 : k * 512 + 512]


def x_final(at, quarters, states, rel, step_size, writes, base):
    rows = CHUNKS * CHUNK
    shapes = (rows, 512), (2 * rows, 512), (rows // 2, WIDE)
    return pl.pallas_call(
        x_kernel,
        grid=(1,),
        in_specs=[whole(pltpu.SMEM)]
        + [full_block(128, QUARTER)] * 4
        + [
            full_block(CHUNKS - 1, 128, WIDE),
            full_block(CHUNKS, CHUNK, HEADS),
            full_block(rows, HEADS),
            full_block(rows, 128),
            full_block(rows, WIDE),
        ],
        out_specs=[full_block(*shape) for shape in shapes] + [full_block(CHUNKS, 128, WIDE)],
        scratch_shapes=[pltpu.VMEM((128, WIDE), BF16), pltpu.VMEM((CHUNKS, 2, 64, WIDE), BF16)],
        out_shape=[jax.ShapeDtypeStruct(shape, BF16) for shape in shapes]
        + [jax.ShapeDtypeStruct((CHUNKS, 128, WIDE), BF16)],
        compiler_params=params(ROOMY_LIMIT),
        cost_estimate=COST,
    )(at, *quarters, states, rel, step_size, writes, base)


def vector_kernel(
    rel_ref, relt_ref, step_ref, read_ref, write_ref, grad_ref, scaled_ref, first_ref, second_ref,
    full_ref, start_ref, wgrad_ref, rgrad_ref, state,
):
    matrix = spread_matrix()

    @pl.when(pl.program_id(0) == 0)
    def _():
        state[...] = start_ref[...].T

    row = lax.broadcasted_iota(jnp.int32, (CHUNK, CHUNK), 0)
    col = lax.broadcasted_iota(jnp.int32, (CHUNK, CHUNK), 1)
    later = jnp.where(col >= 64, 1.0, 0.0).astype(BF16)
    for c in range(2):
        here = slice(c * CHUNK, (c + 1) * CHUNK)
        rel, relt, step = rel_ref[c], relt_ref[c], step_ref[here]
        last = rel[CHUNK - 1 : CHUNK]
        steps = spread(step, matrix)
        weights = spread(step * jnp.exp(last - rel), matrix)
        weighted, coupling = [], None
        for half, inputs_ref in enumerate((first_ref, second_ref)):
            inputs = inputs_ref[here].astype(F32)
            wide = slice(half * 512, half * 512 + 512)
            weighted.append((weights[:, wide] * inputs).astype(BF16))
            stepped = (steps[:, wide] * inputs).astype(BF16)
            for pair in range(HEADS // 4):
                at = slice(pair * 128, pair * 128 + 128)
                grads = grad_ref[here, half * 512 + pair * 128 : half * 512 + pair * 128 + 128].T
                for k in range(2):
                    h = half * HEADS // 2 + 2 * pair + k
                    own = stepped[:, at] * (later if k == 1 else 1 - later)
                    kernel = jnp.exp(jnp.minimum(relt[h : h + 1] - rel[:, h : h + 1], 0.0))
                    term = kernel * dot(own, grads)
                    coupling = term if coupling is None else coupling + term
        coupling = jnp.where(col >= row, coupling, 0.0).astype(BF16)
        full, scaled = full_ref[c], scaled_ref[here]
        wgrad = dot(coupling, read_ref[here])
        new_state = []
        for half in range(2):
            wide = slice(half * 512, half * 512 + 512)
            wgrad = wgrad + dot_nt(weighted[half], full[:, wide])
            new_state.append(dot_tn(write_ref[here], weighted[half]))
        wgrad_ref[here] = wgrad
        rgrad_ref[here] = dot_nt(scaled, state[...].astype(BF16)) + dot_tn(coupling, write_ref[here])
        decay = spread_row(jnp.exp(last), matrix)
        for half in range(2):
            wide = slice(half * 512, half * 512 + 512)
            state[:, wide] = decay[:, wide] * state[:, wide] + new_state[half]


def vectors(rel, relt, step_size, reads, writes, out_grad, scaled, first, second, full, start_state):
    by_two = lambda c: (c, 0)
    by_first = lambda c: (c, 0, 0)
    rows = 2 * CHUNK
    return pl.pallas_call(
        vector_kernel,
        grid=(CHUNKS // 2,),
        out_shape=[jax.ShapeDtypeStruct((CHUNKS * CHUNK, 128), F32)] * 2,
        in_specs=[
            pl.BlockSpec((2, CHUNK, HEADS), by_first),
            pl.BlockSpec((2, HEADS, CHUNK), by_first),
            pl.BlockSpec((rows, HEADS), by_two),
            pl.BlockSpec((rows, 128), by_two),
            pl.BlockSpec((rows, 128), by_two),
            pl.BlockSpec((rows, WIDE), by_two),
            pl.BlockSpec((rows, WIDE), by_two),
            pl.BlockSpec((rows, WIDE // 2), by_two),
            pl.BlockSpec((rows, WIDE // 2), by_two),
            pl.BlockSpec((2, 128, WIDE), by_first),
            pl.BlockSpec((WIDE, 128), lambda c: (0, 0)),
        ],
        out_specs=[pl.BlockSpec((rows, 128), by_two)] * 2,
        scratch_shapes=[pltpu.VMEM((128, WIDE), F32)],
        compiler_params=params(),
        cost_estimate=pl.CostEstimate(flops=50000000000, bytes_accessed=1, transcendentals=0),
    )(rel, relt, step_size, reads, writes, out_grad, scaled, first, second, full, start_state)


def project_kernel(x_ref, w_ref, out_ref, total):
    step = pl.program_id(0)
    product = dot(x_ref[...], w_ref[...])

    @pl.when(step == 0)
    def _():
        total[...] = product

    @pl.when(step == 1)
    def _():
        out_ref[...] = (total[...] + product).astype(BF16)


def project(layer_input, proj_weight, part):
    rows, depth = layer_input.shape
    wide = WIDE // 2
    return pl.pallas_call(
        project_kernel,
        grid=(2,),
        out_shape=jax.ShapeDtypeStruct((rows, wide), BF16),
        in_specs=[
            pl.BlockSpec((rows, depth // 2), lambda i: (0, i)),
            pl.BlockSpec((depth // 2, wide), lambda i: (i, part)),
        ],
        out_specs=pl.BlockSpec((rows, wide), lambda i: (0, 0)),
        scratch_shapes=[pltpu.VMEM((rows, wide), F32)],
        compiler_params=params(61 * MIB),
        cost_estimate=COST,
    )(layer_input, proj_weight)


FAR = ((2, (0, 1)), (2, (2, 3)))
PLAIN = ((1, (2, 3)), (-1, (0, 1)))
ADDED = ((1, (0, 1)), (-1, (2, 3)))


def column_block(s, d, part):
    for_y = turn(s[0], part) * SIDE + turn(s[1], d)
    for_z = turn(s[0], d) * SIDE + turn(s[1], part)
    return jnp.where(s[3] == 0, for_y, for_z)


def columns_spec(d, parts):
    def index(g, s):
        return 0, column_block(s, d, jnp.where(g == 0, ORDER[parts[0]], ORDER[parts[1]]))

    return pl.BlockSpec((CHUNKS * CHUNK, 256), index)


def ring_kernel(at_ref, up_ref, down_ref, keep_ref, got_ref, *refs):
    more, outs = refs[:-2], refs[-2:]
    for k, cols in enumerate((up_ref, down_ref)):
        turned = cols[...].T
        for half, x_ref in enumerate((keep_ref, got_ref)):
            at = slice(512 * half, 512 * half + 512)
            product = dot(turned, x_ref[...])
            if more:
                product = product + more[k][0, :, at].astype(F32)
            outs[k][0, :, at] = product.astype(BF16)


def ring_product(at, way, layer_input, keep, got, more=()):
    rows = layer_input.shape[0]
    (up_to, up_parts), (down_to, down_parts) = way
    block = pl.BlockSpec((1, 256, WIDE), lambda g, s: (g, 0, 0))
    return pl.pallas_call(
        ring_kernel,
        grid_spec=pltpu.PrefetchScalarGridSpec(
            num_scalar_prefetch=1,
            grid=(2,),
            in_specs=[columns_spec(up_to, up_parts), columns_spec(down_to, down_parts)]
            + [pl.BlockSpec((rows, 512), lambda g, s: (0, 0))] * 2
            + [block] * len(more),
            out_specs=[block] * 2,
        ),
        out_shape=[jax.ShapeDtypeStruct((2, 256, WIDE), BF16)] * 2,
        compiler_params=params(),
        cost_estimate=COST,
    )(at, layer_input, layer_input, keep, got, *more)


def plain_kernel(
    at_ref, up_ref, down_ref, first_ref, second_ref, keep_ref, got_ref, up_out, down_out, own_out
):
    outs = (up_out.at[0], down_out.at[0], own_out.at[0], own_out.at[1])
    for cols, out in zip((up_ref, down_ref, first_ref, second_ref), outs):
        turned = cols[...].T
        for half, x_ref in enumerate((keep_ref, got_ref)):
            out[:, 512 * half : 512 * half + 512] = dot(turned, x_ref[...]).astype(BF16)


def plain_product(at, layer_input, keep, got):
    rows = layer_input.shape[0]
    (up_to, up_parts), (down_to, down_parts) = PLAIN
    return pl.pallas_call(
        plain_kernel,
        grid_spec=pltpu.PrefetchScalarGridSpec(
            num_scalar_prefetch=1,
            grid=(2,),
            in_specs=[columns_spec(up_to, up_parts), columns_spec(down_to, down_parts)]
            + [columns_spec(0, (0, 2)), columns_spec(0, (1, 3))]
            + [pl.BlockSpec((rows, 512), lambda g, s: (0, 0))] * 2,
            out_specs=[pl.BlockSpec((1, 256, WIDE), lambda g, s: (g, 0, 0))] * 2
            + [pl.BlockSpec((2, 256, WIDE), lambda g, s: (g, 0, 0))],
        ),
        out_shape=[jax.ShapeDtypeStruct((2, 256, WIDE), BF16)] * 2
        + [jax.ShapeDtypeStruct((4, 256, WIDE), BF16)],
        compiler_params=params(),
        cost_estimate=COST,
    )(at, *[layer_input] * 4, keep, got)


def total_kernel(own_ref, below_add, below_plain, above_plain, above_add, *outs):
    g = pl.program_id(0)
    for k in range(2):
        for half in range(2):
            at = slice(512 * half, 512 * half + 512)
            early, late = outs[SIDE * half + k], outs[SIDE * half + 2 + k]
            own = own_ref[k, :, at].astype(F32)

            @pl.when(g == 0)
            def _():
                total = own + below_add[k, :, at].astype(F32) + above_plain[k, :, at].astype(F32)
                early[...] = total.astype(early.dtype)

            @pl.when(g == 1)
            def _():
                total = own + below_plain[k, :, at].astype(F32) + above_add[k, :, at].astype(F32)
                late[...] = total.astype(late.dtype)


def own_total(own, arrived):
    shape = lambda dtype: jax.ShapeDtypeStruct((256, 512), dtype)
    return pl.pallas_call(
        total_kernel,
        grid=(2,),
        in_specs=[pl.BlockSpec((2, 256, WIDE), lambda g: (g, 0, 0))] + [full_block(2, 256, WIDE)] * 4,
        out_specs=[full_block(256, 512)] * 8,
        out_shape=[shape(BF16)] * 3 + [shape(F32)] + [shape(BF16)] * 4,
        compiler_params=params(),
        cost_estimate=COST,
    )(own, *arrived)


def weight_kernel(scale, at_ref, *refs):
    same, cross, out = refs[:4], refs[4:8], refs[8]
    for terms, place in ((same, at_ref[3]), (cross, 1 - at_ref[3])):
        total = terms[0][...].astype(F32)
        for term in terms[1:]:
            total = total + term[...].astype(F32)
        out[:, pl.ds(pl.multiple_of(place * 512, 512), 512)] = (total * scale).astype(BF16)


def weight_final(at, scale, terms):
    return pl.pallas_call(
        functools.partial(weight_kernel, scale),
        grid=(1,),
        out_shape=jax.ShapeDtypeStruct((256, WIDE), BF16),
        in_specs=[whole(pltpu.SMEM)] + [full_block(256, 512)] * 8,
        out_specs=full_block(256, WIDE),
        compiler_params=params(),
        cost_estimate=COST,
    )(at, *terms)


def input_kernel(x_ref, w_ref, out_ref):
    out_ref[...] = dot_nt(x_ref[...], w_ref[...]).astype(BF16)


def input_product(x_rows, proj_weight):
    depth, tile = proj_weight.shape[0], 2048
    return pl.pallas_call(
        input_kernel,
        grid=(depth // tile,),
        in_specs=[full_block(256, WIDE), pl.BlockSpec((tile, WIDE), lambda i: (i, 0))],
        out_specs=pl.BlockSpec((256, tile), lambda i: (0, i)),
        out_shape=jax.ShapeDtypeStruct((256, depth), BF16),
        compiler_params=params(),
        cost_estimate=COST,
    )(x_rows, proj_weight)


def rest_kernel(at_ref, left_ref, right_ref, w_ref, part_ref, far, next_out, last_out, own, total):
    x, core = at_ref[2], at_ref[3]
    product = dot_nt(left_ref[...], w_ref[:, :512]) + dot_nt(right_ref[...], w_ref[:, 512:])
    total[...] = (product + part_ref[...].astype(F32)).reshape(SIDE, 64, -1)
    step = 1 - 2 * core
    for d, out in ((2, far), (step, next_out), (-step, last_out), (0, own)):
        out[...] = total[turn(x, d)].astype(out.dtype)


def input_rest(at, got, other_weight, part):
    depth, tile = other_weight.shape[0], 2048
    out = pl.BlockSpec((64, tile), lambda i, s: (0, i))
    shape = lambda dtype: jax.ShapeDtypeStruct((64, depth), dtype)
    return pl.pallas_call(
        rest_kernel,
        grid_spec=pltpu.PrefetchScalarGridSpec(
            num_scalar_prefetch=1,
            grid=(depth // tile,),
            in_specs=[
                pl.BlockSpec((256, 512), lambda i, s: (2, 0)),
                pl.BlockSpec((256, 512), lambda i, s: (3, 0)),
                pl.BlockSpec((tile, WIDE), lambda i, s: (i, 0)),
                pl.BlockSpec((256, tile), lambda i, s: (0, i)),
            ],
            out_specs=[out] * 4,
            scratch_shapes=[pltpu.VMEM((SIDE, 64, tile), F32)],
        ),
        out_shape=[shape(BF16), shape(BF16), shape(BF16), shape(F32)],
        compiler_params=params(),
        cost_estimate=COST,
    )(at, got, got, other_weight, part)


def sum_kernel(own, first, second, third, out):
    total = own[...] + first[...].astype(F32) + second[...].astype(F32) + third[...].astype(F32)
    out[...] = total.astype(BF16)


def input_final(own, *arrived):
    rows, depth = own.shape
    return pl.pallas_call(
        sum_kernel,
        grid=(1,),
        out_shape=jax.ShapeDtypeStruct((rows, depth), BF16),
        in_specs=[full_block(rows, depth)] * 4,
        out_specs=full_block(rows, depth),
        compiler_params=params(),
        cost_estimate=COST,
    )(own, *arrived)


def after(value, *earlier):
    return lax.optimization_barrier((value, earlier))[0]


def body(
    layer_input,
    proj_weight,
    step_size,
    decay_log,
    skip_gain,
    write_vec,
    read_vec,
    out_grad,
    start_state,
    fork_grad,
):
    length = layer_input.shape[0]
    position = lax.axis_index("ctx")
    z, y = position // SIDE, position % SIDE
    column = lax.axis_index("smp")
    x, core = column // 2, column % 2
    writes = write_vec[:, 0]
    reads = read_vec[:, 0]
    rel, relt, steps, scaled, states, *messages = pre(
        decay_log, step_size.T, out_grad, reads, fork_grad.reshape(2, WIDE, 128)
    )
    at = jnp.stack(after([z, y, x, core], *messages))
    far, above, below = (hop(messages[d], 0, d) for d in (2, 1, 3))
    other_weight = hop_smp(proj_weight, 0, 1)
    inputs_a = project(after(layer_input, *messages), proj_weight, 0)
    first = after([messages[0], above, far, below], inputs_a)
    message = group(at, first)
    far, above, below = (hop(message, d, 0) for d in (2, 1, 3))
    inputs_b = project(after(layer_input, message), proj_weight, 1)
    second = after([message, above, far, below], inputs_b, other_weight)
    sent = carry_over(at, first, second)
    far, above, below = (hop(sent[d], 0, d) for d in (2, 1, 3))
    base = diag(skip_gain, rel, relt, steps, reads, writes, after(out_grad, sent[0]))
    quarters = [sent[0], above, far, below]
    keep, give, x_mine, full = x_final(at, quarters, states, rel, steps, writes, base)
    got = first_hop(give, 0, 1)
    part = input_product(x_mine, proj_weight)
    far = ring_product(at, FAR, layer_input, keep, after(got, part))
    far_in = first_hop(far[0], 1, 0), first_hop(far[1], -1, 0)
    *plain, own = plain_product(at, layer_input, after(keep, *far), got)
    plain_in = first_hop(plain[0], 1, 0), first_hop(plain[1], -1, 0)
    sums = input_rest(at, after(got, *plain), other_weight, part)
    near_terms = x_hop(sums[1], 1), x_hop(after(sums[2], plain_in), -1)
    added = ring_product(at, ADDED, layer_input, keep, got, after(far_in, *sums))
    added_in = first_hop(added[0], 1, 0), first_hop(added[1], -1, 0)
    far_term = x_hop(after(sums[0], plain_in), 2)
    write_grad, read_grad = vectors(
        rel, relt, steps, reads, writes, out_grad, scaled, inputs_a, inputs_b, after(full, *added),
        start_state.reshape(WIDE, 128),
    )
    arrived = added_in[0], plain_in[0], plain_in[1], added_in[1]
    totals = own_total(own, after(arrived, write_grad, near_terms[0]))
    same, cross = list(totals[:4]), list(totals[4:])
    for g in range(3):
        same[g] = second_hop(same[g], ORDER[g], 0)
        cross[g] = second_hop(cross[g], ORDER[g], 1)
    cross[3] = second_hop(cross[3], 0, 1)
    input_grad = input_final(after(sums[3], *totals), *near_terms, far_term)
    scale = (length * lax.axis_size("ctx")) ** (-0.5)
    weight_grad = weight_final(at, scale, same + cross)
    return (input_grad, weight_grad, write_grad[:, None], read_grad[:, None])


def solution(mesh):
    placed = (
        P("ctx", None),
        P(None, "smp"),
        P("ctx", "smp"),
        P("smp"),
        P("smp"),
        P("ctx", "smp", None),
        P("ctx", "smp", None),
        P("ctx", "smp"),
        P("ctx", "smp", None, None),
        P("ctx", "smp", None, None),
    )
    return jax.shard_map(
        body,
        mesh=mesh,
        in_specs=placed,
        out_specs=(
            P(("ctx", "smp"), None),
            P("ctx", "smp"),
            P("ctx", "smp", None),
            P("ctx", "smp", None),
        ),
        check_vma=False,
    )
```

```python
import functools

import jax
import jax.numpy as jnp
from jax import lax
from jax.experimental import pallas as pl
from jax.experimental.pallas import tpu as pltpu
from jax.sharding import PartitionSpec as P

SIDE = 4
CHUNK = 128
CHUNKS = 4
HEADS = 16
WIDE = 1024
QUARTER = WIDE // SIDE
TAIL = 16
F32 = jnp.float32
BF16 = jnp.bfloat16
ORDER = (2, 1, 3, 0)
MIB = 1024 * 1024
VMEM_LIMIT = 24 * MIB
ROOMY_LIMIT = 24 * MIB
SMALL_LIMIT = 8 * MIB


def params(limit=VMEM_LIMIT):
    return pltpu.CompilerParams(vmem_limit_bytes=limit)


COST = pl.CostEstimate(flops=1, bytes_accessed=1, transcendentals=0)


def whole(space=pltpu.VMEM):
    return pl.BlockSpec(memory_space=space)


def full_block(*shape):
    return pl.BlockSpec(shape, lambda *_: (0,) * len(shape))


def routed(block, move):
    route = []
    for i in range(SIDE**3 * 2):
        z, y, x, core = i // 32, i // 8 % 4, i // 2 % 4, i % 2
        z, y, x, core = move(z, y, x, core)
        route.append((i, ((z % SIDE * SIDE + y % SIDE) * SIDE + x % SIDE) * 2 + core % 2))
    return lax.ppermute(block, ("ctx", "smp"), route)


def hop(block, dz, dy):
    return routed(block, lambda z, y, x, core: (z + dz, y + dy, x, core))


def hop_smp(block, dx, dc):
    return routed(block, lambda z, y, x, core: (z, y, x + dx, core + dc))


def x_hop(block, d):
    return routed(block, lambda z, y, x, core: (z, y, x + (d if core == 0 else -d), core))


def first_hop(block, d, to_other):
    def move(z, y, x, core):
        core = core ^ to_other
        return (z, y + d, x, core) if core == 0 else (z + d, y, x, core)

    return routed(block, move)


def second_hop(block, d, to_other):
    def move(z, y, x, core):
        return (z + d, y, x, core ^ to_other) if core == 0 else (z, y + d, x, core ^ to_other)

    return routed(block, move)


def dot(a, b):
    return lax.dot_general(a, b, (((1,), (0,)), ((), ())), preferred_element_type=F32)


def dot_nt(a, b):
    return lax.dot_general(a, b, (((1,), (1,)), ((), ())), preferred_element_type=F32)


def dot_tn(a, b):
    return lax.dot_general(a, b, (((0,), (0,)), ((), ())), preferred_element_type=F32)


def halves(v):
    high = v.astype(BF16)
    return high, (v - high.astype(F32)).astype(BF16)


def spread_matrix():
    lane = lax.broadcasted_iota(jnp.int32, (HEADS, WIDE), 1)
    head = lax.broadcasted_iota(jnp.int32, (HEADS, WIDE), 0)
    return ((lane >= head * 64) & (lane < head * 64 + 64)).astype(F32).astype(BF16)


def spread(v, matrix):
    high, low = halves(v)
    return dot(high, matrix) + dot(low, matrix)


def spread_row(v, matrix):
    return spread(jnp.broadcast_to(v, (8, HEADS)), matrix)[0:1]


def tail_rows(row):
    high, low = halves(row)
    at = lax.broadcasted_iota(jnp.int32, (TAIL, row.shape[1]), 0)
    wide = jnp.where(at == 0, high.astype(F32), jnp.where(at == 1, low.astype(F32), 0.0))
    return wide.astype(BF16)


def tail_value(rows):
    rows = rows.astype(F32)
    return rows[0:1] + rows[1:2]


def turn(a, b):
    return lax.rem(a + b + 2 * SIDE, SIDE)


def pieces(v):
    high = v.astype(BF16)
    middle, low = halves(v - high.astype(F32))
    return high, middle, low


def pre_kernel(
    dlog_ref, stept_ref, grad_ref, read_ref, fork_ref,
    rel_ref, relt_ref, step_ref, scaled_ref, state_ref, m0, m1, m2, m3, message,
):
    y = lax.rem(lax.axis_index("ctx"), SIDE)
    row = lax.broadcasted_iota(jnp.int32, (CHUNK, CHUNK), 0)
    col = lax.broadcasted_iota(jnp.int32, (CHUNK, CHUNK), 1)
    lower = jnp.where(row >= col, 1.0, 0.0).astype(BF16)
    upper = jnp.where(row <= col, 1.0, 0.0).astype(BF16)
    same = jnp.where(row == col, 1.0, 0.0).astype(BF16)
    matrix = spread_matrix()
    head = lax.broadcasted_iota(jnp.int32, (HEADS, CHUNK), 0)
    decay_log = jnp.zeros((HEADS, CHUNK), F32)
    for h in range(HEADS):
        decay_log = jnp.where(head == h, dlog_ref[h], decay_log)
    decay_rate = -jnp.exp(decay_log)
    totals = []
    for c in range(CHUNKS):
        here = slice(c * CHUNK, (c + 1) * CHUNK)
        steps = stept_ref[:, here]
        rates = pieces(steps * decay_rate)
        rel = dot_nt(lower, rates[0]) + dot_nt(lower, rates[1]) + dot_nt(lower, rates[2])
        rel_ref[c] = rel
        relt_ref[c] = dot(rates[0], upper) + dot(rates[1], upper) + dot(rates[2], upper)
        cut = pieces(steps)
        step_ref[here] = dot_nt(same, cut[0]) + dot_nt(same, cut[1]) + dot_nt(same, cut[2])
        totals.append(rel[CHUNK - 1 : CHUNK])
        scaled_ref[here] = (spread(jnp.exp(rel), matrix) * grad_ref[here].astype(F32)).astype(BF16)
    state = None
    for c in reversed(range(CHUNKS)):
        here = slice(c * CHUNK, (c + 1) * CHUNK)
        local = dot_tn(read_ref[here], scaled_ref[here])
        if state is None:
            state = local
        else:
            state = local + spread_row(jnp.exp(totals[c]), matrix) * state
        if c > 0:
            state_ref[c - 1] = state.astype(BF16)
    message[0:128] = state.astype(BF16)
    message[128:256] = (fork_ref[0] + fork_ref[1]).T.astype(BF16)
    decay = spread_row(jnp.exp(totals[0] + totals[1] + totals[2] + totals[3]), matrix)
    message[256 : 256 + TAIL] = tail_rows(decay)
    for d, out in enumerate((m0, m1, m2, m3)):
        start = pl.multiple_of(turn(y, d) * QUARTER, QUARTER)
        out[...] = message[:, pl.ds(start, QUARTER)]


def pre(decay_log, stept, out_grad, reads, fork_grad):
    length = CHUNKS * CHUNK
    sent = jax.ShapeDtypeStruct((256 + TAIL, QUARTER), BF16)
    return pl.pallas_call(
        pre_kernel,
        grid=(1,),
        out_shape=[
            jax.ShapeDtypeStruct((CHUNKS, CHUNK, HEADS), F32),
            jax.ShapeDtypeStruct((CHUNKS, HEADS, CHUNK), F32),
            jax.ShapeDtypeStruct((length, HEADS), F32),
            jax.ShapeDtypeStruct((length, WIDE), BF16),
            jax.ShapeDtypeStruct((CHUNKS - 1, 128, WIDE), BF16),
        ]
        + [sent] * 4,
        in_specs=[
            whole(pltpu.SMEM),
            full_block(HEADS, length),
            full_block(length, WIDE),
            full_block(length, 128),
            full_block(2, WIDE, 128),
        ],
        out_specs=[
            full_block(CHUNKS, CHUNK, HEADS),
            full_block(CHUNKS, HEADS, CHUNK),
            full_block(length, HEADS),
            full_block(length, WIDE),
            full_block(CHUNKS - 1, 128, WIDE),
        ]
        + [full_block(256 + TAIL, QUARTER)] * 4,
        scratch_shapes=[pltpu.VMEM((256 + TAIL, WIDE), BF16)],
        compiler_params=params(64 * MIB),
        cost_estimate=COST,
    )(decay_log, stept, out_grad, reads, fork_grad)


def group_kernel(at_ref, a0, a1, a2, a3, out_ref, stack):
    y = at_ref[1]
    for d, ref in enumerate((a0, a1, a2, a3)):
        stack[d] = ref[...]
    total = rate = fork = None
    for b in reversed(range(SIDE)):
        at = turn(y, -b)
        local = stack[at, 0:128].astype(F32)
        decay = tail_value(stack[at, 256 : 256 + TAIL])
        share = stack[at, 128:256].astype(F32)
        if total is None:
            total, rate, fork = local, decay, share
        else:
            total, rate, fork = local + decay * total, rate * decay, fork + share
    out_ref[0:128] = total.astype(BF16)
    out_ref[128:256] = fork.astype(BF16)
    out_ref[256 : 256 + TAIL] = tail_rows(rate)


def group(at, arrived):
    return pl.pallas_call(
        group_kernel,
        out_shape=jax.ShapeDtypeStruct((256 + TAIL, QUARTER), BF16),
        in_specs=[whole(pltpu.SMEM)] + [whole()] * 4,
        out_specs=whole(),
        scratch_shapes=[pltpu.VMEM((SIDE, 256 + TAIL, QUARTER), BF16)],
        compiler_params=params(SMALL_LIMIT),
        cost_estimate=COST,
    )(at, *arrived)


def carry_kernel(at_ref, a0, a1, a2, a3, b0, b1, b2, b3, c0, c1, c2, c3, first, second, out):
    z, y = at_ref[0], at_ref[1]
    for d, ref in enumerate((a0, a1, a2, a3)):
        first[d] = ref[...]
    for d, ref in enumerate((b0, b1, b2, b3)):
        second[d] = ref[...]
    carry = jnp.zeros((128, QUARTER), F32)
    for d in range(SIDE):
        carry = carry + second[d, 128:256].astype(F32)
    mine = carry
    for b in (3, 2, 1):
        at = turn(z, -b)
        decay = tail_value(second[at, 256 : 256 + TAIL])
        carry = second[at, 0:128].astype(F32) + decay * carry
        mine = jnp.where(z == b - 1, carry, mine)
    out[SIDE - 1] = mine.astype(BF16)
    for b in (3, 2, 1):
        at = turn(y, -b)
        decay = tail_value(first[at, 256 : 256 + TAIL])
        mine = first[at, 0:128].astype(F32) + decay * mine
        out[b - 1] = mine.astype(BF16)
    for d, ref in enumerate((c0, c1, c2, c3)):
        ref[...] = out[turn(y, d)]


def carry_over(at, first, second):
    return pl.pallas_call(
        carry_kernel,
        out_shape=[jax.ShapeDtypeStruct((128, QUARTER), BF16)] * 4,
        in_specs=[whole(pltpu.SMEM)] + [whole()] * 8,
        out_specs=[whole()] * 4,
        scratch_shapes=[
            pltpu.VMEM((SIDE, 256 + TAIL, QUARTER), BF16),
            pltpu.VMEM((SIDE, 256 + TAIL, QUARTER), BF16),
            pltpu.VMEM((SIDE, 128, QUARTER), BF16),
        ],
        compiler_params=params(SMALL_LIMIT),
        cost_estimate=COST,
    )(at, *first, *second)


def diag_kernel(skip_ref, rel_ref, relt_ref, step_ref, read_ref, write_ref, grad_ref, out_ref):
    matrix = spread_matrix()
    row = lax.broadcasted_iota(jnp.int32, (CHUNK, CHUNK), 0)
    col = lax.broadcasted_iota(jnp.int32, (CHUNK, CHUNK), 1)
    for c in range(2):
        here = slice(c * CHUNK, (c + 1) * CHUNK)
        scores = jnp.where(col >= row, dot_nt(write_ref[here], read_ref[here]), 0.0)
        rel, relt = rel_ref[c], relt_ref[c]
        steps = spread(step_ref[here], matrix)
        for pair in range(HEADS // 2):
            at = slice(pair * 128, pair * 128 + 128)
            grads = grad_ref[here, at]
            both = []
            for h in (2 * pair, 2 * pair + 1):
                kernel = jnp.exp(jnp.minimum(relt[h : h + 1] - rel[:, h : h + 1], 0.0))
                both.append(dot((scores * kernel).astype(BF16), grads))
            part = steps[:, at] * jnp.where(col < 64, both[0], both[1])
            skip = jnp.where(col < 64, skip_ref[2 * pair], skip_ref[2 * pair + 1])
            out_ref[here, at] = (part + skip * grads.astype(F32)).astype(BF16)


def diag(skip_gain, rel, relt, step_size, reads, writes, out_grad):
    by_two = lambda c: (c, 0)
    rows = 2 * CHUNK
    return pl.pallas_call(
        diag_kernel,
        grid=(CHUNKS // 2,),
        out_shape=jax.ShapeDtypeStruct((CHUNKS * CHUNK, WIDE), BF16),
        in_specs=[
            whole(pltpu.SMEM),
            pl.BlockSpec((2, CHUNK, HEADS), lambda c: (c, 0, 0)),
            pl.BlockSpec((2, HEADS, CHUNK), lambda c: (c, 0, 0)),
            pl.BlockSpec((rows, HEADS), by_two),
            pl.BlockSpec((rows, 128), by_two),
            pl.BlockSpec((rows, 128), by_two),
            pl.BlockSpec((rows, WIDE), by_two),
        ],
        out_specs=pl.BlockSpec((rows, WIDE), by_two),
        compiler_params=params(ROOMY_LIMIT),
        cost_estimate=pl.CostEstimate(flops=4000000000, bytes_accessed=1, transcendentals=0),
    )(skip_gain, rel, relt, step_size, reads, writes, out_grad)


def x_kernel(
    at_ref, q0, q1, q2, q3, state_ref, rel_ref, step_ref, write_ref, base_ref,
    keep_ref, give_ref, mine_ref, full_ref, carried, x_ref,
):
    y, core = at_ref[1], at_ref[3]
    matrix = spread_matrix()
    for d, ref in enumerate((q0, q1, q2, q3)):
        start = pl.multiple_of(turn(y, -d) * QUARTER, QUARTER)
        carried[:, pl.ds(start, QUARTER)] = ref[...]
    later = jnp.zeros((1, HEADS), F32)
    for c in reversed(range(CHUNKS)):
        here = slice(c * CHUNK, (c + 1) * CHUNK)
        rel = rel_ref[c]
        last = rel[CHUNK - 1 : CHUNK]
        if c == CHUNKS - 1:
            full = carried[...]
        else:
            share = spread_row(jnp.exp(later), matrix) * carried[...].astype(F32)
            full = (state_ref[c].astype(F32) + share).astype(BF16)
        full_ref[c] = full
        weights = spread(step_ref[here] * jnp.exp(last - rel), matrix)
        x = (base_ref[here].astype(F32) + weights * dot(write_ref[here], full)).astype(BF16)
        for k in range(2):
            x_ref[c, k] = x[k * 64 : k * 64 + 64]
        later = later + last
    start = pl.multiple_of(core * 512, 512)
    other = pl.multiple_of((1 - core) * 512, 512)
    for c in range(CHUNKS):
        for k in range(2):
            here = slice(c * CHUNK + k * 64, c * CHUNK + k * 64 + 64)
            keep_ref[here] = x_ref[c, k, :, pl.ds(start, 512)]
            give_ref[here] = x_ref[c, k, :, pl.ds(other, 512)]
        there = slice(c * 64, c * 64 + 64)
        mine_ref[there] = x_ref[c, core]
        for k in range(2):
            there = slice(512 + k * 256 + c * 64, 512 + k * 256 + c * 64 + 64)
            give_ref[there] = x_ref[c, 1 - core, :, k * 512 : k * 512 + 512]


def x_final(at, quarters, states, rel, step_size, writes, base):
    rows = CHUNKS * CHUNK
    shapes = (rows, 512), (2 * rows, 512), (rows // 2, WIDE)
    return pl.pallas_call(
        x_kernel,
        grid=(1,),
        in_specs=[whole(pltpu.SMEM)]
        + [full_block(128, QUARTER)] * 4
        + [
            full_block(CHUNKS - 1, 128, WIDE),
            full_block(CHUNKS, CHUNK, HEADS),
            full_block(rows, HEADS),
            full_block(rows, 128),
            full_block(rows, WIDE),
        ],
        out_specs=[full_block(*shape) for shape in shapes] + [full_block(CHUNKS, 128, WIDE)],
        scratch_shapes=[pltpu.VMEM((128, WIDE), BF16), pltpu.VMEM((CHUNKS, 2, 64, WIDE), BF16)],
        out_shape=[jax.ShapeDtypeStruct(shape, BF16) for shape in shapes]
        + [jax.ShapeDtypeStruct((CHUNKS, 128, WIDE), BF16)],
        compiler_params=params(ROOMY_LIMIT),
        cost_estimate=COST,
    )(at, *quarters, states, rel, step_size, writes, base)


def vector_kernel(
    rel_ref, relt_ref, step_ref, read_ref, write_ref, grad_ref, scaled_ref, first_ref, second_ref,
    full_ref, start_ref, wgrad_ref, rgrad_ref, state,
):
    matrix = spread_matrix()

    @pl.when(pl.program_id(0) == 0)
    def _():
        state[...] = start_ref[...].T

    row = lax.broadcasted_iota(jnp.int32, (CHUNK, CHUNK), 0)
    col = lax.broadcasted_iota(jnp.int32, (CHUNK, CHUNK), 1)
    later = jnp.where(col >= 64, 1.0, 0.0).astype(BF16)
    for c in range(2):
        here = slice(c * CHUNK, (c + 1) * CHUNK)
        rel, relt, step = rel_ref[c], relt_ref[c], step_ref[here]
        last = rel[CHUNK - 1 : CHUNK]
        steps = spread(step, matrix)
        weights = spread(step * jnp.exp(last - rel), matrix)
        weighted, coupling = [], None
        for half, inputs_ref in enumerate((first_ref, second_ref)):
            inputs = inputs_ref[here].astype(F32)
            wide = slice(half * 512, half * 512 + 512)
            weighted.append((weights[:, wide] * inputs).astype(BF16))
            stepped = (steps[:, wide] * inputs).astype(BF16)
            for pair in range(HEADS // 4):
                at = slice(pair * 128, pair * 128 + 128)
                grads = grad_ref[here, half * 512 + pair * 128 : half * 512 + pair * 128 + 128].T
                for k in range(2):
                    h = half * HEADS // 2 + 2 * pair + k
                    own = stepped[:, at] * (later if k == 1 else 1 - later)
                    kernel = jnp.exp(jnp.minimum(relt[h : h + 1] - rel[:, h : h + 1], 0.0))
                    term = kernel * dot(own, grads)
                    coupling = term if coupling is None else coupling + term
        coupling = jnp.where(col >= row, coupling, 0.0).astype(BF16)
        full, scaled = full_ref[c], scaled_ref[here]
        wgrad = dot(coupling, read_ref[here])
        new_state = []
        for half in range(2):
            wide = slice(half * 512, half * 512 + 512)
            wgrad = wgrad + dot_nt(weighted[half], full[:, wide])
            new_state.append(dot_tn(write_ref[here], weighted[half]))
        wgrad_ref[here] = wgrad
        rgrad_ref[here] = dot_nt(scaled, state[...].astype(BF16)) + dot_tn(coupling, write_ref[here])
        decay = spread_row(jnp.exp(last), matrix)
        for half in range(2):
            wide = slice(half * 512, half * 512 + 512)
            state[:, wide] = decay[:, wide] * state[:, wide] + new_state[half]


def vectors(rel, relt, step_size, reads, writes, out_grad, scaled, first, second, full, start_state):
    by_two = lambda c: (c, 0)
    by_first = lambda c: (c, 0, 0)
    rows = 2 * CHUNK
    return pl.pallas_call(
        vector_kernel,
        grid=(CHUNKS // 2,),
        out_shape=[jax.ShapeDtypeStruct((CHUNKS * CHUNK, 128), F32)] * 2,
        in_specs=[
            pl.BlockSpec((2, CHUNK, HEADS), by_first),
            pl.BlockSpec((2, HEADS, CHUNK), by_first),
            pl.BlockSpec((rows, HEADS), by_two),
            pl.BlockSpec((rows, 128), by_two),
            pl.BlockSpec((rows, 128), by_two),
            pl.BlockSpec((rows, WIDE), by_two),
            pl.BlockSpec((rows, WIDE), by_two),
            pl.BlockSpec((rows, WIDE // 2), by_two),
            pl.BlockSpec((rows, WIDE // 2), by_two),
            pl.BlockSpec((2, 128, WIDE), by_first),
            pl.BlockSpec((WIDE, 128), lambda c: (0, 0)),
        ],
        out_specs=[pl.BlockSpec((rows, 128), by_two)] * 2,
        scratch_shapes=[pltpu.VMEM((128, WIDE), F32)],
        compiler_params=params(),
        cost_estimate=pl.CostEstimate(flops=50000000000, bytes_accessed=1, transcendentals=0),
    )(rel, relt, step_size, reads, writes, out_grad, scaled, first, second, full, start_state)


def project_kernel(x_ref, w_ref, out_ref, total):
    step = pl.program_id(0)
    product = dot(x_ref[...], w_ref[...])

    @pl.when(step == 0)
    def _():
        total[...] = product

    @pl.when(step == 1)
    def _():
        out_ref[...] = (total[...] + product).astype(BF16)


def project(layer_input, proj_weight, part):
    rows, depth = layer_input.shape
    wide = WIDE // 2
    return pl.pallas_call(
        project_kernel,
        grid=(2,),
        out_shape=jax.ShapeDtypeStruct((rows, wide), BF16),
        in_specs=[
            pl.BlockSpec((rows, depth // 2), lambda i: (0, i)),
            pl.BlockSpec((depth // 2, wide), lambda i: (i, part)),
        ],
        out_specs=pl.BlockSpec((rows, wide), lambda i: (0, 0)),
        scratch_shapes=[pltpu.VMEM((rows, wide), F32)],
        compiler_params=params(61 * MIB),
        cost_estimate=COST,
    )(layer_input, proj_weight)


FAR = ((2, (0, 1)), (2, (2, 3)))
PLAIN = ((1, (2, 3)), (-1, (0, 1)))
ADDED = ((1, (0, 1)), (-1, (2, 3)))


def column_block(s, d, part):
    for_y = turn(s[0], part) * SIDE + turn(s[1], d)
    for_z = turn(s[0], d) * SIDE + turn(s[1], part)
    return jnp.where(s[3] == 0, for_y, for_z)


def columns_spec(d, parts):
    def index(g, s):
        return 0, column_block(s, d, jnp.where(g == 0, ORDER[parts[0]], ORDER[parts[1]]))

    return pl.BlockSpec((CHUNKS * CHUNK, 256), index)


def ring_kernel(at_ref, up_ref, down_ref, keep_ref, got_ref, *refs):
    more, outs = refs[:-2], refs[-2:]
    for k, cols in enumerate((up_ref, down_ref)):
        turned = cols[...].T
        for half, x_ref in enumerate((keep_ref, got_ref)):
            at = slice(512 * half, 512 * half + 512)
            product = dot(turned, x_ref[...])
            if more:
                product = product + more[k][0, :, at].astype(F32)
            outs[k][0, :, at] = product.astype(BF16)


def ring_product(at, way, layer_input, keep, got, more=()):
    rows = layer_input.shape[0]
    (up_to, up_parts), (down_to, down_parts) = way
    block = pl.BlockSpec((1, 256, WIDE), lambda g, s: (g, 0, 0))
    return pl.pallas_call(
        ring_kernel,
        grid_spec=pltpu.PrefetchScalarGridSpec(
            num_scalar_prefetch=1,
            grid=(2,),
            in_specs=[columns_spec(up_to, up_parts), columns_spec(down_to, down_parts)]
            + [pl.BlockSpec((rows, 512), lambda g, s: (0, 0))] * 2
            + [block] * len(more),
            out_specs=[block] * 2,
        ),
        out_shape=[jax.ShapeDtypeStruct((2, 256, WIDE), BF16)] * 2,
        compiler_params=params(),
        cost_estimate=COST,
    )(at, layer_input, layer_input, keep, got, *more)


def plain_kernel(
    at_ref, up_ref, down_ref, first_ref, second_ref, keep_ref, got_ref, up_out, down_out, own_out
):
    outs = (up_out.at[0], down_out.at[0], own_out.at[0], own_out.at[1])
    for cols, out in zip((up_ref, down_ref, first_ref, second_ref), outs):
        turned = cols[...].T
        for half, x_ref in enumerate((keep_ref, got_ref)):
            out[:, 512 * half : 512 * half + 512] = dot(turned, x_ref[...]).astype(BF16)


def plain_product(at, layer_input, keep, got):
    rows = layer_input.shape[0]
    (up_to, up_parts), (down_to, down_parts) = PLAIN
    return pl.pallas_call(
        plain_kernel,
        grid_spec=pltpu.PrefetchScalarGridSpec(
            num_scalar_prefetch=1,
            grid=(2,),
            in_specs=[columns_spec(up_to, up_parts), columns_spec(down_to, down_parts)]
            + [columns_spec(0, (0, 2)), columns_spec(0, (1, 3))]
            + [pl.BlockSpec((rows, 512), lambda g, s: (0, 0))] * 2,
            out_specs=[pl.BlockSpec((1, 256, WIDE), lambda g, s: (g, 0, 0))] * 2
            + [pl.BlockSpec((2, 256, WIDE), lambda g, s: (g, 0, 0))],
        ),
        out_shape=[jax.ShapeDtypeStruct((2, 256, WIDE), BF16)] * 2
        + [jax.ShapeDtypeStruct((4, 256, WIDE), BF16)],
        compiler_params=params(),
        cost_estimate=COST,
    )(at, *[layer_input] * 4, keep, got)


def total_kernel(own_ref, below_add, below_plain, above_plain, above_add, *outs):
    g = pl.program_id(0)
    for k in range(2):
        for half in range(2):
            at = slice(512 * half, 512 * half + 512)
            early, late = outs[SIDE * half + k], outs[SIDE * half + 2 + k]
            own = own_ref[k, :, at].astype(F32)

            @pl.when(g == 0)
            def _():
                total = own + below_add[k, :, at].astype(F32) + above_plain[k, :, at].astype(F32)
                early[...] = total.astype(early.dtype)

            @pl.when(g == 1)
            def _():
                total = own + below_plain[k, :, at].astype(F32) + above_add[k, :, at].astype(F32)
                late[...] = total.astype(late.dtype)


def own_total(own, arrived):
    shape = lambda dtype: jax.ShapeDtypeStruct((256, 512), dtype)
    return pl.pallas_call(
        total_kernel,
        grid=(2,),
        in_specs=[pl.BlockSpec((2, 256, WIDE), lambda g: (g, 0, 0))] + [full_block(2, 256, WIDE)] * 4,
        out_specs=[full_block(256, 512)] * 8,
        out_shape=[shape(BF16)] * 3 + [shape(F32)] + [shape(BF16)] * 4,
        compiler_params=params(),
        cost_estimate=COST,
    )(own, *arrived)


def weight_kernel(scale, at_ref, *refs):
    same, cross, out = refs[:4], refs[4:8], refs[8]
    for terms, place in ((same, at_ref[3]), (cross, 1 - at_ref[3])):
        total = terms[0][...].astype(F32)
        for term in terms[1:]:
            total = total + term[...].astype(F32)
        out[:, pl.ds(pl.multiple_of(place * 512, 512), 512)] = (total * scale).astype(BF16)


def weight_final(at, scale, terms):
    return pl.pallas_call(
        functools.partial(weight_kernel, scale),
        grid=(1,),
        out_shape=jax.ShapeDtypeStruct((256, WIDE), BF16),
        in_specs=[whole(pltpu.SMEM)] + [full_block(256, 512)] * 8,
        out_specs=full_block(256, WIDE),
        compiler_params=params(),
        cost_estimate=COST,
    )(at, *terms)


def input_kernel(x_ref, w_ref, out_ref):
    out_ref[...] = dot_nt(x_ref[...], w_ref[...]).astype(BF16)


def input_product(x_rows, proj_weight):
    depth, tile = proj_weight.shape[0], 2048
    return pl.pallas_call(
        input_kernel,
        grid=(depth // tile,),
        in_specs=[full_block(256, WIDE), pl.BlockSpec((tile, WIDE), lambda i: (i, 0))],
        out_specs=pl.BlockSpec((256, tile), lambda i: (0, i)),
        out_shape=jax.ShapeDtypeStruct((256, depth), BF16),
        compiler_params=params(),
        cost_estimate=COST,
    )(x_rows, proj_weight)


def rest_kernel(at_ref, left_ref, right_ref, w_ref, part_ref, far, next_out, last_out, own, total):
    x, core = at_ref[2], at_ref[3]
    product = dot_nt(left_ref[...], w_ref[:, :512]) + dot_nt(right_ref[...], w_ref[:, 512:])
    total[...] = (product + part_ref[...].astype(F32)).reshape(SIDE, 64, -1)
    step = 1 - 2 * core
    for d, out in ((2, far), (step, next_out), (-step, last_out), (0, own)):
        out[...] = total[turn(x, d)].astype(out.dtype)


def input_rest(at, got, other_weight, part):
    depth, tile = other_weight.shape[0], 2048
    out = pl.BlockSpec((64, tile), lambda i, s: (0, i))
    shape = lambda dtype: jax.ShapeDtypeStruct((64, depth), dtype)
    return pl.pallas_call(
        rest_kernel,
        grid_spec=pltpu.PrefetchScalarGridSpec(
            num_scalar_prefetch=1,
            grid=(depth // tile,),
            in_specs=[
                pl.BlockSpec((256, 512), lambda i, s: (2, 0)),
                pl.BlockSpec((256, 512), lambda i, s: (3, 0)),
                pl.BlockSpec((tile, WIDE), lambda i, s: (i, 0)),
                pl.BlockSpec((256, tile), lambda i, s: (0, i)),
            ],
            out_specs=[out] * 4,
            scratch_shapes=[pltpu.VMEM((SIDE, 64, tile), F32)],
        ),
        out_shape=[shape(BF16), shape(BF16), shape(BF16), shape(F32)],
        compiler_params=params(),
        cost_estimate=COST,
    )(at, got, got, other_weight, part)


def sum_kernel(own, first, second, third, out):
    total = own[...] + first[...].astype(F32) + second[...].astype(F32) + third[...].astype(F32)
    out[...] = total.astype(BF16)


def input_final(own, *arrived):
    rows, depth = own.shape
    return pl.pallas_call(
        sum_kernel,
        grid=(1,),
        out_shape=jax.ShapeDtypeStruct((rows, depth), BF16),
        in_specs=[full_block(rows, depth)] * 4,
        out_specs=full_block(rows, depth),
        compiler_params=params(),
        cost_estimate=COST,
    )(own, *arrived)


def after(value, *earlier):
    return lax.optimization_barrier((value, earlier))[0]


def body(
    layer_input,
    proj_weight,
    step_size,
    decay_log,
    skip_gain,
    write_vec,
    read_vec,
    out_grad,
    start_state,
    fork_grad,
):
    length = layer_input.shape[0]
    position = lax.axis_index("ctx")
    z, y = position // SIDE, position % SIDE
    column = lax.axis_index("smp")
    x, core = column // 2, column % 2
    writes = write_vec[:, 0]
    reads = read_vec[:, 0]
    rel, relt, steps, scaled, states, *messages = pre(
        decay_log, step_size.T, out_grad, reads, fork_grad.reshape(2, WIDE, 128)
    )
    at = jnp.stack(after([z, y, x, core], *messages))
    far, above, below = (hop(messages[d], 0, d) for d in (2, 1, 3))
    other_weight = hop_smp(proj_weight, 0, 1)
    inputs_a = project(after(layer_input, *messages), proj_weight, 0)
    first = after([messages[0], above, far, below], inputs_a)
    message = group(at, first)
    far, above, below = (hop(message, d, 0) for d in (2, 1, 3))
    inputs_b = project(after(layer_input, message), proj_weight, 1)
    second = after([message, above, far, below], inputs_b, other_weight)
    sent = carry_over(at, first, second)
    far, above, below = (hop(sent[d], 0, d) for d in (2, 1, 3))
    base = diag(skip_gain, rel, relt, steps, reads, writes, after(out_grad, sent[0]))
    quarters = [sent[0], above, far, below]
    keep, give, x_mine, full = x_final(at, quarters, states, rel, steps, writes, base)
    got = first_hop(give, 0, 1)
    part = input_product(x_mine, proj_weight)
    far = ring_product(at, FAR, layer_input, keep, after(got, part))
    far_in = first_hop(far[0], 1, 0), first_hop(far[1], -1, 0)
    *plain, own = plain_product(at, layer_input, after(keep, *far), got)
    plain_in = first_hop(plain[0], 1, 0), first_hop(plain[1], -1, 0)
    sums = input_rest(at, after(got, *plain), other_weight, part)
    early_term = x_hop(sums[0], 2)
    added = ring_product(at, ADDED, layer_input, keep, got, after(far_in, *sums))
    added_in = first_hop(added[0], 1, 0), first_hop(added[1], -1, 0)
    late_terms = [x_hop(after(sums[k], plain_in), 3 - 2 * k) for k in (1, 2)]
    write_grad, read_grad = vectors(
        rel, relt, steps, reads, writes, out_grad, scaled, inputs_a, inputs_b, after(full, *added),
        start_state.reshape(WIDE, 128),
    )
    arrived = added_in[0], plain_in[0], plain_in[1], added_in[1]
    totals = own_total(own, after(arrived, write_grad, early_term))
    same, cross = list(totals[:4]), list(totals[4:])
    for g in range(3):
        same[g] = second_hop(same[g], ORDER[g], 0)
        cross[g] = second_hop(cross[g], ORDER[g], 1)
    cross[3] = second_hop(cross[3], 0, 1)
    input_grad = input_final(after(sums[3], *totals), early_term, *late_terms)
    scale = (length * lax.axis_size("ctx")) ** (-0.5)
    weight_grad = weight_final(at, scale, same + cross)
    return (input_grad, weight_grad, write_grad[:, None], read_grad[:, None])


def solution(mesh):
    placed = (
        P("ctx", None),
        P(None, "smp"),
        P("ctx", "smp"),
        P("smp"),
        P("smp"),
        P("ctx", "smp", None),
        P("ctx", "smp", None),
        P("ctx", "smp"),
        P("ctx", "smp", None, None),
        P("ctx", "smp", None, None),
    )
    return jax.shard_map(
        body,
        mesh=mesh,
        in_specs=placed,
        out_specs=(
            P(("ctx", "smp"), None),
            P("ctx", "smp"),
            P("ctx", "smp", None),
            P("ctx", "smp", None),
        ),
        check_vma=False,
    )
```

```python
import functools

import jax
import jax.numpy as jnp
from jax import lax
from jax.experimental import pallas as pl
from jax.experimental.pallas import tpu as pltpu
from jax.sharding import PartitionSpec as P

SIDE = 4
CHUNK = 128
CHUNKS = 4
HEADS = 16
WIDE = 1024
QUARTER = WIDE // SIDE
TAIL = 16
F32 = jnp.float32
BF16 = jnp.bfloat16
ORDER = (2, 1, 3, 0)
MIB = 1024 * 1024
VMEM_LIMIT = 24 * MIB
ROOMY_LIMIT = 24 * MIB
SMALL_LIMIT = 8 * MIB


def params(limit=VMEM_LIMIT):
    return pltpu.CompilerParams(vmem_limit_bytes=limit)


COST = pl.CostEstimate(flops=1, bytes_accessed=1, transcendentals=0)


def whole(space=pltpu.VMEM):
    return pl.BlockSpec(memory_space=space)


def full_block(*shape):
    return pl.BlockSpec(shape, lambda *_: (0,) * len(shape))


def routed(block, move):
    route = []
    for i in range(SIDE**3 * 2):
        z, y, x, core = i // 32, i // 8 % 4, i // 2 % 4, i % 2
        z, y, x, core = move(z, y, x, core)
        route.append((i, ((z % SIDE * SIDE + y % SIDE) * SIDE + x % SIDE) * 2 + core % 2))
    return lax.ppermute(block, ("ctx", "smp"), route)


def hop(block, dz, dy):
    return routed(block, lambda z, y, x, core: (z + dz, y + dy, x, core))


def hop_smp(block, dx, dc):
    return routed(block, lambda z, y, x, core: (z, y, x + dx, core + dc))


def x_hop(block, d):
    return routed(block, lambda z, y, x, core: (z, y, x + (d if core == 0 else -d), core))


def first_hop(block, d, to_other):
    def move(z, y, x, core):
        core = core ^ to_other
        return (z, y + d, x, core) if core == 0 else (z + d, y, x, core)

    return routed(block, move)


def second_hop(block, d, to_other):
    def move(z, y, x, core):
        return (z + d, y, x, core ^ to_other) if core == 0 else (z, y + d, x, core ^ to_other)

    return routed(block, move)


def dot(a, b):
    return lax.dot_general(a, b, (((1,), (0,)), ((), ())), preferred_element_type=F32)


def dot_nt(a, b):
    return lax.dot_general(a, b, (((1,), (1,)), ((), ())), preferred_element_type=F32)


def dot_tn(a, b):
    return lax.dot_general(a, b, (((0,), (0,)), ((), ())), preferred_element_type=F32)


def halves(v):
    high = v.astype(BF16)
    return high, (v - high.astype(F32)).astype(BF16)


def spread_matrix():
    lane = lax.broadcasted_iota(jnp.int32, (HEADS, WIDE), 1)
    head = lax.broadcasted_iota(jnp.int32, (HEADS, WIDE), 0)
    return ((lane >= head * 64) & (lane < head * 64 + 64)).astype(F32).astype(BF16)


def spread(v, matrix):
    high, low = halves(v)
    return dot(high, matrix) + dot(low, matrix)


def spread_row(v, matrix):
    return spread(jnp.broadcast_to(v, (8, HEADS)), matrix)[0:1]


def tail_rows(row):
    high, low = halves(row)
    at = lax.broadcasted_iota(jnp.int32, (TAIL, row.shape[1]), 0)
    wide = jnp.where(at == 0, high.astype(F32), jnp.where(at == 1, low.astype(F32), 0.0))
    return wide.astype(BF16)


def tail_value(rows):
    rows = rows.astype(F32)
    return rows[0:1] + rows[1:2]


def turn(a, b):
    return lax.rem(a + b + 2 * SIDE, SIDE)


def pieces(v):
    high = v.astype(BF16)
    middle, low = halves(v - high.astype(F32))
    return high, middle, low


def pre_kernel(
    dlog_ref, stept_ref, grad_ref, read_ref, fork_ref,
    rel_ref, relt_ref, step_ref, state_ref, m0, m1, m2, m3, message, scaled_ref,
):
    y = lax.rem(lax.axis_index("ctx"), SIDE)
    row = lax.broadcasted_iota(jnp.int32, (CHUNK, CHUNK), 0)
    col = lax.broadcasted_iota(jnp.int32, (CHUNK, CHUNK), 1)
    lower = jnp.where(row >= col, 1.0, 0.0).astype(BF16)
    upper = jnp.where(row <= col, 1.0, 0.0).astype(BF16)
    same = jnp.where(row == col, 1.0, 0.0).astype(BF16)
    matrix = spread_matrix()
    head = lax.broadcasted_iota(jnp.int32, (HEADS, CHUNK), 0)
    decay_log = jnp.zeros((HEADS, CHUNK), F32)
    for h in range(HEADS):
        decay_log = jnp.where(head == h, dlog_ref[h], decay_log)
    decay_rate = -jnp.exp(decay_log)
    totals = []
    for c in range(CHUNKS):
        here = slice(c * CHUNK, (c + 1) * CHUNK)
        steps = stept_ref[:, here]
        rates = pieces(steps * decay_rate)
        rel = dot_nt(lower, rates[0]) + dot_nt(lower, rates[1]) + dot_nt(lower, rates[2])
        rel_ref[c] = rel
        relt_ref[c] = dot(rates[0], upper) + dot(rates[1], upper) + dot(rates[2], upper)
        cut = pieces(steps)
        step_ref[here] = dot_nt(same, cut[0]) + dot_nt(same, cut[1]) + dot_nt(same, cut[2])
        totals.append(rel[CHUNK - 1 : CHUNK])
        scaled_ref[here] = (spread(jnp.exp(rel), matrix) * grad_ref[here].astype(F32)).astype(BF16)
    state = None
    for c in reversed(range(CHUNKS)):
        here = slice(c * CHUNK, (c + 1) * CHUNK)
        local = dot_tn(read_ref[here], scaled_ref[here])
        if state is None:
            state = local
        else:
            state = local + spread_row(jnp.exp(totals[c]), matrix) * state
        if c > 0:
            state_ref[c - 1] = state.astype(BF16)
    message[0:128] = state.astype(BF16)
    message[128:256] = (fork_ref[0] + fork_ref[1]).T.astype(BF16)
    decay = spread_row(jnp.exp(totals[0] + totals[1] + totals[2] + totals[3]), matrix)
    message[256 : 256 + TAIL] = tail_rows(decay)
    for d, out in enumerate((m0, m1, m2, m3)):
        start = pl.multiple_of(turn(y, d) * QUARTER, QUARTER)
        out[...] = message[:, pl.ds(start, QUARTER)]


def pre(decay_log, stept, out_grad, reads, fork_grad):
    length = CHUNKS * CHUNK
    sent = jax.ShapeDtypeStruct((256 + TAIL, QUARTER), BF16)
    return pl.pallas_call(
        pre_kernel,
        grid=(1,),
        out_shape=[
            jax.ShapeDtypeStruct((CHUNKS, CHUNK, HEADS), F32),
            jax.ShapeDtypeStruct((CHUNKS, HEADS, CHUNK), F32),
            jax.ShapeDtypeStruct((length, HEADS), F32),
            jax.ShapeDtypeStruct((CHUNKS - 1, 128, WIDE), BF16),
        ]
        + [sent] * 4,
        in_specs=[
            whole(pltpu.SMEM),
            full_block(HEADS, length),
            full_block(length, WIDE),
            full_block(length, 128),
            full_block(2, WIDE, 128),
        ],
        out_specs=[
            full_block(CHUNKS, CHUNK, HEADS),
            full_block(CHUNKS, HEADS, CHUNK),
            full_block(length, HEADS),
            full_block(CHUNKS - 1, 128, WIDE),
        ]
        + [full_block(256 + TAIL, QUARTER)] * 4,
        scratch_shapes=[pltpu.VMEM((256 + TAIL, WIDE), BF16), pltpu.VMEM((length, WIDE), BF16)],
        compiler_params=params(64 * MIB),
        cost_estimate=COST,
    )(decay_log, stept, out_grad, reads, fork_grad)


def group_kernel(at_ref, a0, a1, a2, a3, out_ref, stack):
    y = at_ref[1]
    for d, ref in enumerate((a0, a1, a2, a3)):
        stack[d] = ref[...]
    total = rate = fork = None
    for b in reversed(range(SIDE)):
        at = turn(y, -b)
        local = stack[at, 0:128].astype(F32)
        decay = tail_value(stack[at, 256 : 256 + TAIL])
        share = stack[at, 128:256].astype(F32)
        if total is None:
            total, rate, fork = local, decay, share
        else:
            total, rate, fork = local + decay * total, rate * decay, fork + share
    out_ref[0:128] = total.astype(BF16)
    out_ref[128:256] = fork.astype(BF16)
    out_ref[256 : 256 + TAIL] = tail_rows(rate)


def group(at, arrived):
    return pl.pallas_call(
        group_kernel,
        out_shape=jax.ShapeDtypeStruct((256 + TAIL, QUARTER), BF16),
        in_specs=[whole(pltpu.SMEM)] + [whole()] * 4,
        out_specs=whole(),
        scratch_shapes=[pltpu.VMEM((SIDE, 256 + TAIL, QUARTER), BF16)],
        compiler_params=params(SMALL_LIMIT),
        cost_estimate=COST,
    )(at, *arrived)


def carry_kernel(at_ref, a0, a1, a2, a3, b0, b1, b2, b3, c0, c1, c2, c3, first, second, out):
    z, y = at_ref[0], at_ref[1]
    for d, ref in enumerate((a0, a1, a2, a3)):
        first[d] = ref[...]
    for d, ref in enumerate((b0, b1, b2, b3)):
        second[d] = ref[...]
    carry = jnp.zeros((128, QUARTER), F32)
    for d in range(SIDE):
        carry = carry + second[d, 128:256].astype(F32)
    mine = carry
    for b in (3, 2, 1):
        at = turn(z, -b)
        decay = tail_value(second[at, 256 : 256 + TAIL])
        carry = second[at, 0:128].astype(F32) + decay * carry
        mine = jnp.where(z == b - 1, carry, mine)
    out[SIDE - 1] = mine.astype(BF16)
    for b in (3, 2, 1):
        at = turn(y, -b)
        decay = tail_value(first[at, 256 : 256 + TAIL])
        mine = first[at, 0:128].astype(F32) + decay * mine
        out[b - 1] = mine.astype(BF16)
    for d, ref in enumerate((c0, c1, c2, c3)):
        ref[...] = out[turn(y, d)]


def carry_over(at, first, second):
    return pl.pallas_call(
        carry_kernel,
        out_shape=[jax.ShapeDtypeStruct((128, QUARTER), BF16)] * 4,
        in_specs=[whole(pltpu.SMEM)] + [whole()] * 8,
        out_specs=[whole()] * 4,
        scratch_shapes=[
            pltpu.VMEM((SIDE, 256 + TAIL, QUARTER), BF16),
            pltpu.VMEM((SIDE, 256 + TAIL, QUARTER), BF16),
            pltpu.VMEM((SIDE, 128, QUARTER), BF16),
        ],
        compiler_params=params(SMALL_LIMIT),
        cost_estimate=COST,
    )(at, *first, *second)


def diag_kernel(
    skip_ref, rel_ref, relt_ref, step_ref, read_ref, write_ref, grad_ref, out_ref, scaled_ref
):
    matrix = spread_matrix()
    row = lax.broadcasted_iota(jnp.int32, (CHUNK, CHUNK), 0)
    col = lax.broadcasted_iota(jnp.int32, (CHUNK, CHUNK), 1)
    for c in range(2):
        here = slice(c * CHUNK, (c + 1) * CHUNK)
        scores = jnp.where(col >= row, dot_nt(write_ref[here], read_ref[here]), 0.0)
        rel, relt = rel_ref[c], relt_ref[c]
        steps = spread(step_ref[here], matrix)
        scaled_ref[here] = (spread(jnp.exp(rel), matrix) * grad_ref[here].astype(F32)).astype(BF16)
        for pair in range(HEADS // 2):
            at = slice(pair * 128, pair * 128 + 128)
            grads = grad_ref[here, at]
            both = []
            for h in (2 * pair, 2 * pair + 1):
                kernel = jnp.exp(jnp.minimum(relt[h : h + 1] - rel[:, h : h + 1], 0.0))
                both.append(dot((scores * kernel).astype(BF16), grads))
            part = steps[:, at] * jnp.where(col < 64, both[0], both[1])
            skip = jnp.where(col < 64, skip_ref[2 * pair], skip_ref[2 * pair + 1])
            out_ref[here, at] = (part + skip * grads.astype(F32)).astype(BF16)


def diag(skip_gain, rel, relt, step_size, reads, writes, out_grad):
    by_two = lambda c: (c, 0)
    rows = 2 * CHUNK
    return pl.pallas_call(
        diag_kernel,
        grid=(CHUNKS // 2,),
        out_shape=[jax.ShapeDtypeStruct((CHUNKS * CHUNK, WIDE), BF16)] * 2,
        in_specs=[
            whole(pltpu.SMEM),
            pl.BlockSpec((2, CHUNK, HEADS), lambda c: (c, 0, 0)),
            pl.BlockSpec((2, HEADS, CHUNK), lambda c: (c, 0, 0)),
            pl.BlockSpec((rows, HEADS), by_two),
            pl.BlockSpec((rows, 128), by_two),
            pl.BlockSpec((rows, 128), by_two),
            pl.BlockSpec((rows, WIDE), by_two),
        ],
        out_specs=[pl.BlockSpec((rows, WIDE), by_two)] * 2,
        compiler_params=params(ROOMY_LIMIT),
        cost_estimate=pl.CostEstimate(flops=4000000000, bytes_accessed=1, transcendentals=0),
    )(skip_gain, rel, relt, step_size, reads, writes, out_grad)


def x_kernel(
    at_ref, q0, q1, q2, q3, state_ref, rel_ref, step_ref, write_ref, base_ref,
    keep_ref, give_ref, mine_ref, full_ref, carried, x_ref,
):
    y, core = at_ref[1], at_ref[3]
    matrix = spread_matrix()
    for d, ref in enumerate((q0, q1, q2, q3)):
        start = pl.multiple_of(turn(y, -d) * QUARTER, QUARTER)
        carried[:, pl.ds(start, QUARTER)] = ref[...]
    later = jnp.zeros((1, HEADS), F32)
    for c in reversed(range(CHUNKS)):
        here = slice(c * CHUNK, (c + 1) * CHUNK)
        rel = rel_ref[c]
        last = rel[CHUNK - 1 : CHUNK]
        if c == CHUNKS - 1:
            full = carried[...]
        else:
            share = spread_row(jnp.exp(later), matrix) * carried[...].astype(F32)
            full = (state_ref[c].astype(F32) + share).astype(BF16)
        full_ref[c] = full
        weights = spread(step_ref[here] * jnp.exp(last - rel), matrix)
        x = (base_ref[here].astype(F32) + weights * dot(write_ref[here], full)).astype(BF16)
        for k in range(2):
            x_ref[c, k] = x[k * 64 : k * 64 + 64]
        later = later + last
    start = pl.multiple_of(core * 512, 512)
    other = pl.multiple_of((1 - core) * 512, 512)
    for c in range(CHUNKS):
        for k in range(2):
            here = slice(c * CHUNK + k * 64, c * CHUNK + k * 64 + 64)
            keep_ref[here] = x_ref[c, k, :, pl.ds(start, 512)]
            give_ref[here] = x_ref[c, k, :, pl.ds(other, 512)]
        there = slice(c * 64, c * 64 + 64)
        mine_ref[there] = x_ref[c, core]
        for k in range(2):
            there = slice(512 + k * 256 + c * 64, 512 + k * 256 + c * 64 + 64)
            give_ref[there] = x_ref[c, 1 - core, :, k * 512 : k * 512 + 512]


def x_final(at, quarters, states, rel, step_size, writes, base):
    rows = CHUNKS * CHUNK
    shapes = (rows, 512), (2 * rows, 512), (rows // 2, WIDE)
    return pl.pallas_call(
        x_kernel,
        grid=(1,),
        in_specs=[whole(pltpu.SMEM)]
        + [full_block(128, QUARTER)] * 4
        + [
            full_block(CHUNKS - 1, 128, WIDE),
            full_block(CHUNKS, CHUNK, HEADS),
            full_block(rows, HEADS),
            full_block(rows, 128),
            full_block(rows, WIDE),
        ],
        out_specs=[full_block(*shape) for shape in shapes] + [full_block(CHUNKS, 128, WIDE)],
        scratch_shapes=[pltpu.VMEM((128, WIDE), BF16), pltpu.VMEM((CHUNKS, 2, 64, WIDE), BF16)],
        out_shape=[jax.ShapeDtypeStruct(shape, BF16) for shape in shapes]
        + [jax.ShapeDtypeStruct((CHUNKS, 128, WIDE), BF16)],
        compiler_params=params(ROOMY_LIMIT),
        cost_estimate=COST,
    )(at, *quarters, states, rel, step_size, writes, base)


def vector_kernel(
    rel_ref, relt_ref, step_ref, read_ref, write_ref, grad_ref, scaled_ref, first_ref, second_ref,
    full_ref, start_ref, wgrad_ref, rgrad_ref, state,
):
    matrix = spread_matrix()

    @pl.when(pl.program_id(0) == 0)
    def _():
        state[...] = start_ref[...].T

    row = lax.broadcasted_iota(jnp.int32, (CHUNK, CHUNK), 0)
    col = lax.broadcasted_iota(jnp.int32, (CHUNK, CHUNK), 1)
    later = jnp.where(col >= 64, 1.0, 0.0).astype(BF16)
    for c in range(2):
        here = slice(c * CHUNK, (c + 1) * CHUNK)
        rel, relt, step = rel_ref[c], relt_ref[c], step_ref[here]
        last = rel[CHUNK - 1 : CHUNK]
        steps = spread(step, matrix)
        weights = spread(step * jnp.exp(last - rel), matrix)
        weighted, coupling = [], None
        for half, inputs_ref in enumerate((first_ref, second_ref)):
            inputs = inputs_ref[here].astype(F32)
            wide = slice(half * 512, half * 512 + 512)
            weighted.append((weights[:, wide] * inputs).astype(BF16))
            stepped = (steps[:, wide] * inputs).astype(BF16)
            for pair in range(HEADS // 4):
                at = slice(pair * 128, pair * 128 + 128)
                grads = grad_ref[here, half * 512 + pair * 128 : half * 512 + pair * 128 + 128].T
                for k in range(2):
                    h = half * HEADS // 2 + 2 * pair + k
                    own = stepped[:, at] * (later if k == 1 else 1 - later)
                    kernel = jnp.exp(jnp.minimum(relt[h : h + 1] - rel[:, h : h + 1], 0.0))
                    term = kernel * dot(own, grads)
                    coupling = term if coupling is None else coupling + term
        coupling = jnp.where(col >= row, coupling, 0.0).astype(BF16)
        full, scaled = full_ref[c], scaled_ref[here]
        wgrad = dot(coupling, read_ref[here])
        new_state = []
        for half in range(2):
            wide = slice(half * 512, half * 512 + 512)
            wgrad = wgrad + dot_nt(weighted[half], full[:, wide])
            new_state.append(dot_tn(write_ref[here], weighted[half]))
        wgrad_ref[here] = wgrad
        rgrad_ref[here] = dot_nt(scaled, state[...].astype(BF16)) + dot_tn(coupling, write_ref[here])
        decay = spread_row(jnp.exp(last), matrix)
        for half in range(2):
            wide = slice(half * 512, half * 512 + 512)
            state[:, wide] = decay[:, wide] * state[:, wide] + new_state[half]


def vectors(rel, relt, step_size, reads, writes, out_grad, scaled, first, second, full, start_state):
    by_two = lambda c: (c, 0)
    by_first = lambda c: (c, 0, 0)
    rows = 2 * CHUNK
    return pl.pallas_call(
        vector_kernel,
        grid=(CHUNKS // 2,),
        out_shape=[jax.ShapeDtypeStruct((CHUNKS * CHUNK, 128), F32)] * 2,
        in_specs=[
            pl.BlockSpec((2, CHUNK, HEADS), by_first),
            pl.BlockSpec((2, HEADS, CHUNK), by_first),
            pl.BlockSpec((rows, HEADS), by_two),
            pl.BlockSpec((rows, 128), by_two),
            pl.BlockSpec((rows, 128), by_two),
            pl.BlockSpec((rows, WIDE), by_two),
            pl.BlockSpec((rows, WIDE), by_two),
            pl.BlockSpec((rows, WIDE // 2), by_two),
            pl.BlockSpec((rows, WIDE // 2), by_two),
            pl.BlockSpec((2, 128, WIDE), by_first),
            pl.BlockSpec((WIDE, 128), lambda c: (0, 0)),
        ],
        out_specs=[pl.BlockSpec((rows, 128), by_two)] * 2,
        scratch_shapes=[pltpu.VMEM((128, WIDE), F32)],
        compiler_params=params(),
        cost_estimate=pl.CostEstimate(flops=50000000000, bytes_accessed=1, transcendentals=0),
    )(rel, relt, step_size, reads, writes, out_grad, scaled, first, second, full, start_state)


def project_kernel(x_ref, w_ref, out_ref, total):
    step = pl.program_id(0)
    product = dot(x_ref[...], w_ref[...])

    @pl.when(step == 0)
    def _():
        total[...] = product

    @pl.when(step == 1)
    def _():
        out_ref[...] = (total[...] + product).astype(BF16)


def project(layer_input, proj_weight, part):
    rows, depth = layer_input.shape
    wide = WIDE // 2
    return pl.pallas_call(
        project_kernel,
        grid=(2,),
        out_shape=jax.ShapeDtypeStruct((rows, wide), BF16),
        in_specs=[
            pl.BlockSpec((rows, depth // 2), lambda i: (0, i)),
            pl.BlockSpec((depth // 2, wide), lambda i: (i, part)),
        ],
        out_specs=pl.BlockSpec((rows, wide), lambda i: (0, 0)),
        scratch_shapes=[pltpu.VMEM((rows, wide), F32)],
        compiler_params=params(61 * MIB),
        cost_estimate=COST,
    )(layer_input, proj_weight)


FAR = ((2, (0, 1)), (2, (2, 3)))
PLAIN = ((1, (2, 3)), (-1, (0, 1)))
ADDED = ((1, (0, 1)), (-1, (2, 3)))


def column_block(s, d, part):
    for_y = turn(s[0], part) * SIDE + turn(s[1], d)
    for_z = turn(s[0], d) * SIDE + turn(s[1], part)
    return jnp.where(s[3] == 0, for_y, for_z)


def columns_spec(d, parts):
    def index(g, s):
        return 0, column_block(s, d, jnp.where(g == 0, ORDER[parts[0]], ORDER[parts[1]]))

    return pl.BlockSpec((CHUNKS * CHUNK, 256), index)


def ring_kernel(at_ref, up_ref, down_ref, keep_ref, got_ref, *refs):
    more, outs = refs[:-2], refs[-2:]
    for k, cols in enumerate((up_ref, down_ref)):
        turned = cols[...].T
        for half, x_ref in enumerate((keep_ref, got_ref)):
            at = slice(512 * half, 512 * half + 512)
            product = dot(turned, x_ref[...])
            if more:
                product = product + more[k][0, :, at].astype(F32)
            outs[k][0, :, at] = product.astype(BF16)


def ring_product(at, way, layer_input, keep, got, more=()):
    rows = layer_input.shape[0]
    (up_to, up_parts), (down_to, down_parts) = way
    block = pl.BlockSpec((1, 256, WIDE), lambda g, s: (g, 0, 0))
    return pl.pallas_call(
        ring_kernel,
        grid_spec=pltpu.PrefetchScalarGridSpec(
            num_scalar_prefetch=1,
            grid=(2,),
            in_specs=[columns_spec(up_to, up_parts), columns_spec(down_to, down_parts)]
            + [pl.BlockSpec((rows, 512), lambda g, s: (0, 0))] * 2
            + [block] * len(more),
            out_specs=[block] * 2,
        ),
        out_shape=[jax.ShapeDtypeStruct((2, 256, WIDE), BF16)] * 2,
        compiler_params=params(),
        cost_estimate=COST,
    )(at, layer_input, layer_input, keep, got, *more)


def plain_kernel(
    at_ref, up_ref, down_ref, first_ref, second_ref, keep_ref, got_ref, up_out, down_out, own_out
):
    outs = (up_out.at[0], down_out.at[0], own_out.at[0], own_out.at[1])
    for cols, out in zip((up_ref, down_ref, first_ref, second_ref), outs):
        turned = cols[...].T
        for half, x_ref in enumerate((keep_ref, got_ref)):
            out[:, 512 * half : 512 * half + 512] = dot(turned, x_ref[...]).astype(BF16)


def plain_product(at, layer_input, keep, got):
    rows = layer_input.shape[0]
    (up_to, up_parts), (down_to, down_parts) = PLAIN
    return pl.pallas_call(
        plain_kernel,
        grid_spec=pltpu.PrefetchScalarGridSpec(
            num_scalar_prefetch=1,
            grid=(2,),
            in_specs=[columns_spec(up_to, up_parts), columns_spec(down_to, down_parts)]
            + [columns_spec(0, (0, 2)), columns_spec(0, (1, 3))]
            + [pl.BlockSpec((rows, 512), lambda g, s: (0, 0))] * 2,
            out_specs=[pl.BlockSpec((1, 256, WIDE), lambda g, s: (g, 0, 0))] * 2
            + [pl.BlockSpec((2, 256, WIDE), lambda g, s: (g, 0, 0))],
        ),
        out_shape=[jax.ShapeDtypeStruct((2, 256, WIDE), BF16)] * 2
        + [jax.ShapeDtypeStruct((4, 256, WIDE), BF16)],
        compiler_params=params(),
        cost_estimate=COST,
    )(at, *[layer_input] * 4, keep, got)


def total_kernel(own_ref, below_add, below_plain, above_plain, above_add, *outs):
    g = pl.program_id(0)
    for k in range(2):
        for half in range(2):
            at = slice(512 * half, 512 * half + 512)
            early, late = outs[SIDE * half + k], outs[SIDE * half + 2 + k]
            own = own_ref[k, :, at].astype(F32)

            @pl.when(g == 0)
            def _():
                total = own + below_add[k, :, at].astype(F32) + above_plain[k, :, at].astype(F32)
                early[...] = total.astype(early.dtype)

            @pl.when(g == 1)
            def _():
                total = own + below_plain[k, :, at].astype(F32) + above_add[k, :, at].astype(F32)
                late[...] = total.astype(late.dtype)


def own_total(own, arrived):
    shape = lambda dtype: jax.ShapeDtypeStruct((256, 512), dtype)
    return pl.pallas_call(
        total_kernel,
        grid=(2,),
        in_specs=[pl.BlockSpec((2, 256, WIDE), lambda g: (g, 0, 0))] + [full_block(2, 256, WIDE)] * 4,
        out_specs=[full_block(256, 512)] * 8,
        out_shape=[shape(BF16)] * 3 + [shape(F32)] + [shape(BF16)] * 4,
        compiler_params=params(),
        cost_estimate=COST,
    )(own, *arrived)


def weight_kernel(scale, at_ref, *refs):
    same, cross, out = refs[:4], refs[4:8], refs[8]
    for terms, place in ((same, at_ref[3]), (cross, 1 - at_ref[3])):
        total = terms[0][...].astype(F32)
        for term in terms[1:]:
            total = total + term[...].astype(F32)
        out[:, pl.ds(pl.multiple_of(place * 512, 512), 512)] = (total * scale).astype(BF16)


def weight_final(at, scale, terms):
    return pl.pallas_call(
        functools.partial(weight_kernel, scale),
        grid=(1,),
        out_shape=jax.ShapeDtypeStruct((256, WIDE), BF16),
        in_specs=[whole(pltpu.SMEM)] + [full_block(256, 512)] * 8,
        out_specs=full_block(256, WIDE),
        compiler_params=params(),
        cost_estimate=COST,
    )(at, *terms)


def input_kernel(x_ref, w_ref, out_ref):
    out_ref[...] = dot_nt(x_ref[...], w_ref[...]).astype(BF16)


def input_product(x_rows, proj_weight):
    depth, tile = proj_weight.shape[0], 2048
    return pl.pallas_call(
        input_kernel,
        grid=(depth // tile,),
        in_specs=[full_block(256, WIDE), pl.BlockSpec((tile, WIDE), lambda i: (i, 0))],
        out_specs=pl.BlockSpec((256, tile), lambda i: (0, i)),
        out_shape=jax.ShapeDtypeStruct((256, depth), BF16),
        compiler_params=params(),
        cost_estimate=COST,
    )(x_rows, proj_weight)


def rest_kernel(at_ref, left_ref, right_ref, w_ref, part_ref, far, next_out, last_out, own, total):
    x, core = at_ref[2], at_ref[3]
    product = dot_nt(left_ref[...], w_ref[:, :512]) + dot_nt(right_ref[...], w_ref[:, 512:])
    total[...] = (product + part_ref[...].astype(F32)).reshape(SIDE, 64, -1)
    step = 1 - 2 * core
    for d, out in ((2, far), (step, next_out), (-step, last_out), (0, own)):
        out[...] = total[turn(x, d)].astype(out.dtype)


def input_rest(at, got, other_weight, part):
    depth, tile = other_weight.shape[0], 2048
    out = pl.BlockSpec((64, tile), lambda i, s: (0, i))
    shape = lambda dtype: jax.ShapeDtypeStruct((64, depth), dtype)
    return pl.pallas_call(
        rest_kernel,
        grid_spec=pltpu.PrefetchScalarGridSpec(
            num_scalar_prefetch=1,
            grid=(depth // tile,),
            in_specs=[
                pl.BlockSpec((256, 512), lambda i, s: (2, 0)),
                pl.BlockSpec((256, 512), lambda i, s: (3, 0)),
                pl.BlockSpec((tile, WIDE), lambda i, s: (i, 0)),
                pl.BlockSpec((256, tile), lambda i, s: (0, i)),
            ],
            out_specs=[out] * 4,
            scratch_shapes=[pltpu.VMEM((SIDE, 64, tile), F32)],
        ),
        out_shape=[shape(BF16), shape(BF16), shape(BF16), shape(F32)],
        compiler_params=params(),
        cost_estimate=COST,
    )(at, got, got, other_weight, part)


def sum_kernel(own, first, second, third, out):
    total = own[...] + first[...].astype(F32) + second[...].astype(F32) + third[...].astype(F32)
    out[...] = total.astype(BF16)


def input_final(own, *arrived):
    rows, depth = own.shape
    return pl.pallas_call(
        sum_kernel,
        grid=(1,),
        out_shape=jax.ShapeDtypeStruct((rows, depth), BF16),
        in_specs=[full_block(rows, depth)] * 4,
        out_specs=full_block(rows, depth),
        compiler_params=params(),
        cost_estimate=COST,
    )(own, *arrived)


def after(value, *earlier):
    return lax.optimization_barrier((value, earlier))[0]


def body(
    layer_input,
    proj_weight,
    step_size,
    decay_log,
    skip_gain,
    write_vec,
    read_vec,
    out_grad,
    start_state,
    fork_grad,
):
    length = layer_input.shape[0]
    position = lax.axis_index("ctx")
    z, y = position // SIDE, position % SIDE
    column = lax.axis_index("smp")
    x, core = column // 2, column % 2
    writes = write_vec[:, 0]
    reads = read_vec[:, 0]
    rel, relt, steps, states, *messages = pre(
        decay_log, step_size.T, out_grad, reads, fork_grad.reshape(2, WIDE, 128)
    )
    at = jnp.stack(after([z, y, x, core], *messages))
    far, above, below = (hop(messages[d], 0, d) for d in (2, 1, 3))
    other_weight = hop_smp(proj_weight, 0, 1)
    inputs_a = project(after(layer_input, *messages), proj_weight, 0)
    first = after([messages[0], above, far, below], inputs_a)
    message = group(at, first)
    far, above, below = (hop(message, d, 0) for d in (2, 1, 3))
    inputs_b = project(after(layer_input, message), proj_weight, 1)
    second = after([message, above, far, below], inputs_b, other_weight)
    sent = carry_over(at, first, second)
    far, above, below = (hop(sent[d], 0, d) for d in (2, 1, 3))
    base, scaled = diag(skip_gain, rel, relt, steps, reads, writes, after(out_grad, sent[0]))
    quarters = [sent[0], above, far, below]
    keep, give, x_mine, full = x_final(at, quarters, states, rel, steps, writes, base)
    got = first_hop(give, 0, 1)
    part = input_product(x_mine, proj_weight)
    far = ring_product(at, FAR, layer_input, keep, after(got, part))
    far_in = first_hop(far[0], 1, 0), first_hop(far[1], -1, 0)
    *plain, own = plain_product(at, layer_input, after(keep, *far), got)
    plain_in = first_hop(plain[0], 1, 0), first_hop(plain[1], -1, 0)
    sums = input_rest(at, after(got, *plain), other_weight, part)
    early_term = x_hop(sums[0], 2)
    added = ring_product(at, ADDED, layer_input, keep, got, after(far_in, *sums))
    added_in = first_hop(added[0], 1, 0), first_hop(added[1], -1, 0)
    late_terms = [x_hop(after(sums[k], plain_in), 3 - 2 * k) for k in (1, 2)]
    write_grad, read_grad = vectors(
        rel, relt, steps, reads, writes, out_grad, scaled, inputs_a, inputs_b, after(full, *added),
        start_state.reshape(WIDE, 128),
    )
    arrived = added_in[0], plain_in[0], plain_in[1], added_in[1]
    totals = own_total(own, after(arrived, write_grad, early_term))
    same, cross = list(totals[:4]), list(totals[4:])
    for g in range(3):
        same[g] = second_hop(same[g], ORDER[g], 0)
        cross[g] = second_hop(cross[g], ORDER[g], 1)
    cross[3] = second_hop(cross[3], 0, 1)
    input_grad = input_final(after(sums[3], *totals), early_term, *late_terms)
    scale = (length * lax.axis_size("ctx")) ** (-0.5)
    weight_grad = weight_final(at, scale, same + cross)
    return (input_grad, weight_grad, write_grad[:, None], read_grad[:, None])


def solution(mesh):
    placed = (
        P("ctx", None),
        P(None, "smp"),
        P("ctx", "smp"),
        P("smp"),
        P("smp"),
        P("ctx", "smp", None),
        P("ctx", "smp", None),
        P("ctx", "smp"),
        P("ctx", "smp", None, None),
        P("ctx", "smp", None, None),
    )
    return jax.shard_map(
        body,
        mesh=mesh,
        in_specs=placed,
        out_specs=(
            P(("ctx", "smp"), None),
            P("ctx", "smp"),
            P("ctx", "smp", None),
            P("ctx", "smp", None),
        ),
        check_vma=False,
    )
```
